256 devices in a mesh: pat: 16 (over x_lo, y, core), tile: 16 (over z, x_hi).
Axes of the slice: x: 4 (x_hi: 2, x_lo: 2; x = x_hi * 2 + x_lo), y: 4, z: 8, core: 2. Of those that a mesh axis runs over, the one named last changes fastest.
Arguments:
- patch_class_features: bfloat16 [32768, 1536], P(('pat', 'tile')), may hold values from -6 to 6
- live_tiles: int32 [256], P(('pat', 'tile')), may hold values from 32 to 128, as said below
- tile_patient: int32 [32768], P(('pat', 'tile')), may hold values from 0 to 3, as said below
- ln_gain: float32 [1536], replicated, may hold values from 0.25 to 1.75
- up_weight: bfloat16 [1536, 6144], P(None, 'tile'), may hold values from -0.15625 to 0.15625
- down_weight: bfloat16 [6144, 1536], P('tile'), may hold values from -0.078125 to 0.078125
- tanh_weight: bfloat16 [1536, 256], P('tile'), may hold values from -0.15625 to 0.15625
- sigmoid_weight: bfloat16 [1536, 256], P('tile'), may hold values from -0.15625 to 0.15625
- score_weight: float32 [256], replicated, may hold values from -0.25 to 0.25
- queue_keys: bfloat16 [16384, 1536], P('tile'), may hold values from -6 to 6
- queue_labels: int32 [16384], P('tile'), may hold values from 0 to 3, as said below
- patient_labels: int32 [64], P('pat'), may hold values from 0 to 3
- loss_scale: float32 [], replicated, may hold values from 1024 to 8192
Outputs:
- up_grad: float32 [1536, 6144], P('pat', 'tile')
- down_grad: float32 [6144, 1536], P('tile', 'pat')
- tanh_grad: float32 [1536, 256], P('tile')
- sigmoid_grad: float32 [1536, 256], P('tile')
- score_grad: float32 [256], replicated
- contrastive_loss: float32 [], replicated
The draws below stay inside these ranges and needn't reach their ends.
Inputs may be any that keep to these rules, and one draw needn't show every extreme that they name: `live_tiles`: some device has all 128 slots live in every draw. `tile_patient`: every patient has at least one live tile. `queue_labels`: every class appears in the queue.
All inputs are finite; a program needn't handle non-finite values.
Results may differ from the reference program's by a relative error of at most 0.03.
Values may be sent and summed in bfloat16 or wider, within the bound.
A program may use at most 192 MiB of HBM per device.

```python
import math
import jax
import jax.numpy as jnp
from jax import lax

D = 1536
FF = 6144
GATE_DIM = 256
CLASSES = 4
PAT_DEV = 4
TILE_DEV = 128
TILES = 32768
NPAT = 64
QUEUE = 16384
N_PAT = 16
N_TILE = 16


def draw_live_tiles(key, part):
    key = jax.random.fold_in(key, 11)
    device_count = N_PAT * N_TILE
    counts = jax.random.randint(key, (device_count,), max(1, TILE_DEV // 4), TILE_DEV + 1)
    full_at = jax.random.randint(jax.random.fold_in(key, 1), (), 0, device_count)
    return jnp.where(jnp.arange(device_count) == full_at, TILE_DEV, counts).astype(jnp.int32)


def draw_tile_patient(key, part):
    key = jax.random.fold_in(key, 12)
    draw_one = jax.random.randint(jax.random.fold_in(key, 1), (TILES,), 0, PAT_DEV)
    draw_two = jax.random.randint(jax.random.fold_in(key, 2), (TILES,), 0, PAT_DEV)
    skewed = jnp.minimum(draw_one, draw_two)
    slot_index = jnp.arange(TILES, dtype=jnp.int32)
    device_tile = slot_index // TILE_DEV % N_TILE
    first_slot = (slot_index % TILE_DEV == 0) & (device_tile < PAT_DEV)
    return jnp.where(first_slot, device_tile, skewed).astype(jnp.int32)


def draw_queue_labels(key, part):
    key = jax.random.fold_in(key, 13)
    labels = jax.random.randint(key, (QUEUE,), 0, CLASSES)
    slot_index = jnp.arange(QUEUE, dtype=jnp.int32)
    return jnp.where(slot_index < CLASSES, slot_index, labels).astype(jnp.int32)


def set_ends(result, own_key, smallest, high):
    longest = result.shape.index(max(result.shape))
    spots = []
    for shift in (0, 1):
        where = [jax.random.randint(jax.random.fold_in(own_key, axis), (), 0, length) for axis, length in enumerate(result.shape)]
        where[longest] = (where[longest] + shift) % result.shape[longest]
        spots.append(tuple(where))
    return result.at[spots[0]].set(smallest).at[spots[1]].set(high)


def block_levels(own_key, shape, shards, smallest, largest):
    def one(dim, parts):
        heights = jax.random.uniform(jax.random.fold_in(jax.random.fold_in(own_key, 6), dim), (parts,), jnp.float32, smallest / len(shards), largest / len(shards))
        return jnp.repeat(jnp.exp(heights), shape[dim] // parts).reshape((-1,) + (1,) * (len(shape) - dim - 1))

    level = one(*shards[0])
    for cut in shards[1:]:
        level = level * one(*cut)
    return level


def gaussian(stream_key, extent, scale, most, cuts=(), held_as=jnp.bfloat16):
    values = scale * jax.random.normal(stream_key, extent, jnp.float32)
    if cuts:
        values = values * block_levels(stream_key, extent, cuts, -0.22, 0.18)
    return jnp.clip(values, -most, most).astype(held_as)


def setup_inputs(seed: int = 0) -> dict:
    keys = jax.random.split(jax.random.key(seed), 14)
    return {
        "patch_class_features": gaussian(keys[0], (TILES, D), 1.0, 6.0, ((0, 256),)),
        "live_tiles": draw_live_tiles(jax.random.fold_in(keys[13], 71), 0),
        "tile_patient": draw_tile_patient(jax.random.fold_in(keys[13], 71), 0),
        "ln_gain": jnp.clip(1.0 + 0.15 * jax.random.normal(keys[3], (D,), jnp.float32), 0.25, 1.75),
        "up_weight": gaussian(keys[4], (D, FF), D ** -0.5, 0.15625, ((1, 16),)),
        "down_weight": gaussian(keys[5], (FF, D), FF ** -0.5, 0.078125, ((0, 16),)),
        "tanh_weight": gaussian(keys[6], (D, GATE_DIM), D ** -0.5, 0.15625, ((0, 16),)),
        "sigmoid_weight": gaussian(keys[7], (D, GATE_DIM), D ** -0.5, 0.15625, ((0, 16),)),
        "score_weight": jnp.clip(jax.random.uniform(keys[8], (GATE_DIM,), jnp.float32, -0.25, 0.25), -0.25, 0.25),
        "queue_keys": gaussian(keys[9], (QUEUE, D), 1.0, 6.0, ((0, 16),)),
        "queue_labels": draw_queue_labels(jax.random.fold_in(keys[13], 71), 0),
        "patient_labels": set_ends(jax.random.randint(keys[11], (NPAT,), 0, CLASSES), jax.random.fold_in(keys[11], 1), 0, CLASSES - 1).astype(jnp.int32),
        "loss_scale": jnp.clip(jnp.exp(jax.random.uniform(keys[12], (), jnp.float32, math.log(1024.0), math.log(8192.0))), 1024.0, 8192.0),
    }


sharpness_divisor = 0.07
highest = lax.Precision.HIGHEST

def layer_norm(row_block, ln_gain):
    values = row_block.astype(jnp.float32)
    center = values - lax.optimization_barrier(jnp.mean(values, axis=1, keepdims=True))
    spread = lax.optimization_barrier(jnp.mean(center * center, axis=1, keepdims=True))
    return (center * lax.rsqrt(spread + 1e-06) * ln_gain).astype(jnp.bfloat16)

def gelu_value(preact):
    return 0.5 * preact * (1.0 + lax.erf(preact * 0.7071067811865476))

def gelu_slope(preact):
    return 0.5 * (1.0 + lax.erf(preact * 0.7071067811865476)) + preact * jnp.exp(-0.5 * preact * preact) * 0.3989422804014327

def down_project(hidden, down_weight):
    slice_width = down_weight.shape[0] // N_TILE

    def add_block(totals, block_index):
        start = block_index * slice_width
        block_part = lax.dynamic_slice_in_dim(hidden, start, slice_width, 1)
        weight_part = lax.dynamic_slice_in_dim(down_weight, start, slice_width, 0)
        block_term = jnp.dot(block_part, weight_part, preferred_element_type=jnp.float32).astype(jnp.bfloat16)
        block_term = lax.optimization_barrier(block_term)
        return (totals + block_term.astype(jnp.float32), None)
    start_total = jnp.zeros((hidden.shape[0], down_weight.shape[1]), jnp.float32)
    totals, discarded_result = lax.scan(add_block, start_total, jnp.arange(N_TILE, dtype=jnp.int32))
    return totals

def reference(patch_class_features, live_tiles, tile_patient, ln_gain, up_weight, down_weight, tanh_weight, sigmoid_weight, score_weight, queue_keys, queue_labels, patient_labels, loss_scale):
    group_rows = N_TILE * TILE_DEV
    slot_index = jnp.arange(TILES, dtype=jnp.int32)
    live = slot_index % TILE_DEV < live_tiles[slot_index // TILE_DEV]
    patient = slot_index // group_rows * PAT_DEV + tile_patient
    onehot = ((patient[:, None] == jnp.arange(NPAT, dtype=jnp.int32)[None, :]) & live[:, None]).astype(jnp.float32)
    grouped = patch_class_features.reshape(N_PAT, group_rows, D)

    def forward(row_block):
        normed = layer_norm(row_block, ln_gain)
        hidden = gelu_value(jnp.dot(normed, up_weight, preferred_element_type=jnp.float32)).astype(jnp.bfloat16)
        return row_block.astype(jnp.float32) + down_project(hidden, down_weight)
    tile_state = lax.map(forward, grouped).reshape(TILES, D)
    head_in = tile_state.astype(jnp.bfloat16)
    tanh_val = jnp.tanh(jnp.dot(head_in, tanh_weight, preferred_element_type=jnp.float32))
    sigmoid_val = jax.nn.sigmoid(jnp.dot(head_in, sigmoid_weight, preferred_element_type=jnp.float32))
    gate_product = tanh_val * sigmoid_val
    tile_score = lax.optimization_barrier(jnp.sum(gate_product * score_weight, axis=1))
    pool_mass = onehot * jnp.exp(tile_score)[:, None]
    total_mass = lax.optimization_barrier(jnp.sum(pool_mass, axis=0))
    pooled = jnp.dot(pool_mass.T, tile_state, precision=highest) / total_mass[:, None]
    length = jnp.sqrt(lax.optimization_barrier(jnp.sum(pooled * pooled, axis=1)) + 1e-06)
    rescaled_bag_embedding = pooled / length[:, None]
    key_values = queue_keys.astype(jnp.float32)
    direction_queue_entry = (key_values / jnp.sqrt(lax.optimization_barrier(jnp.sum(key_values * key_values, axis=1, keepdims=True)) + 1e-06)).astype(jnp.bfloat16)
    cosine_match_scores = jnp.dot(rescaled_bag_embedding.astype(jnp.bfloat16), direction_queue_entry.T, preferred_element_type=jnp.float32) / sharpness_divisor
    same_label = (patient_labels[:, None] == queue_labels[None, :]).astype(jnp.float32)
    exp_logits = jnp.exp(cosine_match_scores)
    exp_total = lax.optimization_barrier(jnp.sum(exp_logits, axis=1))
    positives = lax.optimization_barrier(jnp.sum(same_label, axis=1))
    positive_sum = lax.optimization_barrier(jnp.sum(same_label * cosine_match_scores, axis=1))
    contrastive_loss = jnp.sum(jnp.log(exp_total) - positive_sum / positives)
    score_derivative_lines = (loss_scale * (exp_logits / exp_total[:, None] - same_label / positives[:, None])).astype(jnp.bfloat16)
    rescaled_derivative = jnp.dot(score_derivative_lines, direction_queue_entry, preferred_element_type=jnp.float32) / sharpness_divisor
    pooled_grad = (rescaled_derivative - rescaled_bag_embedding * lax.optimization_barrier(jnp.sum(rescaled_bag_embedding * rescaled_derivative, axis=1, keepdims=True))) / length[:, None]
    alpha_row = lax.optimization_barrier(jnp.sum(pool_mass / total_mass[None, :], axis=1))
    row_grad = jnp.dot(onehot, pooled_grad, precision=highest)
    row_center = jnp.dot(onehot, pooled, precision=highest)
    score_grads = alpha_row * lax.optimization_barrier(jnp.sum((tile_state - row_center) * row_grad, axis=1))
    common = score_grads[:, None] * score_weight
    tanh_pre = (common * sigmoid_val * (1.0 - tanh_val * tanh_val)).astype(jnp.bfloat16)
    sigmoid_pre = (common * tanh_val * sigmoid_val * (1.0 - sigmoid_val)).astype(jnp.bfloat16)
    tanh_grad = jnp.dot(head_in.T, tanh_pre, preferred_element_type=jnp.float32)
    sigmoid_grad = jnp.dot(head_in.T, sigmoid_pre, preferred_element_type=jnp.float32)
    score_grad = lax.optimization_barrier(jnp.sum(score_grads[:, None] * gate_product, axis=0))
    state_grad = alpha_row[:, None] * row_grad + jnp.dot(tanh_pre, tanh_weight.T, preferred_element_type=jnp.float32) + jnp.dot(sigmoid_pre, sigmoid_weight.T, preferred_element_type=jnp.float32)
    out_grads = state_grad.astype(jnp.bfloat16)

    def backward(totals, inputs):
        row_block, grad_block = inputs
        normed = layer_norm(row_block, ln_gain)
        preact = jnp.dot(normed, up_weight, preferred_element_type=jnp.float32)
        hidden = gelu_value(preact).astype(jnp.bfloat16)
        hidden_grad = jnp.dot(grad_block, down_weight.T, preferred_element_type=jnp.float32)
        pre_grad = (hidden_grad * gelu_slope(preact)).astype(jnp.bfloat16)
        return ((totals[0] + jnp.dot(normed.T, pre_grad, preferred_element_type=jnp.float32), totals[1] + jnp.dot(hidden.T, grad_block, preferred_element_type=jnp.float32)), None)
    start_totals = (jnp.zeros((D, FF), jnp.float32), jnp.zeros((FF, D), jnp.float32))
    weight_totals, discarded_result = lax.scan(backward, start_totals, (grouped, out_grads.reshape(N_PAT, group_rows, D)))
    return (weight_totals[0], weight_totals[1], tanh_grad, sigmoid_grad, score_grad, contrastive_loss)
```

```python
import jax
import jax.numpy as jnp
from jax import lax
from jax.experimental import pallas as pl
from jax.experimental.pallas import tpu as pltpu
from jax.sharding import PartitionSpec as P

MESH = pl.DeviceIdType.MESH
F32 = jnp.float32
BF16 = jnp.bfloat16
HIGH = lax.Precision.HIGHEST
INV_TEMP = 1.0 / 0.07
NZ = 8
NY = 4
NX = 4
ROWS = 128
TOK = NZ * ROWS
D = 1536
HID = 384
GATE = 256
VMEM_LIMIT = 56 << 20


class Place:
    def __init__(self):
        self.pat = lax.axis_index("pat")
        self.tile = lax.axis_index("tile")
        self.z = lax.div(self.tile, 2)
        self.q = lax.rem(self.tile, 2)
        self.xl = lax.div(self.pat, 8)
        self.y = lax.rem(lax.div(self.pat, 2), 4)
        self.c = lax.rem(self.pat, 2)
        self.x = self.q * 2 + self.xl

    def at(self, z=None, y=None, x=None, c=None):
        z = self.z if z is None else z
        y = self.y if y is None else y
        c = self.c if c is None else c
        if x is None:
            xl, q = self.xl, self.q
        else:
            xl, q = lax.rem(x, 2), lax.div(x, 2)
        return (xl * 8 + y * 2 + c, z * 2 + q)

    def dz(self, d):
        return lax.rem(self.z + (d + NZ), NZ)

    def dy(self, d):
        return lax.rem(self.y + (d + NY), NY)

    def dx(self, d):
        return lax.rem(self.x + (d + NX), NX)


def meet(partners):
    barrier = pltpu.get_barrier_semaphore()
    for device in partners:
        pl.semaphore_signal(barrier, inc=1, device_id=device, device_id_type=MESH)
    pl.semaphore_wait(barrier, len(partners))


class Mail:
    def __init__(self, send_sem, recv_sem):
        self.send_sem, self.recv_sem = send_sem, recv_sem
        self.next = 0
        self.sent = []

    def slots(self, n):
        first = self.next
        self.next += n
        return first

    def send(self, k, src, dst, device):
        copy = pltpu.make_async_remote_copy(
            src_ref=src, dst_ref=dst, send_sem=self.send_sem.at[k], recv_sem=self.recv_sem.at[k],
            device_id=device, device_id_type=MESH,
        )
        copy.start()
        self.sent.append(copy)

    def arrive(self, k, dst, device):
        pltpu.make_async_remote_copy(
            src_ref=dst, dst_ref=dst, send_sem=self.send_sem.at[k], recv_sem=self.recv_sem.at[k],
            device_id=device, device_id_type=MESH,
        ).wait_recv()

    def finish(self):
        for copy in self.sent:
            copy.wait_send()


def rows_at(index, size, offset=0, count=None):
    count = size if count is None else count
    return pl.ds(pl.multiple_of(index * size + offset, 16), count)


def lanes_at(index, size):
    return pl.ds(pl.multiple_of(index * size, 128), size)


class ZGather:
    def __init__(self, mail, place, ref, own, size):
        self.mail, self.place, self.ref, self.own, self.size = mail, place, ref, own, size
        self.half = size // 2
        self.key = mail.slots(16)
        self.chains = ((1, 0, 4), (-1, 1, 4), (1, 1, 3), (-1, 0, 3))

    def piece(self, owner, half):
        return self.ref.at[rows_at(owner, self.size, half * self.half, self.half)]

    def step(self, s):
        p = self.place
        for i, (way, half, steps) in enumerate(self.chains):
            if s > 0 and s <= steps:
                self.mail.arrive(self.key + i * 4 + s - 1, self.piece(p.dz(-way * s), half), p.at(z=p.dz(-way)))
            if s < steps:
                dst = self.piece(p.dz(-way * s), half)
                if s == 0:
                    src = self.own.at[pl.ds(half * self.half, self.half)]
                else:
                    src = dst
                self.mail.send(self.key + i * 4 + s, src, dst, p.at(z=p.dz(way)))


class ZReduce:
    def __init__(self, mail, place, ref, size, stage, recv):
        self.mail, self.place, self.ref, self.size = mail, place, ref, size
        self.stage, self.recv = stage, recv
        self.half = size // 2
        self.key = mail.slots(16)
        self.chains = ((1, 0, 4), (-1, 1, 4), (1, 1, 3), (-1, 0, 3))

    def piece(self, owner, half):
        return rows_at(owner, self.size, half * self.half, self.half)

    def step(self, s):
        p = self.place
        for i, (way, half, steps) in enumerate(self.chains):
            if s < steps:
                dest = self.piece(p.dz(way * (steps - s)), half)
                if s == 0:
                    src = self.ref.at[dest]
                else:
                    self.mail.arrive(self.key + i * 4 + s - 1, self.recv.at[i, s - 1], p.at(z=p.dz(-way)))
                    src = self.stage.at[i, s - 1]
                    src[...] = (self.ref[dest].astype(F32) + self.recv[i, s - 1].astype(F32)).astype(BF16)
                self.mail.send(self.key + i * 4 + s, src, self.recv.at[i, s], p.at(z=p.dz(way)))

    def total(self):
        p = self.place
        for i, (way, half, steps) in enumerate(self.chains):
            self.mail.arrive(self.key + i * 4 + steps - 1, self.recv.at[i, steps - 1], p.at(z=p.dz(-way)))
        first = self.ref[self.piece(p.z, 0)].astype(F32) + self.recv[0, 3].astype(F32) + self.recv[3, 2].astype(F32)
        second = self.ref[self.piece(p.z, 1)].astype(F32) + self.recv[1, 3].astype(F32) + self.recv[2, 2].astype(F32)
        return jnp.concatenate([first, second], axis=0)


class Swap:
    def __init__(self, mail, ref, me, n, device_of):
        self.mail, self.ref, self.me, self.n, self.device_of = mail, ref, me, n, device_of
        self.key = mail.slots(n - 1)

    def other(self, d):
        return lax.rem(self.me + d, self.n)

    def start(self):
        for d in range(1, self.n):
            mine = self.ref.at[self.me]
            self.mail.send(self.key + d - 1, mine, mine, self.device_of(self.other(d)))

    def wait(self):
        for d in range(1, self.n):
            source = self.other(self.n - d)
            self.mail.arrive(self.key + d - 1, self.ref.at[source], self.device_of(source))

    def total(self):
        self.wait()
        value = self.ref[0].astype(F32)
        for j in range(1, self.n):
            value = value + self.ref[j].astype(F32)
        return value


def gather_kernel(nm, up, dn, wg, n_all, up_all, dn_all, w_all, send_sem, recv_sem, local_sem):
    p = Place()
    mail = Mail(send_sem, recv_sem)
    beside = p.at(x=3 - p.x)
    mate = p.at(c=1 - p.c)
    above, below = p.at(y=p.dy(1)), p.at(y=p.dy(-1))
    meet([p.at(z=p.dz(1)), p.at(z=p.dz(-1)), beside, mate, above, below])
    tokens = ZGather(mail, p, n_all, nm, ROWS)
    tokens.step(0)

    def w_block(z, q, y):
        return w_all.at[pl.ds(pl.multiple_of(z * 192 + q * 96, 96), 96), lanes_at(y, 128)]

    def up_half(q, c):
        return up_all.at[rows_at(c, 768), lanes_at(q, HID)]

    def dn_half(q, c):
        return dn_all.at[pl.ds(pl.multiple_of(q * HID + c * 192, 192), 192)]

    k_w = mail.slots(1)
    mail.send(k_w, wg.at[:, lanes_at(p.y, 128)], w_block(p.z, p.q, p.y), beside)
    k_half = mail.slots(2)
    mail.send(k_half, up.at[rows_at(p.c, 768)], up_half(p.q, p.c), beside)
    mail.send(k_half + 1, dn.at[rows_at(p.c, 192)], dn_half(p.q, p.c), beside)
    locals_ = [
        pltpu.make_async_copy(wg.at[:, lanes_at(p.y, 128)], w_block(p.z, p.q, p.y), local_sem.at[0]),
        pltpu.make_async_copy(nm, n_all.at[rows_at(p.z, ROWS)], local_sem.at[1]),
        pltpu.make_async_copy(up, up_all.at[:, lanes_at(p.q, HID)], local_sem.at[2]),
        pltpu.make_async_copy(dn, dn_all.at[rows_at(p.q, HID)], local_sem.at[3]),
    ]
    for copy in locals_:
        copy.start()
    locals_[0].wait()
    mail.arrive(k_w, w_block(p.z, 1 - p.q, p.y), beside)
    k_z = mail.slots(7)

    def w_rows(z):
        return w_all.at[pl.ds(pl.multiple_of(z * 192, 192), 192), lanes_at(p.y, 128)]

    def gate_step(s):
        for way, steps, key in ((1, 4, k_z), (-1, 3, k_z + 4)):
            if s > 0 and s <= steps:
                mail.arrive(key + s - 1, w_rows(p.dz(-way * s)), p.at(z=p.dz(-way)))
            if s < steps:
                block = w_rows(p.dz(-way * s))
                mail.send(key + s, block, block, p.at(z=p.dz(way)))

    gate_step(0)
    for s in range(1, 4):
        tokens.step(s)
        gate_step(s)
    gate_step(4)

    def w_lanes(y, half=None):
        if half is None:
            return w_all.at[:, lanes_at(y, 128)]
        return w_all.at[pl.ds(half * 768, 768), lanes_at(y, 128)]

    k_y = mail.slots(4)
    mail.send(k_y, w_lanes(p.y), w_lanes(p.y), above)
    mail.send(k_y + 1, w_lanes(p.y), w_lanes(p.y), below)
    k_mate = mail.slots(2)
    theirs, other = 1 - p.q, 1 - p.c
    mail.arrive(k_half, up_half(theirs, p.c), beside)
    mail.send(k_mate, up_half(theirs, p.c), up_half(theirs, p.c), mate)
    mail.arrive(k_half + 1, dn_half(theirs, p.c), beside)
    mail.send(k_mate + 1, dn_half(theirs, p.c), dn_half(theirs, p.c), mate)
    mail.arrive(k_y, w_lanes(p.dy(-1)), below)
    mail.send(k_y + 2, w_lanes(p.dy(-1), 0), w_lanes(p.dy(-1), 0), above)
    mail.arrive(k_y + 1, w_lanes(p.dy(1)), above)
    mail.send(k_y + 3, w_lanes(p.dy(1), 1), w_lanes(p.dy(1), 1), below)
    tokens.step(4)
    mail.arrive(k_y + 2, w_lanes(p.dy(2), 0), below)
    mail.arrive(k_y + 3, w_lanes(p.dy(2), 1), above)
    mail.arrive(k_mate, up_half(theirs, other), mate)
    mail.arrive(k_mate + 1, dn_half(theirs, other), mate)
    for copy in locals_[1:]:
        copy.wait()
    mail.finish()


ANY = pl.BlockSpec(memory_space=pl.ANY)
VMEM = pl.BlockSpec(memory_space=pltpu.VMEM)


def shape(dims, dtype):
    return jax.ShapeDtypeStruct(dims, dtype)


def gather(nm, up, dn, wg):
    return pl.pallas_call(
        gather_kernel,
        name="gather",
        out_shape=(
            shape((TOK, D), BF16),
            shape((D, 2 * HID), BF16),
            shape((2 * HID, D), BF16),
            shape((D, 2 * GATE), BF16),
        ),
        in_specs=[ANY] * 4,
        out_specs=(ANY,) * 4,
        scratch_shapes=[
            pltpu.SemaphoreType.DMA((32,)),
            pltpu.SemaphoreType.DMA((32,)),
            pltpu.SemaphoreType.DMA((4,)),
        ],
        compiler_params=pltpu.CompilerParams(collective_id=1, has_side_effects=True),
    )(nm, up, dn, wg)


def two_part(a):
    top = a.astype(BF16).astype(F32)
    return jnp.concatenate([top, a - top], axis=0).astype(BF16)


def dot_two(a, b, transposed=False):
    dims = (((1,), (1,)), ((), ())) if transposed else (((1,), (0,)), ((), ()))
    both = lax.dot_general(two_part(a), b, dims, preferred_element_type=F32)
    half = a.shape[0]
    return both[:half] + both[half:]


def head_kernel(
    part, x_ref, w_ref, h_ref, dn_ref, key_ref, qlab_ref, plab_ref, marker_ref, sw_ref, scale_ref,
    uv_all, score_all, alpha_all, pm_all, grad_out, misc,
    uv_own, stage, recv, pbuf, zbuf, xbuf, sbuf, send_sem, recv_sem,
):
    p = Place()
    mail = Mail(send_sem, recv_sem)
    z_dev = lambda z: p.at(z=z)
    q_dev = lambda q: (p.pat, p.z * 2 + q)
    meet([p.at(z=p.dz(d)) for d in range(1, NZ)] + [q_dev(1 - p.q)])
    reduce = ZReduce(mail, p, part, ROWS, stage, recv)
    gather_uv = ZGather(mail, p, uv_all, uv_own, ROWS)
    swap_p = Swap(mail, pbuf, p.z, NZ, z_dev)
    swap_z = [Swap(mail, zbuf.at[i], p.z, NZ, z_dev) for i in range(3)]
    swap_x = [Swap(mail, xbuf.at[i], p.q, 2, q_dev) for i in range(3)]
    swap_s = Swap(mail, sbuf, p.z, NZ, z_dev)

    row8 = lax.broadcasted_iota(jnp.int32, (8, 128), 0)
    first4 = row8 < 4
    first4_wide = lax.broadcasted_iota(jnp.int32, (8, 768), 0) < 4
    lane = lax.broadcasted_iota(jnp.int32, (8, 128), 1)

    def pack(v):
        return jnp.where(first4_wide, v[:, :768], v[:, 768:])

    def unpack(v):
        other = pltpu.roll(v, 4, 0)
        return jnp.concatenate([jnp.where(first4_wide, v, other), jnp.where(first4_wide, other, v)], axis=1)

    reduce.step(0)
    gate_x = jnp.dot(x_ref[...], w_ref[...], preferred_element_type=F32)
    reduce.step(1)
    same = (plab_ref[...] == qlab_ref[...]).astype(F32)
    label_sums = jnp.dot(same.astype(BF16), key_ref[...], preferred_element_type=F32)
    positives = jnp.sum(same, axis=1, keepdims=True)
    reduce.step(2)
    reduce.step(3)
    gates = reduce.total() + gate_x
    tanh_val = jnp.tanh(gates[:, :GATE])
    sigmoid_val = jax.nn.sigmoid(gates[:, GATE:])
    product = tanh_val * sigmoid_val
    sw = sw_ref[...]
    score = lax.dot_general(
        jnp.broadcast_to(sw, (8, GATE)), product, (((1,), (1,)), ((), ())), precision=HIGH, preferred_element_type=F32
    )
    onehot = marker_ref[...] == lax.rem(row8, 4)
    mass = jnp.where(onehot, jnp.exp(score), 0.0)
    pbuf[p.z] = mass
    swap_p.start()
    common = sw * sigmoid_val
    uv_own[:, :GATE] = (common * (1.0 - tanh_val * tanh_val)).astype(BF16)
    uv_own[:, GATE:] = (common * tanh_val * (1.0 - sigmoid_val)).astype(BF16)
    gather_uv.step(0)
    uv_all[rows_at(p.z, ROWS)] = uv_own[...]
    vec_x = dot_two(mass, x_ref[...])
    swap_p.wait()

    held = jnp.zeros((8, 2 * HID), F32)
    total = jnp.zeros((8, 1), F32)
    for z in range(NZ):
        block = pbuf[z]
        pm_all[z] = block
        held += dot_two(block, h_ref[pl.ds(z * ROWS, ROWS)])
        total += jnp.sum(block, axis=1, keepdims=True)
    vec = dot_two(held, dn_ref[...]) + vec_x

    def post(i, packed, small):
        zbuf[i, p.z, :, :768] = packed
        zbuf[i, p.z, :, 768:] = small
        swap_z[i].start()

    def collect_z(i):
        xbuf[i, p.q] = swap_z[i].total()
        swap_x[i].start()

    post(0, pack(vec), jnp.broadcast_to(total, (8, 128)))
    gather_uv.step(1)
    post(1, pack(label_sums), jnp.broadcast_to(positives, (8, 128)))
    collect_z(0)
    gather_uv.step(2)
    collect_z(1)
    summed = swap_x[0].total()
    total_mass = summed[:, 768:769]
    pooled = unpack(summed[:, :768]) / total_mass
    length = jnp.sqrt(jnp.sum(pooled * pooled, axis=1, keepdims=True) + 1e-06)
    unit = pooled / length

    logits = lax.dot_general(
        unit.astype(BF16), key_ref[...], (((1,), (1,)), ((), ())), preferred_element_type=F32
    ) / 0.07
    exps = jnp.exp(logits)
    exp_part = jnp.sum(exps, axis=1, keepdims=True)
    pos_part = jnp.sum(same * logits, axis=1, keepdims=True)
    post(2, pack(dot_two(exps, key_ref[...])), jnp.where(lane == 0, exp_part, pos_part))
    gather_uv.step(3)
    labels_total = swap_x[1].total()
    pos_count = labels_total[:, 768:769]
    collect_z(2)
    gather_uv.step(4)
    queue_total = swap_x[2].total()
    exp_total = queue_total[:, 768:769]
    pos_logits = queue_total[:, 769:770]
    unit_grad = (scale_ref[...] * INV_TEMP) * (
        unpack(queue_total[:, :768]) / exp_total - unpack(labels_total[:, :768]) / pos_count
    )
    pooled_grad = (unit_grad - unit * jnp.sum(unit * unit_grad, axis=1, keepdims=True)) / length
    grad_out[...] = pooled_grad

    through = dot_two(pooled_grad, dn_ref[...], True)
    own_dots = dot_two(pooled_grad, x_ref[...], True)
    for z in range(NZ):
        dots = dot_two(through, h_ref[pl.ds(z * ROWS, ROWS)], True)
        dots = dots + jnp.where(p.z == z, own_dots, 0.0)
        picked = jnp.where((pbuf[z] > 0.0) & first4, dots, 0.0)
        sbuf[p.z, pl.ds(z, 1)] = jnp.sum(picked, axis=0, keepdims=True)
    swap_s.start()
    center = jnp.sum(pooled * pooled_grad, axis=1, keepdims=True)
    log_part = jnp.log(exp_total) - pos_logits / pos_count
    loss = jnp.sum(jnp.where(first4, jnp.broadcast_to(log_part, (8, 128)), 0.0), axis=0, keepdims=True)
    for z in range(NZ):
        block = jnp.where(first4, pbuf[z], 0.0)
        alpha_all[pl.ds(z, 1)] = jnp.sum(block / total_mass, axis=0, keepdims=True)
        score_all[pl.ds(z, 1)] = jnp.sum(jnp.where(block > 0.0, center, 0.0), axis=0, keepdims=True)
    score_all[...] = alpha_all[...] * (swap_s.total() - score_all[...])
    score_part = lax.dot_general(
        jnp.broadcast_to(score_all[pl.ds(p.z, 1)], (8, ROWS)), product, (((1,), (0,)), ((), ())),
        precision=HIGH, preferred_element_type=F32,
    )
    misc[...] = jnp.where(
        row8 == 0, score_part[:, :128], jnp.where(row8 == 1, score_part[:, 128:], jnp.where(row8 == 2, loss / 16.0, 0.0))
    )
    mail.finish()


def head(part, x, w, h, dn, keys, qlab, plab, marker, sw, scale):
    return pl.pallas_call(
        head_kernel,
        name="head",
        out_shape=(
            shape((TOK, 2 * GATE), BF16),
            shape((NZ, 128), F32),
            shape((NZ, 128), F32),
            shape((NZ, 8, 128), F32),
            shape((8, D), F32),
            shape((8, 128), F32),
        ),
        in_specs=[VMEM] * 11,
        out_specs=(VMEM,) * 6,
        scratch_shapes=[
            pltpu.VMEM((ROWS, 2 * GATE), BF16),
            pltpu.VMEM((4, 3, ROWS // 2, 2 * GATE), BF16),
            pltpu.VMEM((4, 4, ROWS // 2, 2 * GATE), BF16),
            pltpu.VMEM((NZ, 8, 128), F32),
            pltpu.VMEM((3, NZ, 8, 896), F32),
            pltpu.VMEM((3, 2, 8, 896), F32),
            pltpu.VMEM((NZ, 8, 128), F32),
            pltpu.SemaphoreType.DMA((72,)),
            pltpu.SemaphoreType.DMA((72,)),
        ],
        compiler_params=pltpu.CompilerParams(collective_id=2, has_side_effects=True, vmem_limit_bytes=VMEM_LIMIT),
    )(part, x, w, h, dn, keys, qlab, plab, marker, sw, scale)


def add_into(acc, others):
    value = acc[...].astype(F32)
    for other in others:
        value = value + other[...].astype(F32)
    acc[...] = value.astype(BF16)


def ring_sum(mail, key, pos, nxt, prv, get, half, hbuf, fbuf):
    at = lambda d: lax.rem(pos + d, 4)
    mail.send(key, half(get(at(2)), 0), hbuf.at[0], nxt)
    mail.send(key + 1, half(get(at(2)), 1), hbuf.at[1], prv)
    yield
    mail.arrive(key, hbuf.at[0], prv)
    add_into(half(get(at(1)), 0), [hbuf.at[0]])
    mail.send(key + 2, get(at(1)), fbuf.at[0], nxt)
    mail.arrive(key + 1, hbuf.at[1], nxt)
    add_into(half(get(at(3)), 1), [hbuf.at[1]])
    mail.send(key + 3, get(at(3)), fbuf.at[1], prv)
    yield
    mail.arrive(key + 2, fbuf.at[0], prv)
    mail.arrive(key + 3, fbuf.at[1], nxt)


def reduce_kernel(
    up, dn, gt, misc, up_out, dn_out, gate_out, misc_out,
    up0, dn0, gt0, up_acc, dn_acc, g_acc, u_yh, u_yf, u_xh, u_xf, d_xh, d_xf, d_yh, d_yf,
    g_stage, g_recv, g_y, g_x, g_c, m_z, m_y, m_x, m_c, send_sem, recv_sem,
):
    p = Place()
    mail = Mail(send_sem, recv_sem)
    mate = p.at(c=1 - p.c)
    y_dev = lambda y: p.at(y=y)
    x_dev = lambda x: p.at(x=x)
    z_dev = lambda z: p.at(z=z)
    c_dev = lambda c: p.at(c=c)
    meet(
        [mate]
        + [y_dev(p.dy(d)) for d in (1, 2, 3)]
        + [x_dev(p.dx(d)) for d in (1, 2, 3)]
        + [z_dev(p.dz(d)) for d in range(1, NZ)]
    )
    k0 = mail.slots(3)
    mail.send(k0, gt.at[:, lanes_at(1 - p.c, GATE)], gt0, mate)
    mail.send(k0 + 1, up.at[:, 1 - p.c], up0, mate)
    mail.send(k0 + 2, dn.at[:, 1 - p.c], dn0, mate)
    q_lanes = lanes_at(p.q, HID)
    k_up, k_dn = mail.slots(8), mail.slots(8)
    rows_half = lambda ref, i: ref.at[pl.ds(i * 48, 48)]

    def first_sum(src, received, acc):
        def body(i, carry):
            acc[lax.div(i, 4), lax.rem(i, 4)] = (src[i, p.c].astype(F32) + received[i].astype(F32)).astype(BF16)
            return carry

        lax.fori_loop(0, 8, body, 0)

    def up_chain():
        yield
        mail.arrive(k0 + 1, up0, mate)
        first_sum(up, up0, up_acc)
        yield from ring_sum(
            mail, k_up, p.y, y_dev(p.dy(1)), y_dev(p.dy(-1)),
            lambda d: up_acc.at[:, d], lambda ref, i: ref.at[i], u_yh, u_yf,
        )
        add_into(up_acc.at[:, p.y], [u_yf.at[0], u_yf.at[1]])
        chunk = lambda d: up_acc.at[lax.rem(d, 2), p.y, :, lanes_at(lax.div(d, 2), HID)]
        yield from ring_sum(
            mail, k_up + 4, p.x, x_dev(p.dx(1)), x_dev(p.dx(-1)), chunk, rows_half, u_xh, u_xf
        )
        up_out[...] = chunk(p.x)[...].astype(F32) + u_xf[0].astype(F32) + u_xf[1].astype(F32)

    def dn_chain():
        yield
        mail.arrive(k0 + 2, dn0, mate)
        first_sum(dn, dn0, dn_acc)
        chunk_x = lambda d: dn_acc.at[lax.rem(d, 2), :, :, lanes_at(lax.div(d, 2), HID)]
        yield from ring_sum(
            mail, k_dn, p.x, x_dev(p.dx(1)), x_dev(p.dx(-1)),
            chunk_x, lambda ref, i: ref.at[pl.ds(i * 2, 2)], d_xh, d_xf,
        )
        add_into(chunk_x(p.x), [d_xf.at[0], d_xf.at[1]])
        chunk_y = lambda d: dn_acc.at[p.xl, d, :, q_lanes]
        yield from ring_sum(
            mail, k_dn + 4, p.y, y_dev(p.dy(1)), y_dev(p.dy(-1)), chunk_y, rows_half, d_yh, d_yf
        )
        dn_out[...] = chunk_y(p.y)[...].astype(F32) + d_yf[0].astype(F32) + d_yf[1].astype(F32)

    def gate_chain():
        zred = ZReduce(mail, p, g_acc, 192, g_stage, g_recv)
        in_y = Swap(mail, g_y, p.y, 4, y_dev)
        k_x = mail.slots(3)
        in_c = Swap(mail, g_c, p.c, 2, c_dev)
        yield
        mail.arrive(k0, gt0, mate)
        g_acc[...] = (gt[:, lanes_at(p.c, GATE)].astype(F32) + gt0[...].astype(F32)).astype(BF16)
        zred.step(0)
        for s in range(1, 4):
            yield
            zred.step(s)
        yield
        g_y[p.y] = zred.total().astype(BF16)
        in_y.start()
        yield
        in_y.wait()

        def row_sum(q):
            rows = pl.ds(pl.multiple_of(q * 96, 96), 96)
            value = g_y[0, rows].astype(F32)
            for j in range(1, 4):
                value = value + g_y[j, rows].astype(F32)
            return value.astype(BF16)

        g_x[0] = row_sum(p.q)
        for d in (1, 2, 3):
            there = p.dx(d)
            g_x[4 + d] = row_sum(lax.div(there, 2))
            mail.send(k_x + d - 1, g_x.at[4 + d], g_x.at[d], x_dev(there))
        yield
        for d in (1, 2, 3):
            mail.arrive(k_x + d - 1, g_x.at[d], x_dev(p.dx(-d)))
        value = g_x[0].astype(F32)
        for d in (1, 2, 3):
            value = value + g_x[d].astype(F32)
        g_c[p.c] = value.astype(BF16)
        in_c.start()
        yield
        in_c.wait()
        gate_out[...] = g_c[...].astype(F32)

    def misc_chain():
        stages = [
            (Swap(mail, m_z, p.z, NZ, z_dev), m_z, p.z),
            (Swap(mail, m_y, p.y, 4, y_dev), m_y, p.y),
            (Swap(mail, m_x, p.x, 4, x_dev), m_x, p.x),
            (Swap(mail, m_c, p.c, 2, c_dev), m_c, p.c),
        ]
        value = misc[...]
        for swap, buf, me in stages:
            buf[me] = value
            swap.start()
            yield
            value = swap.total()
        misc_out[...] = value

    running = [gate_chain(), up_chain(), dn_chain(), misc_chain()]
    while running:
        left = []
        for chain in running:
            try:
                next(chain)
                left.append(chain)
            except StopIteration:
                pass
        running = left
    mail.finish()


def reduce(up, dn, gt, misc):
    vm = lambda *dims: pltpu.VMEM(dims, BF16)
    return pl.pallas_call(
        reduce_kernel,
        name="reduce",
        out_shape=(
            shape((96, HID), F32),
            shape((96, HID), F32),
            shape((2, 96, GATE), F32),
            shape((8, 128), F32),
        ),
        in_specs=[VMEM] * 4,
        out_specs=(VMEM,) * 4,
        scratch_shapes=[
            vm(8, 96, 2 * HID),
            vm(8, 96, 2 * HID),
            vm(D, GATE),
            vm(2, 4, 96, 2 * HID),
            vm(2, 4, 96, 2 * HID),
            vm(D, GATE),
            vm(2, 96, 2 * HID),
            vm(2, 2, 96, 2 * HID),
            vm(2, 48, HID),
            vm(2, 96, HID),
            vm(2, 2, 96, HID),
            vm(2, 4, 96, HID),
            vm(2, 48, HID),
            vm(2, 96, HID),
            vm(4, 3, 96, GATE),
            vm(4, 4, 96, GATE),
            vm(4, 192, GATE),
            vm(8, 96, GATE),
            vm(2, 96, GATE),
            pltpu.VMEM((NZ, 8, 128), F32),
            pltpu.VMEM((4, 8, 128), F32),
            pltpu.VMEM((4, 8, 128), F32),
            pltpu.VMEM((2, 8, 128), F32),
            pltpu.SemaphoreType.DMA((64,)),
            pltpu.SemaphoreType.DMA((64,)),
        ],
        compiler_params=pltpu.CompilerParams(collective_id=3, has_side_effects=True, vmem_limit_bytes=VMEM_LIMIT),
    )(up.reshape(8, 2, 96, 2 * HID), dn.reshape(8, 2, 96, 2 * HID), gt, misc)


def layer_norm(row_block, ln_gain):
    values = row_block.astype(F32)
    center = values - jnp.mean(values, axis=1, keepdims=True)
    spread = jnp.mean(center * center, axis=1, keepdims=True)
    return (center * lax.rsqrt(spread + 1e-06) * ln_gain).astype(BF16)


def gelu_value(preact):
    return 0.5 * preact * (1.0 + lax.erf(preact * 0.7071067811865476))


def gelu_slope(preact):
    return (
        0.5 * (1.0 + lax.erf(preact * 0.7071067811865476))
        + preact * jnp.exp(-0.5 * preact * preact) * 0.3989422804014327
    )


def dot(a, b, dims=((1,), (0,))):
    return lax.dot_general(a, b, (dims, ((), ())), preferred_element_type=F32)


def per_device(
    patch_class_features, live_tiles, tile_patient, ln_gain, up_weight, down_weight, tanh_weight,
    sigmoid_weight, score_weight, queue_keys, queue_labels, patient_labels, loss_scale,
):
    slot = lax.broadcasted_iota(jnp.int32, (ROWS,), 0)
    marker = jnp.where(slot < live_tiles[0], tile_patient, 16)[None, :]
    normed_own = layer_norm(patch_class_features, ln_gain)
    gate_weight = jnp.concatenate([tanh_weight, sigmoid_weight], axis=1)
    normed, up, down, w = gather(normed_own, up_weight, down_weight, gate_weight)

    key_squares = jnp.einsum("kd,kd->k", queue_keys, queue_keys, preferred_element_type=F32)
    keys = (queue_keys * lax.rsqrt(key_squares + 1e-06)[:, None]).astype(BF16)
    preact = dot(normed, up)
    hidden = gelu_value(preact).astype(BF16)
    through = dot(down, w).astype(BF16)
    part = dot(hidden, through).astype(BF16)
    labels = jnp.concatenate([patient_labels, patient_labels])[:, None]
    uv, score_grads, alpha, mass, pooled_grad, misc = head(
        part, patch_class_features, w, hidden, down, keys, queue_labels[None, :], labels, marker,
        score_weight[None, :], loss_scale.reshape(1, 1),
    )

    pre = (score_grads.reshape(TOK, 1) * uv.astype(F32)).astype(BF16)
    weights = jnp.where(mass > 0.0, alpha[:, None, :], 0.0)[:, :4]
    weights = weights.transpose(0, 2, 1).reshape(TOK, 4).astype(BF16)
    grad4 = pooled_grad[:4].astype(BF16)
    grad_hidden = dot(grad4, down, ((1,), (1,))).astype(BF16)
    hidden_grad = dot(pre, through, ((1,), (1,))) + dot(weights, grad_hidden)
    pre_grad = (hidden_grad * gelu_slope(preact)).astype(BF16)
    up_part = dot(normed, pre_grad, ((0,), (0,))).astype(BF16)
    held = dot(pre, hidden, ((0,), (0,))).astype(BF16)
    held4 = dot(weights, hidden, ((0,), (0,))).astype(BF16)
    down_part = (dot(w, held) + dot(grad4, held4, ((0,), (0,)))).astype(BF16)
    z = lax.axis_index("tile") // 2
    pre_own = lax.dynamic_slice_in_dim(pre, z * ROWS, ROWS, 0)
    gate_part = (dot(down, held, ((0,), (1,))) + dot(patch_class_features, pre_own, ((0,), (0,)))).astype(BF16)
    up_grad, down_grad, gate_grad, total = reduce(up_part, down_part, gate_part, misc)
    return (up_grad, down_grad.T, gate_grad[0], gate_grad[1], total[:2].reshape(2 * 128), total[2, 0])


def solution(mesh):
    placed = (
        P(("pat", "tile"), None),
        P(("pat", "tile")),
        P(("pat", "tile")),
        P(),
        P(None, "tile"),
        P("tile", None),
        P("tile", None),
        P("tile", None),
        P(),
        P("tile", None),
        P("tile"),
        P("pat"),
        P(),
    )
    return jax.shard_map(
        per_device,
        mesh=mesh,
        in_specs=placed,
        out_specs=(P("pat", "tile"), P("tile", "pat"), P("tile", None), P("tile", None), P(), P()),
        check_vma=False,
    )
```

```python
import jax
import jax.numpy as jnp
from jax import lax
from jax.experimental import pallas as pl
from jax.experimental.pallas import tpu as pltpu
from jax.sharding import PartitionSpec as P

MESH = pl.DeviceIdType.MESH
F32 = jnp.float32
BF16 = jnp.bfloat16
HIGH = lax.Precision.HIGHEST
INV_TEMP = 1.0 / 0.07
NZ = 8
NY = 4
NX = 4
ROWS = 128
TOK = NZ * ROWS
D = 1536
HID = 384
GATE = 256
VMEM_LIMIT = 63 << 20


class Place:
    def __init__(self):
        self.pat = lax.axis_index("pat")
        self.tile = lax.axis_index("tile")
        self.z = lax.div(self.tile, 2)
        self.q = lax.rem(self.tile, 2)
        self.xl = lax.div(self.pat, 8)
        self.y = lax.rem(lax.div(self.pat, 2), 4)
        self.c = lax.rem(self.pat, 2)
        self.x = self.q * 2 + self.xl

    def at(self, z=None, y=None, x=None, c=None):
        z = self.z if z is None else z
        y = self.y if y is None else y
        c = self.c if c is None else c
        if x is None:
            xl, q = self.xl, self.q
        else:
            xl, q = lax.rem(x, 2), lax.div(x, 2)
        return (xl * 8 + y * 2 + c, z * 2 + q)

    def dz(self, d):
        return lax.rem(self.z + (d + NZ), NZ)

    def dy(self, d):
        return lax.rem(self.y + (d + NY), NY)

    def dx(self, d):
        return lax.rem(self.x + (d + NX), NX)


def dot(a, b, dims=((1,), (0,))):
    return lax.dot_general(a, b, (dims, ((), ())), preferred_element_type=F32)


class Mail:
    def __init__(self, send_sem, recv_sem):
        self.send_sem, self.recv_sem = send_sem, recv_sem
        self.next = 0
        self.sent = []

    def slots(self, n):
        first = self.next
        self.next += n
        return first

    def send(self, k, src, dst, device):
        copy = pltpu.make_async_remote_copy(
            src_ref=src, dst_ref=dst, send_sem=self.send_sem.at[k], recv_sem=self.recv_sem.at[k],
            device_id=device, device_id_type=MESH,
        )
        copy.start()
        self.sent.append(copy)

    def arrive(self, k, dst, device):
        pltpu.make_async_remote_copy(
            src_ref=dst, dst_ref=dst, send_sem=self.send_sem.at[k], recv_sem=self.recv_sem.at[k],
            device_id=device, device_id_type=MESH,
        ).wait_recv()

    def finish(self):
        for copy in self.sent:
            copy.wait_send()


def rows_at(index, size, offset=0, count=None):
    count = size if count is None else count
    return pl.ds(pl.multiple_of(index * size + offset, 16), count)


def lanes_at(index, size):
    return pl.ds(pl.multiple_of(index * size, 128), size)


class ZGather:
    def __init__(self, mail, place, ref, size):
        self.mail, self.place, self.ref, self.size = mail, place, ref, size
        self.half = size // 2
        self.key = mail.slots(16)
        self.chains = ((1, 0, 4), (-1, 0, 3), (1, 1, 3), (-1, 1, 4))

    def piece(self, owner, half):
        return self.ref.at[rows_at(owner, self.size, half * self.half, self.half)]

    def step(self, s, which=(0, 1, 2, 3)):
        p = self.place
        for i in which:
            way, half, steps = self.chains[i]
            block = self.piece(p.dz(-way * s), half)
            if 0 < s <= steps:
                self.mail.arrive(self.key + i * 4 + s - 1, block, p.at(z=p.dz(-way)))
            if s < steps:
                self.mail.send(self.key + i * 4 + s, block, block, p.at(z=p.dz(way)))


class ZReduce:
    def __init__(self, mail, place, ref, size, stage, recv):
        self.mail, self.place, self.ref, self.size = mail, place, ref, size
        self.stage, self.recv = stage, recv
        self.half = size // 2
        self.key = mail.slots(16)
        self.chains = ((1, 0, 4), (-1, 1, 4), (1, 1, 3), (-1, 0, 3))

    def piece(self, owner, half):
        return rows_at(owner, self.size, half * self.half, self.half)

    def step(self, s):
        p = self.place
        for i, (way, half, steps) in enumerate(self.chains):
            if s < steps:
                dest = self.piece(p.dz(way * (steps - s)), half)
                if s == 0:
                    src = self.ref.at[dest]
                else:
                    self.mail.arrive(self.key + i * 4 + s - 1, self.recv.at[i, s - 1], p.at(z=p.dz(-way)))
                    src = self.stage.at[i, s - 1]
                    src[...] = (self.ref[dest].astype(F32) + self.recv[i, s - 1].astype(F32)).astype(BF16)
                self.mail.send(self.key + i * 4 + s, src, self.recv.at[i, s], p.at(z=p.dz(way)))

    def total(self):
        p = self.place
        for i, (way, half, steps) in enumerate(self.chains):
            self.mail.arrive(self.key + i * 4 + steps - 1, self.recv.at[i, steps - 1], p.at(z=p.dz(-way)))
        first = self.ref[self.piece(p.z, 0)].astype(F32) + self.recv[0, 3].astype(F32) + self.recv[3, 2].astype(F32)
        second = self.ref[self.piece(p.z, 1)].astype(F32) + self.recv[1, 3].astype(F32) + self.recv[2, 2].astype(F32)
        return jnp.concatenate([first, second], axis=0)


class Swap:
    def __init__(self, mail, ref, me, n, device_of):
        self.mail, self.ref, self.me, self.n, self.device_of = mail, ref, me, n, device_of
        self.key = mail.slots(n - 1)

    def other(self, d):
        return lax.rem(self.me + d, self.n)

    def start(self):
        for d in range(1, self.n):
            mine = self.ref.at[self.me]
            self.mail.send(self.key + d - 1, mine, mine, self.device_of(self.other(d)))

    def wait(self):
        for d in range(1, self.n):
            source = self.other(self.n - d)
            self.mail.arrive(self.key + d - 1, self.ref.at[source], self.device_of(source))

    def total(self):
        self.wait()
        value = self.ref[0].astype(F32)
        for j in range(1, self.n):
            value = value + self.ref[j].astype(F32)
        return value


def two_part(a):
    top = a.astype(BF16).astype(F32)
    return jnp.concatenate([top, a - top], axis=0).astype(BF16)


def dot_two(a, b, transposed=False):
    dims = (((1,), (1,)), ((), ())) if transposed else (((1,), (0,)), ((), ()))
    both = lax.dot_general(two_part(a), b, dims, preferred_element_type=F32)
    half = a.shape[0]
    return both[:half] + both[half:]


def add_into(acc, others):
    value = acc[...].astype(F32)
    for other in others:
        value = value + other[...].astype(F32)
    acc[...] = value.astype(BF16)


def ring_sum(mail, key, pos, nxt, prv, get, half, hbuf, fbuf):
    at = lambda d: lax.rem(pos + d, 4)
    mail.send(key, half(get(at(2)), 0), hbuf.at[0], nxt)
    mail.send(key + 1, half(get(at(2)), 1), hbuf.at[1], prv)
    yield
    mail.arrive(key, hbuf.at[0], prv)
    add_into(half(get(at(1)), 0), [hbuf.at[0]])
    mail.send(key + 2, get(at(1)), fbuf.at[0], nxt)
    mail.arrive(key + 1, hbuf.at[1], nxt)
    add_into(half(get(at(3)), 1), [hbuf.at[1]])
    mail.send(key + 3, get(at(3)), fbuf.at[1], prv)
    yield
    mail.arrive(key + 2, fbuf.at[0], prv)
    mail.arrive(key + 3, fbuf.at[1], nxt)


K_GELU = 0.7071067811865476
K_SLOPE = 0.3989422804014327
BLOCK16 = 16


def gelu_rows(pre_t, h_s, slope_s, t, row, lanes):
    v = pre_t[pl.ds(t, BLOCK16)]
    half = 0.5 * (1.0 + lax.erf(v * K_GELU))
    h_s[pl.ds(row, BLOCK16), lanes] = (v * half).astype(BF16)
    slope_s[pl.ds(row, BLOCK16), lanes] = (half + v * jnp.exp(-0.5 * v * v) * K_SLOPE).astype(BF16)


def kernel(
    x_ref, live, tile_patient, gain, up_hbm, dn_hbm, wt, ws, sw_ref, keys_hbm, qlab, plab, scale,
    up_out, dn_out, gate_out, misc_out,
    n_all, n_t, x_t, up_b, dn_b, dn_t, wq, w_x, thru, thru_t, h_s, h_t, slope_s, part, uv_all, keys, keys_t,
    pg_s, pre_s, held_t, held, pre_t,
    stage, recv, pbuf, zbuf, xbuf, sbuf, score_all, alpha_all, col_t,
    gt_p, up0, dn0, gt0, up_acc, dn_acc, g_acc, u_yh, u_yf, u_xh, u_xf, d_xh, d_xf, d_yh, d_yf,
    g_stage, g_recv, g_y, g_x, g_c, m_z, m_y, m_x, m_c,
    send_sem, recv_sem, local_sem,
):
    p = Place()
    mail = Mail(send_sem, recv_sem)
    mate, beside = p.at(c=1 - p.c), p.at(x=3 - p.x)
    above, below = p.at(y=p.dy(1)), p.at(y=p.dy(-1))
    z_dev = lambda z: p.at(z=z)
    y_dev = lambda y: p.at(y=y)
    x_dev = lambda x: p.at(x=x)
    c_dev = lambda c: p.at(c=c)
    q_dev = lambda q: (p.pat, p.z * 2 + q)
    partners = (
        [z_dev(p.dz(d)) for d in range(1, NZ)]
        + [y_dev(p.dy(d)) for d in (1, 2, 3)]
        + [x_dev(p.dx(d)) for d in (1, 2, 3)]
        + [mate]
    )
    barrier = pltpu.get_barrier_semaphore()
    for device in partners:
        pl.semaphore_signal(barrier, inc=1, device_id=device, device_id_type=MESH)

    fetch_up = pltpu.make_async_copy(up_hbm, up_b.at[p.q], local_sem.at[0])
    fetch_dn = pltpu.make_async_copy(dn_hbm, dn_b.at[p.q], local_sem.at[1])
    fetch_keys = pltpu.make_async_copy(keys_hbm, keys, local_sem.at[2])
    fetch_up.start()
    fetch_dn.start()
    fetch_keys.start()

    def norm_rows(i, carry):
        v = x_ref[pl.ds(pl.multiple_of(i * BLOCK16, BLOCK16), BLOCK16)].astype(F32)
        center = v - jnp.mean(v, axis=1, keepdims=True)
        spread = jnp.mean(center * center, axis=1, keepdims=True)
        n_all[pl.ds(pl.multiple_of(p.z * ROWS + i * BLOCK16, BLOCK16), BLOCK16)] = (
            center * lax.rsqrt(spread + 1e-06) * gain[...]
        ).astype(BF16)
        return carry

    g_rows = pl.ds(pl.multiple_of(p.c * 48, 16), 48)
    g_lanes = lanes_at(lax.rem(p.y, 2), 128)
    wq[p.c, p.y, p.z, p.q] = jnp.where(p.y < 2, wt[g_rows, g_lanes], ws[g_rows, g_lanes])

    lax.fori_loop(0, 4, norm_rows, 0)
    pl.semaphore_wait(barrier, len(partners))

    tokens = ZGather(mail, p, n_all, ROWS)
    k_w = mail.slots(1)
    own_w = wq.at[p.c, p.y, p.z, p.q]
    mail.send(k_w, own_w, own_w, beside)
    tokens.step(0, (0, 1))
    lax.fori_loop(4, 8, norm_rows, 0)
    tokens.step(0, (2, 3))

    k_half = mail.slots(2)
    up_half = lambda q, c: up_b.at[q, rows_at(c, 768)]
    dn_half = lambda q, c: dn_b.at[q, rows_at(c, 192)]
    fetch_up.wait()
    mail.send(k_half, up_half(p.q, p.c), up_half(p.q, p.c), beside)
    fetch_dn.wait()
    mail.send(k_half + 1, dn_half(p.q, p.c), dn_half(p.q, p.c), beside)

    def hidden(owners, q):
        lhs = jnp.concatenate([n_all[rows_at(o, ROWS)] for o in owners], axis=0)
        count = len(owners) * ROWS
        pre_t[pl.ds(0, count)] = dot(lhs, up_b[q])
        lanes = lanes_at(q, HID)
        for j, o in enumerate(owners):
            def body(i, carry, j=j, o=o):
                t = pl.multiple_of(j * ROWS + i * BLOCK16, BLOCK16)
                row = pl.multiple_of(o * ROWS + i * BLOCK16, BLOCK16)
                gelu_rows(pre_t, h_s, slope_s, t, row, lanes)
                return carry

            lax.fori_loop(0, ROWS // BLOCK16, body, 0)

    def turn(owners):
        for o in owners:
            n_t[:, lanes_at(o, ROWS)] = n_all[rows_at(o, ROWS)].T

    k_wz = mail.slots(7)
    w_z = lambda z: wq.at[p.c, p.y, z]

    def w_step(s):
        for way, steps, key in ((1, 4, k_wz), (-1, 3, k_wz + 4)):
            block = w_z(p.dz(-way * s))
            if 0 < s <= steps:
                mail.arrive(key + s - 1, block, z_dev(p.dz(-way)))
            if s < steps:
                mail.send(key + s, block, block, z_dev(p.dz(way)))

    mail.arrive(k_w, wq.at[p.c, p.y, p.z, 1 - p.q], beside)
    w_step(0)
    hidden([p.z], p.q)
    turn([p.z])
    x_t[...] = x_ref[...].T
    w_step(1)
    tokens.step(1, (0, 1))
    tokens.step(1, (2, 3))
    w_step(2)
    near = [p.dz(1), p.dz(-1)]
    hidden(near, p.q)
    turn(near)
    w_step(3)
    fetch_keys.wait()

    def key_rows(i, carry):
        at = pl.ds(pl.multiple_of(i * BLOCK16, BLOCK16), BLOCK16)
        v = keys[at].astype(F32)
        keys[at] = (v * lax.rsqrt(jnp.sum(v * v, axis=1, keepdims=True) + 1e-06)).astype(BF16)
        return carry

    lax.fori_loop(0, 32, key_rows, 0)
    w_step(4)
    k_wy = mail.slots(4)
    w_y = lambda y: wq.at[p.c, y]
    w_yh = lambda y, half: wq.at[p.c, y, pl.ds(half * 4, 4)]
    mail.send(k_wy, w_y(p.y), w_y(p.y), above)
    mail.send(k_wy + 1, w_y(p.y), w_y(p.y), below)
    tokens.step(2, (0, 1))
    theirs, other = 1 - p.q, 1 - p.c
    k_mate = mail.slots(3)
    mail.arrive(k_half, up_half(theirs, p.c), beside)
    mail.send(k_mate, up_half(theirs, p.c), up_half(theirs, p.c), mate)
    tokens.step(2, (2, 3))
    lax.fori_loop(32, 64, key_rows, 0)
    mid = [p.dz(2), p.dz(-2)]
    hidden(mid, p.q)
    turn(mid)
    mail.arrive(k_wy, w_y(p.dy(-1)), below)
    mail.send(k_wy + 2, w_yh(p.dy(-1), 0), w_yh(p.dy(-1), 0), above)
    mail.arrive(k_wy + 1, w_y(p.dy(1)), above)
    mail.send(k_wy + 3, w_yh(p.dy(1), 1), w_yh(p.dy(1), 1), below)
    mail.arrive(k_mate, up_half(theirs, other), mate)
    hidden([p.z], theirs)
    hidden(near, theirs)
    tokens.step(3, (0, 1))
    mail.arrive(k_wy + 2, w_yh(p.dy(2), 0), below)
    mail.arrive(k_wy + 3, w_yh(p.dy(2), 1), above)
    mail.send(k_mate + 2, wq.at[p.c], wq.at[p.c], mate)
    tokens.step(3, (2, 3))
    for j in range(2):
        keys_t[:, pl.ds(j * 512, 512)] = keys[pl.ds(j * 512, 512)].T
    hidden(mid, theirs)
    far = [p.dz(3), p.dz(-3)]
    hidden(far, p.q)
    mail.arrive(k_half + 1, dn_half(theirs, p.c), beside)
    mail.send(k_mate + 1, dn_half(theirs, p.c), dn_half(theirs, p.c), mate)
    hidden(far, theirs)
    turn(far)
    mail.arrive(k_mate + 2, wq.at[other], mate)

    def place_w(t, carry):
        for y in range(4):
            for c in range(2):
                row = pl.multiple_of(t * 96 + c * 48, 16)
                w_x[pl.ds(row, 48), pl.ds(y * 128, 128)] = wq[c, y, lax.div(t, 2), lax.rem(t, 2)]
        return carry

    lax.fori_loop(0, 16, place_w, 0)
    w_full = lambda: w_x[:, pl.ds(0, 2 * GATE)]
    mail.arrive(k_mate + 1, dn_half(theirs, other), mate)
    for q in range(2):
        thru[pl.ds(q * HID, HID)] = dot(dn_b[q], w_full()).astype(BF16)

    def gate_part(o, carry):
        at = rows_at(o, ROWS)
        part[at] = dot(h_s[at], thru[...]).astype(BF16)
        return carry

    lax.fori_loop(0, NZ - 1, lambda d, carry: gate_part(lax.rem(p.z + 5 + d, NZ), carry), 0)
    tokens.step(4)
    last = p.dz(4)
    hidden([last], 0)
    hidden([last], 1)
    gate_part(last, 0)

    reduce = ZReduce(mail, p, part, ROWS, stage, recv)
    gather_uv = ZGather(mail, p, uv_all, ROWS)
    swap_p = Swap(mail, pbuf, p.z, NZ, z_dev)
    swap_z = [Swap(mail, zbuf.at[i], p.z, NZ, z_dev) for i in range(3)]
    swap_x = [Swap(mail, xbuf.at[i], p.q, 2, q_dev) for i in range(3)]
    swap_s = Swap(mail, sbuf, p.z, NZ, z_dev)

    row8 = lax.broadcasted_iota(jnp.int32, (8, 128), 0)
    first4 = row8 < 4
    row_patient = lax.rem(row8, 4)
    first4_wide = lax.broadcasted_iota(jnp.int32, (8, 768), 0) < 4
    lane = lax.broadcasted_iota(jnp.int32, (8, 128), 1)

    def pack(v):
        return jnp.where(first4_wide, v[:, :768], v[:, 768:])

    def unpack(v):
        rolled = pltpu.roll(v, 4, 0)
        return jnp.concatenate([jnp.where(first4_wide, v, rolled), jnp.where(first4_wide, rolled, v)], axis=1)

    reduce.step(0)
    turn([last])
    for q in range(2):
        dn_t[:, pl.ds(q * HID, HID)] = dn_b[q].T
    gate_x = dot(x_ref[...], w_full())
    reduce.step(1)
    same = jnp.zeros((8, 1024), jnp.int32)
    row_wide = lax.rem(lax.broadcasted_iota(jnp.int32, (8, 1024), 0), 4)
    labels = jnp.broadcast_to(qlab[...], (8, 1024))
    for k in range(4):
        same = jnp.where((row_wide == k) & (labels == plab[k]), 1, same)
    same = same.astype(F32)
    label_sums = dot(same.astype(BF16), keys[...])
    positives = jnp.sum(same, axis=1, keepdims=True)
    reduce.step(2)
    for z in range(NZ):
        h_t[:, pl.ds(z * ROWS, ROWS)] = h_s[pl.ds(z * ROWS, ROWS)].T
    reduce.step(3)
    gates = reduce.total() + gate_x
    tanh_val = jnp.tanh(gates[:, :GATE])
    sigmoid_val = jax.nn.sigmoid(gates[:, GATE:])
    product = tanh_val * sigmoid_val
    sw = sw_ref[...]
    score = lax.dot_general(
        jnp.broadcast_to(sw, (8, GATE)), product, (((1,), (1,)), ((), ())), precision=HIGH, preferred_element_type=F32
    )
    in_tile = lax.broadcasted_iota(jnp.int32, (8, 128), 1) < live[0]
    onehot = (jnp.broadcast_to(tile_patient[...], (8, 128)) == row_patient) & in_tile
    mass = jnp.where(onehot, jnp.exp(score), 0.0)
    pbuf[p.z] = mass
    swap_p.start()
    common = sw * sigmoid_val
    own_rows = rows_at(p.z, ROWS)
    uv_all[own_rows, pl.ds(0, GATE)] = (common * (1.0 - tanh_val * tanh_val)).astype(BF16)
    uv_all[own_rows, pl.ds(GATE, GATE)] = (common * tanh_val * (1.0 - sigmoid_val)).astype(BF16)
    gather_uv.step(0)
    vec_x = dot_two(mass, x_ref[...])
    swap_p.wait()

    total = jnp.zeros((8, 1), F32)
    for z in range(NZ):
        total += jnp.sum(pbuf[z], axis=1, keepdims=True)
    mass_all = jnp.concatenate([pbuf[z] for z in range(NZ)], axis=1)
    mass_h = dot_two(mass_all, h_s[...])
    vec = dot_two(mass_h[:, :HID], dn_b[0]) + dot_two(mass_h[:, HID:], dn_b[1]) + vec_x

    def post(i, packed, small):
        zbuf[i, p.z, :, pl.ds(0, 768)] = packed
        zbuf[i, p.z, :, pl.ds(768, 128)] = small
        swap_z[i].start()

    def collect_z(i):
        xbuf[i, p.q] = swap_z[i].total()
        swap_x[i].start()

    post(0, pack(vec), jnp.broadcast_to(total, (8, 128)))
    gather_uv.step(1)
    collect_z(0)
    post(1, pack(label_sums), jnp.broadcast_to(positives, (8, 128)))
    summed = swap_x[0].total()
    total_mass = summed[:, 768:769]
    pooled = unpack(summed[:, :768]) / total_mass
    length = jnp.sqrt(jnp.sum(pooled * pooled, axis=1, keepdims=True) + 1e-06)
    unit = pooled / length

    logits = dot(unit.astype(BF16), keys_t[...]) / 0.07
    exps = jnp.exp(logits)
    exp_part = jnp.sum(exps, axis=1, keepdims=True)
    pos_part = jnp.sum(same * logits, axis=1, keepdims=True)
    post(2, pack(dot_two(exps, keys[...])), jnp.where(lane == 0, exp_part, pos_part))
    gather_uv.step(2)
    collect_z(1)
    thru_t[...] = thru[...].T
    gather_uv.step(3)
    collect_z(2)
    gather_uv.step(4)

    def scaled(b, carry):
        at = rows_at(b, ROWS)
        pre_t[pl.ds(0, ROWS)] = dot(uv_all[at], thru_t[:, pl.ds(0, HID)])
        pre_t[pl.ds(ROWS, ROWS)] = dot(uv_all[at], thru_t[:, pl.ds(HID, HID)])

        def body(i, inner):
            t = pl.multiple_of(i * BLOCK16, BLOCK16)
            row = pl.ds(pl.multiple_of(b * ROWS + t, BLOCK16), BLOCK16)
            for q in range(2):
                lanes = pl.ds(q * HID, HID)
                v = pre_t[pl.ds(pl.multiple_of(q * ROWS + t, BLOCK16), BLOCK16)]
                pg_s[row, lanes] = (v * slope_s[row, lanes].astype(F32)).astype(BF16)
            return inner

        lax.fori_loop(0, ROWS // BLOCK16, body, 0)
        return carry

    labels_total = swap_x[1].total()
    pos_count = labels_total[:, 768:769]
    queue_total = swap_x[2].total()
    exp_total = queue_total[:, 768:769]
    pos_logits = queue_total[:, 769:770]
    unit_grad = (scale[0] * INV_TEMP) * (
        unpack(queue_total[:, :768]) / exp_total - unpack(labels_total[:, :768]) / pos_count
    )
    pooled_grad = (unit_grad - unit * jnp.sum(unit * unit_grad, axis=1, keepdims=True)) / length

    grad_h = dot_two(pooled_grad, dn_t[...])
    own_dots = dot_two(pooled_grad, x_t[...])
    dots = dot_two(grad_h, h_t[...])
    for z in range(NZ):
        block = dots[:, z * ROWS : (z + 1) * ROWS] + jnp.where(p.z == z, own_dots, 0.0)
        picked = jnp.where((pbuf[z] > 0.0) & first4, block, 0.0)
        sbuf[p.z, pl.ds(z, 1)] = jnp.sum(picked, axis=0, keepdims=True)
    swap_s.start()
    center = jnp.sum(pooled * pooled_grad, axis=1, keepdims=True)
    log_part = jnp.log(exp_total) - pos_logits / pos_count
    loss = jnp.sum(jnp.where(first4, jnp.broadcast_to(log_part, (8, 128)), 0.0), axis=0, keepdims=True)
    for z in range(NZ):
        block = jnp.where(first4, pbuf[z], 0.0)
        alpha_all[pl.ds(z, 1)] = jnp.sum(block / total_mass, axis=0, keepdims=True)
        score_all[pl.ds(z, 1)] = jnp.sum(jnp.where(block > 0.0, center, 0.0), axis=0, keepdims=True)
    lax.fori_loop(0, NZ, scaled, 0)
    pad = jnp.zeros((120, 768), F32)
    grad_h_pad = jnp.concatenate([jnp.where(first4_wide, grad_h, 0.0), pad], axis=0).astype(BF16)
    grad_pad = jnp.concatenate([pooled_grad, jnp.zeros((120, D), F32)], axis=0)
    for j in range(D // 128):
        w_x[pl.ds(j * 128, 128), pl.ds(512, 128)] = grad_pad[:, j * 128 : (j + 1) * 128].T.astype(BF16)
    score_all[...] = alpha_all[...] * (swap_s.total() - score_all[...])

    def columns(b, carry):
        mass_b = jnp.where(first4, pbuf[b], 0.0)
        weight = jnp.where(mass_b > 0.0, jnp.broadcast_to(alpha_all[pl.ds(b, 1)], (8, 128)), 0.0)
        grad = jnp.broadcast_to(score_all[pl.ds(b, 1)], (8, 128))
        turned = jnp.concatenate([weight, grad, jnp.zeros((112, 128), F32)], axis=0).T
        col_t[...] = turned
        at = rows_at(b, ROWS)
        both = dot(turned.astype(BF16), grad_h_pad)
        pre_t[pl.ds(0, ROWS)] = both[:, :HID]
        pre_t[pl.ds(ROWS, ROWS)] = both[:, HID:]

        def body(i, inner):
            t = pl.multiple_of(i * BLOCK16, BLOCK16)
            row = pl.ds(pl.multiple_of(b * ROWS + t, BLOCK16), BLOCK16)
            s = col_t[pl.ds(t, BLOCK16)][:, 8:9]
            pre_s[row] = (s * uv_all[row].astype(F32)).astype(BF16)
            for q in range(2):
                lanes = pl.ds(q * HID, HID)
                v = pre_t[pl.ds(pl.multiple_of(q * ROWS + t, BLOCK16), BLOCK16)]
                pg_s[row, lanes] = (
                    s * pg_s[row, lanes].astype(F32) + v * slope_s[row, lanes].astype(F32)
                ).astype(BF16)
            return inner

        lax.fori_loop(0, ROWS // BLOCK16, body, 0)
        return carry + dot_two(weight, h_s[at])

    held4 = lax.fori_loop(0, NZ, columns, jnp.zeros((8, 768), F32))
    score_part = lax.dot_general(
        jnp.broadcast_to(score_all[pl.ds(p.z, 1)], (8, ROWS)), product, (((1,), (0,)), ((), ())),
        precision=HIGH, preferred_element_type=F32,
    )
    misc = jnp.where(
        row8 == 0, score_part[:, :128], jnp.where(row8 == 1, score_part[:, 128:], jnp.where(row8 == 2, loss / 16.0, 0.0))
    )

    def misc_chain(value):
        stages = [
            (Swap(mail, m_z, p.z, NZ, z_dev), m_z, p.z),
            (Swap(mail, m_y, p.y, 4, y_dev), m_y, p.y),
            (Swap(mail, m_x, p.x, 4, x_dev), m_x, p.x),
            (Swap(mail, m_c, p.c, 2, c_dev), m_c, p.c),
        ]
        for swap, buf, me in stages:
            buf[me] = value
            swap.start()
            yield
            value = swap.total()
        misc_out[...] = value
        yield

    misc_steps = misc_chain(misc)
    next(misc_steps)

    for j in range(3):
        held_t[pl.ds(j * 256, 256)] = dot(h_t[pl.ds(j * 256, 256)], pre_s[...]).astype(BF16)

    def gate_rows(i, carry):
        at = pl.ds(pl.multiple_of(i * 256, 256), 256)
        gt_p[at] = (dot(dn_t[at], held_t[...]) + dot(x_t[at], pre_s[own_rows])).astype(BF16)
        return carry

    lax.fori_loop(0, 6, gate_rows, 0)
    k_gt = mail.slots(1)
    mail.send(k_gt, gt_p.at[:, lanes_at(other, GATE)], gt0, mate)
    held[pl.ds(0, 512)] = held_t[...].T
    held[pl.ds(512, 128)] = jnp.concatenate([jnp.where(first4_wide, held4, 0.0), pad], axis=0).astype(BF16)

    up_p = lambda i, c: keys_t.at[pl.ds(pl.multiple_of((i * 2 + c) * 96, 96), 96), pl.ds(0, 768)]
    dn_p = lambda i, c: keys.at[
        pl.ds(pl.multiple_of((lax.rem(i, 4) * 2 + c) * 96, 96), 96), lanes_at(lax.div(i, 4), 768)
    ]
    k_up0, k_dn0 = mail.slots(8), mail.slots(8)

    def compute(block, lhs, rhs, index, k, buf):
        def body(j, carry):
            i = index(j)
            value = dot(lhs[pl.ds(pl.multiple_of(i * 192, 192), 192)], rhs[...]).astype(BF16)
            block(i, 0)[...] = value[:96]
            block(i, 1)[...] = value[96:]
            return carry

        lax.fori_loop(0, 2, body, 0)
        for j in range(2):
            mail.send(k + j, block(index(j), other), buf.at[index(j)], mate)

    def collect(block, index, k, buf, acc):
        for j in range(2):
            mail.arrive(k + j, buf.at[index(j)], mate)

        def body(j, carry):
            i = index(j)
            acc[lax.div(i, 4), lax.rem(i, 4)] = (block(i, p.c)[...].astype(F32) + buf[i].astype(F32)).astype(BF16)
            return carry

        lax.fori_loop(0, 2, body, 0)

    up_index = [lambda j, d=d: j * 4 + p.dy(d) for d in (2, 1, -1, 0)]
    dn_index = [lambda j, x=x, h=h: x * 4 + h * 2 + j for x in (p.xl, 1 - p.xl) for h in (0, 1)]
    up_go = lambda g: compute(up_p, n_t, pg_s, up_index[g], k_up0 + 2 * g, up0)
    up_take = lambda g: collect(up_p, up_index[g], k_up0 + 2 * g, up0, up_acc)
    dn_go = lambda g: compute(dn_p, w_x, held, dn_index[g], k_dn0 + 2 * g, dn0)
    dn_take = lambda g: collect(dn_p, dn_index[g], k_dn0 + 2 * g, dn0, dn_acc)
    rows_half = lambda ref, i: ref.at[pl.ds(i * 48, 48)]
    k_up, k_dn = mail.slots(8), mail.slots(8)
    up_chunk = lambda d: up_acc.at[lax.rem(d, 2), p.y, :, lanes_at(lax.div(d, 2), HID)]
    dn_chunk_x = lambda d: dn_acc.at[lax.rem(d, 2), :, :, lanes_at(lax.div(d, 2), HID)]
    dn_chunk = lambda d: dn_acc.at[p.xl, d, :, lanes_at(p.q, HID)]
    up_y = ring_sum(
        mail, k_up, p.y, above, below, lambda d: up_acc.at[:, d], lambda ref, i: ref.at[i], u_yh, u_yf
    )
    up_x = ring_sum(mail, k_up + 4, p.x, x_dev(p.dx(1)), x_dev(p.dx(-1)), up_chunk, rows_half, u_xh, u_xf)
    dn_x = ring_sum(
        mail, k_dn, p.x, x_dev(p.dx(1)), x_dev(p.dx(-1)), dn_chunk_x, lambda ref, i: ref.at[pl.ds(i * 2, 2)], d_xh, d_xf
    )
    dn_y = ring_sum(mail, k_dn + 4, p.y, above, below, dn_chunk, rows_half, d_yh, d_yf)
    step = lambda chain: next(chain, None)
    zred = ZReduce(mail, p, g_acc, 192, g_stage, g_recv)
    in_y = Swap(mail, g_y, p.y, 4, y_dev)
    k_x = mail.slots(3)
    in_c = Swap(mail, g_c, p.c, 2, c_dev)

    up_go(0)
    mail.arrive(k_gt, gt0, mate)
    g_acc[...] = (gt_p[:, lanes_at(p.c, GATE)].astype(F32) + gt0[...].astype(F32)).astype(BF16)
    zred.step(0)
    up_go(1)
    up_take(0)
    step(up_y)
    step(misc_steps)
    zred.step(1)
    up_go(2)
    dn_go(0)
    zred.step(2)
    dn_go(1)
    up_take(1)
    up_take(2)
    step(up_y)
    dn_take(0)
    dn_take(1)
    step(dn_x)
    zred.step(3)
    step(misc_steps)
    dn_go(2)
    dn_go(3)
    up_go(3)
    g_y[p.y] = zred.total().astype(BF16)
    in_y.start()
    dn_take(2)
    dn_take(3)
    step(dn_x)
    up_take(3)
    step(misc_steps)
    step(up_y)
    add_into(up_acc.at[:, p.y], [u_yf.at[0], u_yf.at[1]])
    step(up_x)
    in_y.wait()

    def row_sum(q):
        rows = pl.ds(pl.multiple_of(q * 96, 96), 96)
        value = g_y[0, rows].astype(F32)
        for j in range(1, 4):
            value = value + g_y[j, rows].astype(F32)
        return value.astype(BF16)

    for d in (1, 2, 3):
        there = p.dx(d)
        g_x[4 + d] = row_sum(lax.div(there, 2))
        mail.send(k_x + d - 1, g_x.at[4 + d], g_x.at[d], x_dev(there))
    g_x[0] = row_sum(p.q)
    step(dn_x)
    add_into(dn_chunk_x(p.x), [d_xf.at[0], d_xf.at[1]])
    step(dn_y)
    step(up_x)
    step(misc_steps)
    for d in (1, 2, 3):
        mail.arrive(k_x + d - 1, g_x.at[d], x_dev(p.dx(-d)))
    value = g_x[0].astype(F32)
    for d in (1, 2, 3):
        value = value + g_x[d].astype(F32)
    g_c[p.c] = value.astype(BF16)
    in_c.start()
    step(dn_y)
    step(up_x)
    up_out[...] = up_chunk(p.x)[...].astype(F32) + u_xf[0].astype(F32) + u_xf[1].astype(F32)
    in_c.wait()
    gate_out[...] = g_c[...].astype(F32)
    step(dn_y)
    dn_out[...] = (dn_chunk(p.y)[...].astype(F32) + d_yf[0].astype(F32) + d_yf[1].astype(F32)).T
    mail.finish()


ANY = pl.BlockSpec(memory_space=pl.ANY)
VMEM = pl.BlockSpec(memory_space=pltpu.VMEM)
SMEM = pl.BlockSpec(memory_space=pltpu.SMEM)


def per_device(
    patch_class_features, live_tiles, tile_patient, ln_gain, up_weight, down_weight, tanh_weight,
    sigmoid_weight, score_weight, queue_keys, queue_labels, patient_labels, loss_scale,
):
    out = lambda *dims: jax.ShapeDtypeStruct(dims, F32)
    vm = lambda *dims: pltpu.VMEM(dims, BF16)
    vf = lambda *dims: pltpu.VMEM(dims, F32)
    up_grad, down_grad, gate_grad, total = pl.pallas_call(
        kernel,
        name="step",
        out_shape=(out(96, HID), out(HID, 96), out(2, 96, GATE), out(8, 128)),
        in_specs=[VMEM, SMEM, VMEM, VMEM, ANY, ANY, VMEM, VMEM, VMEM, ANY, VMEM, SMEM, SMEM],
        out_specs=(VMEM,) * 4,
        scratch_shapes=[
            vm(TOK, D),
            vm(D, TOK),
            vm(D, ROWS),
            vm(2, D, HID),
            vm(2, HID, D),
            vm(D, 2 * HID),
            vm(2, 4, NZ, 2, 48, 128),
            vm(D, 640),
            vm(2 * HID, 2 * GATE),
            vm(2 * GATE, 2 * HID),
            vm(TOK, 2 * HID),
            vm(2 * HID, TOK),
            vm(TOK, 2 * HID),
            vm(TOK, 2 * GATE),
            vm(TOK, 2 * GATE),
            vm(1024, D),
            vm(D, 1024),
            vm(TOK, 2 * HID),
            vm(TOK, 2 * GATE),
            vm(2 * HID, 2 * GATE),
            vm(640, 2 * HID),
            vf(256, HID),
            vm(4, 3, ROWS // 2, 2 * GATE),
            vm(4, 4, ROWS // 2, 2 * GATE),
            vf(NZ, 8, 128),
            vf(3, NZ, 8, 896),
            vf(3, 2, 8, 896),
            vf(NZ, 8, 128),
            vf(NZ, 128),
            vf(NZ, 128),
            vf(128, 128),
            vm(D, 2 * GATE),
            vm(8, 96, 2 * HID),
            vm(8, 96, 2 * HID),
            vm(D, GATE),
            vm(2, 4, 96, 2 * HID),
            vm(2, 4, 96, 2 * HID),
            vm(D, GATE),
            vm(2, 96, 2 * HID),
            vm(2, 2, 96, 2 * HID),
            vm(2, 48, HID),
            vm(2, 96, HID),
            vm(2, 2, 96, HID),
            vm(2, 4, 96, HID),
            vm(2, 48, HID),
            vm(2, 96, HID),
            vm(4, 3, 96, GATE),
            vm(4, 4, 96, GATE),
            vm(4, 192, GATE),
            vm(8, 96, GATE),
            vm(2, 96, GATE),
            vf(NZ, 8, 128),
            vf(4, 8, 128),
            vf(4, 8, 128),
            vf(2, 8, 128),
            pltpu.SemaphoreType.DMA((192,)),
            pltpu.SemaphoreType.DMA((192,)),
            pltpu.SemaphoreType.DMA((4,)),
        ],
        compiler_params=pltpu.CompilerParams(collective_id=1, has_side_effects=True, vmem_limit_bytes=VMEM_LIMIT),
    )(
        patch_class_features, live_tiles, tile_patient[None, :], ln_gain[None, :], up_weight, down_weight,
        tanh_weight, sigmoid_weight, score_weight[None, :], queue_keys, queue_labels[None, :], patient_labels,
        loss_scale.reshape(1),
    )
    return (up_grad, down_grad, gate_grad[0], gate_grad[1], total[:2].reshape(2 * 128), total[2, 0])


def solution(mesh):
    placed = (
        P(("pat", "tile"), None),
        P(("pat", "tile")),
        P(("pat", "tile")),
        P(),
        P(None, "tile"),
        P("tile", None),
        P("tile", None),
        P("tile", None),
        P(),
        P("tile", None),
        P("tile"),
        P("pat"),
        P(),
    )
    return jax.shard_map(
        per_device,
        mesh=mesh,
        in_specs=placed,
        out_specs=(P("pat", "tile"), P("tile", "pat"), P("tile", None), P("tile", None), P(), P()),
        check_vma=False,
    )
```

```python
import jax
import jax.numpy as jnp
from jax import lax
from jax.experimental import pallas as pl
from jax.experimental.pallas import tpu as pltpu
from jax.sharding import PartitionSpec as P

MESH = pl.DeviceIdType.MESH
F32 = jnp.float32
BF16 = jnp.bfloat16
HIGH = lax.Precision.HIGHEST
INV_TEMP = 1.0 / 0.07
NZ = 8
NY = 4
NX = 4
ROWS = 128
TOK = NZ * ROWS
D = 1536
HID = 384
GATE = 256
VMEM_LIMIT = 63 << 20


class Place:
    def __init__(self):
        self.pat = lax.axis_index("pat")
        self.tile = lax.axis_index("tile")
        self.z = lax.div(self.tile, 2)
        self.q = lax.rem(self.tile, 2)
        self.xl = lax.div(self.pat, 8)
        self.y = lax.rem(lax.div(self.pat, 2), 4)
        self.c = lax.rem(self.pat, 2)
        self.x = self.q * 2 + self.xl

    def at(self, z=None, y=None, x=None, c=None):
        z = self.z if z is None else z
        y = self.y if y is None else y
        c = self.c if c is None else c
        if x is None:
            xl, q = self.xl, self.q
        else:
            xl, q = lax.rem(x, 2), lax.div(x, 2)
        return (xl * 8 + y * 2 + c, z * 2 + q)

    def dz(self, d):
        return lax.rem(self.z + (d + NZ), NZ)

    def dy(self, d):
        return lax.rem(self.y + (d + NY), NY)

    def dx(self, d):
        return lax.rem(self.x + (d + NX), NX)


def dot(a, b, dims=((1,), (0,))):
    return lax.dot_general(a, b, (dims, ((), ())), preferred_element_type=F32)


class Mail:
    def __init__(self, send_sem, recv_sem):
        self.send_sem, self.recv_sem = send_sem, recv_sem
        self.next = 0
        self.sent = []

    def slots(self, n):
        first = self.next
        self.next += n
        return first

    def send(self, k, src, dst, device):
        copy = pltpu.make_async_remote_copy(
            src_ref=src, dst_ref=dst, send_sem=self.send_sem.at[k], recv_sem=self.recv_sem.at[k],
            device_id=device, device_id_type=MESH,
        )
        copy.start()
        self.sent.append(copy)

    def arrive(self, k, dst, device):
        pltpu.make_async_remote_copy(
            src_ref=dst, dst_ref=dst, send_sem=self.send_sem.at[k], recv_sem=self.recv_sem.at[k],
            device_id=device, device_id_type=MESH,
        ).wait_recv()

    def finish(self):
        for copy in self.sent:
            copy.wait_send()


def rows_at(index, size, offset=0, count=None):
    count = size if count is None else count
    return pl.ds(pl.multiple_of(index * size + offset, 16), count)


def lanes_at(index, size):
    return pl.ds(pl.multiple_of(index * size, 128), size)


class ZGather:
    def __init__(self, mail, place, ref, size):
        self.mail, self.place, self.ref, self.size = mail, place, ref, size
        self.half = size // 2
        self.key = mail.slots(16)
        self.chains = ((1, 0, 4), (-1, 0, 3), (1, 1, 3), (-1, 1, 4))

    def piece(self, owner, half):
        return self.ref.at[rows_at(owner, self.size, half * self.half, self.half)]

    def step(self, s, which=(0, 1, 2, 3)):
        p = self.place
        for i in which:
            way, half, steps = self.chains[i]
            block = self.piece(p.dz(-way * s), half)
            if 0 < s <= steps:
                self.mail.arrive(self.key + i * 4 + s - 1, block, p.at(z=p.dz(-way)))
            if s < steps:
                self.mail.send(self.key + i * 4 + s, block, block, p.at(z=p.dz(way)))


class ZReduce:
    def __init__(self, mail, place, ref, size, stage, recv):
        self.mail, self.place, self.ref, self.size = mail, place, ref, size
        self.stage, self.recv = stage, recv
        self.half = size // 2
        self.key = mail.slots(16)
        self.chains = ((1, 0, 4), (-1, 1, 4), (1, 1, 3), (-1, 0, 3))

    def piece(self, owner, half):
        return rows_at(owner, self.size, half * self.half, self.half)

    def step(self, s):
        p = self.place
        for i, (way, half, steps) in enumerate(self.chains):
            if s < steps:
                dest = self.piece(p.dz(way * (steps - s)), half)
                if s == 0:
                    src = self.ref.at[dest]
                else:
                    self.mail.arrive(self.key + i * 4 + s - 1, self.recv.at[i, s - 1], p.at(z=p.dz(-way)))
                    src = self.stage.at[i, s - 1]
                    src[...] = (self.ref[dest].astype(F32) + self.recv[i, s - 1].astype(F32)).astype(BF16)
                self.mail.send(self.key + i * 4 + s, src, self.recv.at[i, s], p.at(z=p.dz(way)))

    def total(self):
        p = self.place
        for i, (way, half, steps) in enumerate(self.chains):
            self.mail.arrive(self.key + i * 4 + steps - 1, self.recv.at[i, steps - 1], p.at(z=p.dz(-way)))
        first = self.ref[self.piece(p.z, 0)].astype(F32) + self.recv[0, 3].astype(F32) + self.recv[3, 2].astype(F32)
        second = self.ref[self.piece(p.z, 1)].astype(F32) + self.recv[1, 3].astype(F32) + self.recv[2, 2].astype(F32)
        return jnp.concatenate([first, second], axis=0)


class Swap:
    def __init__(self, mail, ref, me, n, device_of):
        self.mail, self.ref, self.me, self.n, self.device_of = mail, ref, me, n, device_of
        self.key = mail.slots(n - 1)

    def other(self, d):
        return lax.rem(self.me + d, self.n)

    def start(self):
        for d in range(1, self.n):
            mine = self.ref.at[self.me]
            self.mail.send(self.key + d - 1, mine, mine, self.device_of(self.other(d)))

    def wait(self):
        for d in range(1, self.n):
            source = self.other(self.n - d)
            self.mail.arrive(self.key + d - 1, self.ref.at[source], self.device_of(source))

    def total(self):
        self.wait()
        value = self.ref[0].astype(F32)
        for j in range(1, self.n):
            value = value + self.ref[j].astype(F32)
        return value


def two_part(a):
    top = a.astype(BF16).astype(F32)
    return jnp.concatenate([top, a - top], axis=0).astype(BF16)


def dot_two(a, b, transposed=False):
    dims = (((1,), (1,)), ((), ())) if transposed else (((1,), (0,)), ((), ()))
    both = lax.dot_general(two_part(a), b, dims, preferred_element_type=F32)
    half = a.shape[0]
    return both[:half] + both[half:]


def add_into(acc, others):
    value = acc[...].astype(F32)
    for other in others:
        value = value + other[...].astype(F32)
    acc[...] = value.astype(BF16)


def ring_sum(mail, key, pos, nxt, prv, get, half, hbuf, fbuf):
    at = lambda d: lax.rem(pos + d, 4)
    mail.send(key, half(get(at(2)), 0), hbuf.at[0], nxt)
    mail.send(key + 1, half(get(at(2)), 1), hbuf.at[1], prv)
    yield
    mail.arrive(key, hbuf.at[0], prv)
    add_into(half(get(at(1)), 0), [hbuf.at[0]])
    mail.send(key + 2, get(at(1)), fbuf.at[0], nxt)
    mail.arrive(key + 1, hbuf.at[1], nxt)
    add_into(half(get(at(3)), 1), [hbuf.at[1]])
    mail.send(key + 3, get(at(3)), fbuf.at[1], prv)
    yield
    mail.arrive(key + 2, fbuf.at[0], prv)
    mail.arrive(key + 3, fbuf.at[1], nxt)


K_GELU = 0.7071067811865476
K_SLOPE = 0.3989422804014327
BLOCK16 = 16


def gelu_rows(pre_t, h_s, slope_s, t, row, lanes):
    v = pre_t[pl.ds(t, BLOCK16)]
    half = 0.5 * (1.0 + lax.erf(v * K_GELU))
    h_s[pl.ds(row, BLOCK16), lanes] = (v * half).astype(BF16)
    slope_s[pl.ds(row, BLOCK16), lanes] = (half + v * jnp.exp(-0.5 * v * v) * K_SLOPE).astype(BF16)


def kernel(
    x_ref, live, tile_patient, gain, up_hbm, dn_hbm, wt, ws, sw_ref, keys_hbm, qlab, plab, scale,
    up_out, dn_out, gate_out, misc_out,
    n_all, n_t, x_t, up_b, dn_b, dn_t, wq, w_x, thru, thru_t, h_s, h_t, slope_s, part, uv_all, keys, keys_t,
    pg_s, pre_s, held_t, held, pre_t,
    stage, recv, pbuf, zbuf, xbuf, sbuf, score_all, alpha_all, pull_s,
    gt_p, up0, dn0, gt0, up_acc, dn_acc, g_acc, u_yh, u_yf, u_xh, u_xf, d_xh, d_xf, d_yh, d_yf,
    g_stage, g_recv, g_y, g_x, g_c, m_z, m_y, m_x, m_c,
    send_sem, recv_sem, local_sem,
):
    p = Place()
    mail = Mail(send_sem, recv_sem)
    mate, beside = p.at(c=1 - p.c), p.at(x=3 - p.x)
    above, below = p.at(y=p.dy(1)), p.at(y=p.dy(-1))
    z_dev = lambda z: p.at(z=z)
    y_dev = lambda y: p.at(y=y)
    x_dev = lambda x: p.at(x=x)
    c_dev = lambda c: p.at(c=c)
    q_dev = lambda q: (p.pat, p.z * 2 + q)
    partners = (
        [z_dev(p.dz(d)) for d in range(1, NZ)]
        + [y_dev(p.dy(d)) for d in (1, 2, 3)]
        + [x_dev(p.dx(d)) for d in (1, 2, 3)]
        + [mate]
    )
    barrier = pltpu.get_barrier_semaphore()
    for device in partners:
        pl.semaphore_signal(barrier, inc=1, device_id=device, device_id_type=MESH)

    fetch_up = pltpu.make_async_copy(up_hbm, up_b.at[p.q], local_sem.at[0])
    fetch_dn = pltpu.make_async_copy(dn_hbm, dn_b.at[p.q], local_sem.at[1])
    fetch_keys = pltpu.make_async_copy(keys_hbm, keys, local_sem.at[2])
    fetch_up.start()
    fetch_dn.start()
    fetch_keys.start()

    def norm_rows(half):
        v = x_ref[pl.ds(half * 64, 64)].astype(F32)
        center = v - jnp.mean(v, axis=1, keepdims=True)
        spread = jnp.mean(center * center, axis=1, keepdims=True)
        n_all[rows_at(p.z, ROWS, half * 64, 64)] = (center * lax.rsqrt(spread + 1e-06) * gain[...][None, :]).astype(BF16)

    g_rows = pl.ds(pl.multiple_of(p.c * 48, 16), 48)
    g_lanes = lanes_at(lax.rem(p.y, 2), 128)
    wq[p.c, p.y, p.z, p.q] = jnp.where(p.y < 2, wt[g_rows, g_lanes], ws[g_rows, g_lanes])

    norm_rows(0)
    pl.semaphore_wait(barrier, len(partners))

    tokens = ZGather(mail, p, n_all, ROWS)
    k_w = mail.slots(1)
    own_w = wq.at[p.c, p.y, p.z, p.q]
    mail.send(k_w, own_w, own_w, beside)
    tokens.step(0, (0, 1))
    norm_rows(1)
    tokens.step(0, (2, 3))

    up_piece = lambda q, y, c: up_b.at[q, rows_at(y * 2 + c, 192)]
    dn_piece = lambda q, y, c: dn_b.at[q, rows_at(y * 2 + c, 48)]
    theirs, other = 1 - p.q, 1 - p.c
    k_px, k_py, k_pm = mail.slots(2), mail.slots(6), mail.slots(8)
    fetch_up.wait()
    mail.send(k_px, up_piece(p.q, p.y, p.c), up_piece(p.q, p.y, p.c), beside)
    fetch_dn.wait()
    mail.send(k_px + 1, dn_piece(p.q, p.y, p.c), dn_piece(p.q, p.y, p.c), beside)

    def to_mate(d, piece, which):
        mail.send(k_pm + which * 4 + d, piece(theirs, p.dy(d), p.c), piece(theirs, p.dy(d), p.c), mate)

    def pieces_x():
        for which, piece in enumerate((up_piece, dn_piece)):
            block = piece(theirs, p.y, p.c)
            mail.arrive(k_px + which, block, beside)
            mail.send(k_py + which * 2, block, block, above)
            mail.send(k_py + which * 2 + 1, block, block, below)
            to_mate(0, piece, which)

    def pieces_y():
        for which, piece in enumerate((up_piece, dn_piece)):
            under, over = piece(theirs, p.dy(-1), p.c), piece(theirs, p.dy(1), p.c)
            mail.arrive(k_py + which * 2, under, below)
            if which == 0:
                mail.send(k_py + 4, under, under, above)
            to_mate(3, piece, which)
            mail.arrive(k_py + which * 2 + 1, over, above)
            if which == 1:
                mail.send(k_py + 5, over, over, below)
            to_mate(1, piece, which)

    def pieces_far():
        mail.arrive(k_py + 4, up_piece(theirs, p.dy(2), p.c), below)
        to_mate(2, up_piece, 0)
        mail.arrive(k_py + 5, dn_piece(theirs, p.dy(2), p.c), above)
        to_mate(2, dn_piece, 1)

    def pieces_mate(which):
        piece = (up_piece, dn_piece)[which]
        for d in range(4):
            mail.arrive(k_pm + which * 4 + d, piece(theirs, p.dy(d), other), mate)

    def hidden(owners, q):
        lhs = jnp.concatenate([n_all[rows_at(o, ROWS)] for o in owners], axis=0)
        count = len(owners) * ROWS
        pre_t[pl.ds(0, count)] = dot(lhs, up_b[q])
        lanes = lanes_at(q, HID)
        for j, o in enumerate(owners):
            def body(i, carry, j=j, o=o):
                t = pl.multiple_of(j * ROWS + i * BLOCK16, BLOCK16)
                row = pl.multiple_of(o * ROWS + i * BLOCK16, BLOCK16)
                gelu_rows(pre_t, h_s, slope_s, t, row, lanes)
                return carry

            lax.fori_loop(0, ROWS // BLOCK16, body, 0)

    def turn(owners):
        for o in owners:
            n_t[:, lanes_at(o, ROWS)] = n_all[rows_at(o, ROWS)].T

    k_wz = mail.slots(7)
    w_z = lambda z: wq.at[p.c, p.y, z]

    def w_step(s):
        for way, steps, key in ((1, 4, k_wz), (-1, 3, k_wz + 4)):
            block = w_z(p.dz(-way * s))
            if 0 < s <= steps:
                mail.arrive(key + s - 1, block, z_dev(p.dz(-way)))
            if s < steps:
                mail.send(key + s, block, block, z_dev(p.dz(way)))

    def key_rows(i):
        at = pl.ds(i * 256, 256)
        v = keys[at].astype(F32)
        keys[at] = (v * lax.rsqrt(jnp.sum(v * v, axis=1, keepdims=True) + 1e-06)).astype(BF16)

    k_wy, k_wm = mail.slots(4), mail.slots(1)
    w_y = lambda y: wq.at[p.c, y]
    w_yh = lambda y, half: wq.at[p.c, y, pl.ds(half * 4, 4)]
    near = [p.dz(1), p.dz(-1)]
    mid = [p.dz(2), p.dz(-2)]
    far = [p.dz(3), p.dz(-3)]

    mail.arrive(k_w, wq.at[p.c, p.y, p.z, 1 - p.q], beside)
    w_step(0)
    hidden([p.z], p.q)
    turn([p.z])
    x_t[...] = x_ref[...].T
    w_step(1)
    tokens.step(1, (0, 1))
    fetch_keys.wait()
    key_rows(0)
    pieces_x()
    w_step(2)
    tokens.step(1, (2, 3))
    w_step(3)
    hidden(near, p.q)
    turn(near)
    key_rows(1)
    w_step(4)
    mail.send(k_wy, w_y(p.y), w_y(p.y), above)
    mail.send(k_wy + 1, w_y(p.y), w_y(p.y), below)
    tokens.step(2, (0, 1))
    pieces_y()
    key_rows(2)
    key_rows(3)
    tokens.step(2, (2, 3))
    hidden(mid, p.q)
    turn(mid)
    mail.arrive(k_wy, w_y(p.dy(-1)), below)
    mail.send(k_wy + 2, w_yh(p.dy(-1), 0), w_yh(p.dy(-1), 0), above)
    mail.arrive(k_wy + 1, w_y(p.dy(1)), above)
    mail.send(k_wy + 3, w_yh(p.dy(1), 1), w_yh(p.dy(1), 1), below)
    pieces_far()
    tokens.step(3, (0, 1))
    mail.arrive(k_wy + 2, w_yh(p.dy(2), 0), below)
    mail.arrive(k_wy + 3, w_yh(p.dy(2), 1), above)
    mail.send(k_wm, wq.at[p.c], wq.at[p.c], mate)
    pieces_mate(0)
    hidden([p.z], theirs)
    hidden(near, theirs)
    hidden(mid, theirs)
    for j in range(2):
        keys_t[:, pl.ds(j * 512, 512)] = keys[pl.ds(j * 512, 512)].T
    tokens.step(3, (2, 3))
    hidden(far, p.q)
    hidden(far, theirs)
    turn(far)
    mail.arrive(k_wm, wq.at[other], mate)

    def place_w(t, carry):
        for y in range(4):
            for c in range(2):
                row = pl.multiple_of(t * 96 + c * 48, 16)
                w_x[pl.ds(row, 48), pl.ds(y * 128, 128)] = wq[c, y, lax.div(t, 2), lax.rem(t, 2)]
        return carry

    lax.fori_loop(0, 16, place_w, 0)
    w_full = lambda: w_x[:, pl.ds(0, 2 * GATE)]
    pieces_mate(1)
    for q in range(2):
        thru[pl.ds(q * HID, HID)] = dot(dn_b[q], w_full()).astype(BF16)

    def gate_part(o, carry):
        at = rows_at(o, ROWS)
        part[at] = dot(h_s[at], thru[...]).astype(BF16)
        return carry

    lax.fori_loop(0, NZ - 1, lambda d, carry: gate_part(lax.rem(p.z + 5 + d, NZ), carry), 0)
    tokens.step(4)
    last = p.dz(4)
    hidden([last], 0)
    hidden([last], 1)
    gate_part(last, 0)

    reduce = ZReduce(mail, p, part, ROWS, stage, recv)
    gather_uv = ZGather(mail, p, uv_all, ROWS)
    swap_p = Swap(mail, pbuf, p.z, NZ, z_dev)
    swap_z = [Swap(mail, zbuf.at[i], p.z, NZ, z_dev) for i in range(3)]
    swap_x = [Swap(mail, xbuf.at[i], p.q, 2, q_dev) for i in range(3)]
    swap_s = Swap(mail, sbuf, p.z, NZ, z_dev)

    row8 = lax.broadcasted_iota(jnp.int32, (8, 128), 0)
    first4 = row8 < 4
    row_patient = lax.rem(row8, 4)
    first4_wide = lax.broadcasted_iota(jnp.int32, (8, 768), 0) < 4
    lane = lax.broadcasted_iota(jnp.int32, (8, 128), 1)

    def pack(v):
        return jnp.where(first4_wide, v[:, :768], v[:, 768:])

    def unpack(v):
        rolled = pltpu.roll(v, 4, 0)
        return jnp.concatenate([jnp.where(first4_wide, v, rolled), jnp.where(first4_wide, rolled, v)], axis=1)

    reduce.step(0)
    turn([last])
    for q in range(2):
        dn_t[:, pl.ds(q * HID, HID)] = dn_b[q].T
    gate_x = dot(x_ref[...], w_full())
    reduce.step(1)
    same = jnp.zeros((8, 1024), jnp.int32)
    row_wide = lax.rem(lax.broadcasted_iota(jnp.int32, (8, 1024), 0), 4)
    labels = jnp.broadcast_to(qlab[...], (8, 1024))
    for k in range(4):
        same = jnp.where((row_wide == k) & (labels == plab[k]), 1, same)
    same = same.astype(F32)
    label_sums = dot(same.astype(BF16), keys[...])
    positives = jnp.sum(same, axis=1, keepdims=True)
    reduce.step(2)
    for z in range(NZ):
        h_t[:, pl.ds(z * ROWS, ROWS)] = h_s[pl.ds(z * ROWS, ROWS)].T
    reduce.step(3)
    gates = reduce.total() + gate_x
    tanh_val = jnp.tanh(gates[:, :GATE])
    sigmoid_val = jax.nn.sigmoid(gates[:, GATE:])
    product = tanh_val * sigmoid_val
    sw = sw_ref[...]
    score = lax.dot_general(
        jnp.broadcast_to(sw, (8, GATE)), product, (((1,), (1,)), ((), ())), precision=HIGH, preferred_element_type=F32
    )
    in_tile = lax.broadcasted_iota(jnp.int32, (8, 128), 1) < live[0]
    onehot = (jnp.broadcast_to(tile_patient[...], (8, 128)) == row_patient) & in_tile
    mass = jnp.where(onehot, jnp.exp(score), 0.0)
    pbuf[p.z] = mass
    swap_p.start()
    common = sw * sigmoid_val
    own_rows = rows_at(p.z, ROWS)
    uv_all[own_rows, pl.ds(0, GATE)] = (common * (1.0 - tanh_val * tanh_val)).astype(BF16)
    uv_all[own_rows, pl.ds(GATE, GATE)] = (common * tanh_val * (1.0 - sigmoid_val)).astype(BF16)
    gather_uv.step(0)

    def post(i, packed, small):
        zbuf[i, p.z, :, pl.ds(0, 768)] = packed
        zbuf[i, p.z, :, pl.ds(768, 128)] = small
        swap_z[i].start()

    def collect_z(i):
        xbuf[i, p.q] = swap_z[i].total()
        swap_x[i].start()

    post(1, pack(label_sums), jnp.broadcast_to(positives, (8, 128)))
    vec_x = dot_two(mass, x_ref[...])
    swap_p.wait()

    total = jnp.zeros((8, 1), F32)
    for z in range(NZ):
        total += jnp.sum(pbuf[z], axis=1, keepdims=True)
    mass_all = jnp.concatenate([pbuf[z] for z in range(NZ)], axis=1)
    mass_h = dot_two(mass_all, h_s[...])
    vec = dot_two(mass_h[:, :HID], dn_b[0]) + dot_two(mass_h[:, HID:], dn_b[1]) + vec_x

    post(0, pack(vec), jnp.broadcast_to(total, (8, 128)))
    collect_z(0)
    gather_uv.step(1)
    collect_z(1)
    thru_t[...] = thru[...].T
    summed = swap_x[0].total()
    total_mass = summed[:, 768:769]
    pooled = unpack(summed[:, :768]) / total_mass
    length = jnp.sqrt(jnp.sum(pooled * pooled, axis=1, keepdims=True) + 1e-06)
    unit = pooled / length

    logits = dot(unit.astype(BF16), keys_t[...]) / 0.07
    exps = jnp.exp(logits)
    exp_part = jnp.sum(exps, axis=1, keepdims=True)
    pos_part = jnp.sum(same * logits, axis=1, keepdims=True)
    post(2, pack(dot_two(exps, keys[...])), jnp.where(lane == 0, exp_part, pos_part))
    collect_z(2)
    gather_uv.step(2)
    labels_total = swap_x[1].total()
    pos_count = labels_total[:, 768:769]
    queue_total = swap_x[2].total()
    exp_total = queue_total[:, 768:769]
    pos_logits = queue_total[:, 769:770]
    unit_grad = (scale[0] * INV_TEMP) * (
        unpack(queue_total[:, :768]) / exp_total - unpack(labels_total[:, :768]) / pos_count
    )
    pooled_grad = (unit_grad - unit * jnp.sum(unit * unit_grad, axis=1, keepdims=True)) / length

    grad_h = dot_two(pooled_grad, dn_t[...])
    own_dots = dot_two(pooled_grad, x_t[...])
    dots = dot_two(grad_h, h_t[...])
    for z in range(NZ):
        block = dots[:, z * ROWS : (z + 1) * ROWS] + jnp.where(p.z == z, own_dots, 0.0)
        picked = jnp.where((pbuf[z] > 0.0) & first4, block, 0.0)
        sbuf[p.z, pl.ds(z, 1)] = jnp.sum(picked, axis=0, keepdims=True)
    swap_s.start()
    center = jnp.sum(pooled * pooled_grad, axis=1, keepdims=True)
    log_part = jnp.log(exp_total) - pos_logits / pos_count
    loss = jnp.sum(jnp.where(first4, jnp.broadcast_to(log_part, (8, 128)), 0.0), axis=0, keepdims=True)
    for z in range(NZ):
        block = jnp.where(first4, pbuf[z], 0.0)
        alpha_all[pl.ds(z, 1)] = jnp.sum(block / total_mass, axis=0, keepdims=True)
        score_all[pl.ds(z, 1)] = jnp.sum(jnp.where(block > 0.0, center, 0.0), axis=0, keepdims=True)
    gather_uv.step(3)
    pad = jnp.zeros((120, 768), F32)
    grad_h_pad = jnp.concatenate([jnp.where(first4_wide, grad_h, 0.0), pad], axis=0).astype(BF16)
    rest = jnp.zeros((120, 128), F32)

    def pulled(b, carry):
        mass_b = jnp.where(first4, pbuf[b], 0.0)
        weight = jnp.where(mass_b > 0.0, jnp.broadcast_to(alpha_all[pl.ds(b, 1)], (8, 128)), 0.0)
        at = rows_at(b, ROWS)
        turned = jnp.concatenate([weight, rest], axis=0).T.astype(BF16)
        pull_s[at] = (dot(turned, grad_h_pad) * slope_s[at].astype(F32)).astype(BF16)
        return carry + dot_two(weight, h_s[at])

    held4 = lax.fori_loop(0, NZ, pulled, jnp.zeros((8, 768), F32))
    held[pl.ds(512, 128)] = jnp.concatenate([jnp.where(first4_wide, held4, 0.0), pad], axis=0).astype(BF16)
    grad_pad = jnp.concatenate([pooled_grad, jnp.zeros((120, D), F32)], axis=0)
    for j in range(D // 128):
        w_x[pl.ds(j * 128, 128), pl.ds(512, 128)] = grad_pad[:, j * 128 : (j + 1) * 128].T.astype(BF16)
    gather_uv.step(4)

    def scaled(b, carry):
        at = pl.ds(pl.multiple_of(b * 256, 256), 256)
        pg_s[at] = (dot(uv_all[at], thru_t[...]) * slope_s[at].astype(F32)).astype(BF16)
        return carry

    lax.fori_loop(0, 4, scaled, 0)
    score_all[...] = alpha_all[...] * (swap_s.total() - score_all[...])

    def apply_scores(b, carry):
        at = rows_at(b, ROWS)
        grad = jnp.broadcast_to(score_all[pl.ds(b, 1)], (ROWS, ROWS)).T[:, 0:1]
        pre_s[at] = (grad * uv_all[at].astype(F32)).astype(BF16)
        pg_s[at] = (grad * pg_s[at].astype(F32) + pull_s[at].astype(F32)).astype(BF16)
        return carry

    lax.fori_loop(0, NZ, apply_scores, 0)
    score_part = lax.dot_general(
        jnp.broadcast_to(score_all[pl.ds(p.z, 1)], (8, ROWS)), product, (((1,), (0,)), ((), ())),
        precision=HIGH, preferred_element_type=F32,
    )
    misc = jnp.where(
        row8 == 0, score_part[:, :128], jnp.where(row8 == 1, score_part[:, 128:], jnp.where(row8 == 2, loss / 16.0, 0.0))
    )

    def misc_chain(value):
        stages = [
            (Swap(mail, m_z, p.z, NZ, z_dev), m_z, p.z),
            (Swap(mail, m_y, p.y, 4, y_dev), m_y, p.y),
            (Swap(mail, m_x, p.x, 4, x_dev), m_x, p.x),
            (Swap(mail, m_c, p.c, 2, c_dev), m_c, p.c),
        ]
        for swap, buf, me in stages:
            buf[me] = value
            swap.start()
            yield
            value = swap.total()
        misc_out[...] = value
        yield

    misc_steps = misc_chain(misc)
    next(misc_steps)

    def gate_grads():
        for j in range(3):
            held_t[pl.ds(j * 256, 256)] = dot(h_t[pl.ds(j * 256, 256)], pre_s[...]).astype(BF16)

        def gate_rows(i, carry):
            at = pl.ds(pl.multiple_of(i * 512, 512), 512)
            gt_p[at] = (dot(dn_t[at], held_t[...]) + dot(x_t[at], pre_s[own_rows])).astype(BF16)
            return carry

        lax.fori_loop(0, 3, gate_rows, 0)
        mail.send(k_gt, gt_p.at[:, lanes_at(other, GATE)], gt0, mate)
        held[pl.ds(0, 512)] = held_t[...].T

    k_gt = mail.slots(1)
    up_p = lambda i, c: keys_t.at[pl.ds(pl.multiple_of((i * 2 + c) * 96, 96), 96), pl.ds(0, 768)]
    dn_p = lambda i, c: keys.at[
        pl.ds(pl.multiple_of((lax.rem(i, 4) * 2 + c) * 96, 96), 96), lanes_at(lax.div(i, 4), 768)
    ]
    k_up0, k_dn0 = mail.slots(8), mail.slots(8)

    def compute(block, lhs, rhs, index, k, buf):
        def body(j, carry):
            i = index(j)
            value = dot(lhs[pl.ds(pl.multiple_of(i * 192, 192), 192)], rhs[...]).astype(BF16)
            block(i, 0)[...] = value[:96]
            block(i, 1)[...] = value[96:]
            return carry

        lax.fori_loop(0, 2, body, 0)
        for j in range(2):
            mail.send(k + j, block(index(j), other), buf.at[index(j)], mate)

    def collect(block, index, k, buf, acc):
        for j in range(2):
            mail.arrive(k + j, buf.at[index(j)], mate)

        def body(j, carry):
            i = index(j)
            acc[lax.div(i, 4), lax.rem(i, 4)] = (block(i, p.c)[...].astype(F32) + buf[i].astype(F32)).astype(BF16)
            return carry

        lax.fori_loop(0, 2, body, 0)

    up_index = [lambda j, d=d: j * 4 + p.dy(d) for d in (2, 1, -1, 0)]
    dn_index = [lambda j, x=x, h=h: x * 4 + h * 2 + j for x in (p.xl, 1 - p.xl) for h in (0, 1)]
    up_go = lambda g: compute(up_p, n_t, pg_s, up_index[g], k_up0 + 2 * g, up0)
    up_take = lambda g: collect(up_p, up_index[g], k_up0 + 2 * g, up0, up_acc)
    dn_go = lambda g: compute(dn_p, w_x, held, dn_index[g], k_dn0 + 2 * g, dn0)
    dn_take = lambda g: collect(dn_p, dn_index[g], k_dn0 + 2 * g, dn0, dn_acc)
    rows_half = lambda ref, i: ref.at[pl.ds(i * 48, 48)]
    k_up, k_dn = mail.slots(8), mail.slots(8)
    up_chunk = lambda d: up_acc.at[lax.rem(d, 2), p.y, :, lanes_at(lax.div(d, 2), HID)]
    dn_chunk_x = lambda d: dn_acc.at[lax.rem(d, 2), :, :, lanes_at(lax.div(d, 2), HID)]
    dn_chunk = lambda d: dn_acc.at[p.xl, d, :, lanes_at(p.q, HID)]
    up_y = ring_sum(
        mail, k_up, p.y, above, below, lambda d: up_acc.at[:, d], lambda ref, i: ref.at[i], u_yh, u_yf
    )
    up_x = ring_sum(mail, k_up + 4, p.x, x_dev(p.dx(1)), x_dev(p.dx(-1)), up_chunk, rows_half, u_xh, u_xf)
    dn_x = ring_sum(
        mail, k_dn, p.x, x_dev(p.dx(1)), x_dev(p.dx(-1)), dn_chunk_x, lambda ref, i: ref.at[pl.ds(i * 2, 2)], d_xh, d_xf
    )
    dn_y = ring_sum(mail, k_dn + 4, p.y, above, below, dn_chunk, rows_half, d_yh, d_yf)
    step = lambda chain: next(chain, None)
    zred = ZReduce(mail, p, g_acc, 192, g_stage, g_recv)
    in_y = Swap(mail, g_y, p.y, 4, y_dev)
    k_x = mail.slots(3)
    in_c = Swap(mail, g_c, p.c, 2, c_dev)

    def row_sum(q):
        rows = pl.ds(pl.multiple_of(q * 96, 96), 96)
        value = g_y[0, rows].astype(F32)
        for j in range(1, 4):
            value = value + g_y[j, rows].astype(F32)
        return value.astype(BF16)

    up_go(0)
    up_go(1)
    gate_grads()
    up_take(0)
    step(up_y)
    up_go(2)
    dn_go(0)
    mail.arrive(k_gt, gt0, mate)
    g_acc[...] = (gt_p[:, lanes_at(p.c, GATE)].astype(F32) + gt0[...].astype(F32)).astype(BF16)
    zred.step(0)
    dn_go(1)
    step(misc_steps)
    up_take(1)
    up_take(2)
    step(up_y)
    zred.step(1)
    dn_take(0)
    dn_take(1)
    step(dn_x)
    dn_go(2)
    dn_go(3)
    zred.step(2)
    up_go(3)
    step(misc_steps)
    dn_take(2)
    dn_take(3)
    step(dn_x)
    zred.step(3)
    up_take(3)
    step(up_y)
    add_into(up_acc.at[:, p.y], [u_yf.at[0], u_yf.at[1]])
    step(up_x)
    g_y[p.y] = zred.total().astype(BF16)
    in_y.start()
    step(misc_steps)
    step(dn_x)
    add_into(dn_chunk_x(p.x), [d_xf.at[0], d_xf.at[1]])
    step(dn_y)
    step(up_x)
    in_y.wait()
    for d in (1, 2, 3):
        there = p.dx(d)
        g_x[4 + d] = row_sum(lax.div(there, 2))
        mail.send(k_x + d - 1, g_x.at[4 + d], g_x.at[d], x_dev(there))
    g_x[0] = row_sum(p.q)
    step(misc_steps)
    step(dn_y)
    step(up_x)
    up_out[...] = up_chunk(p.x)[...].astype(F32) + u_xf[0].astype(F32) + u_xf[1].astype(F32)
    for d in (1, 2, 3):
        mail.arrive(k_x + d - 1, g_x.at[d], x_dev(p.dx(-d)))
    value = g_x[0].astype(F32)
    for d in (1, 2, 3):
        value = value + g_x[d].astype(F32)
    g_c[p.c] = value.astype(BF16)
    in_c.start()
    step(dn_y)
    dn_out[...] = dn_chunk(p.y)[...].astype(F32) + d_yf[0].astype(F32) + d_yf[1].astype(F32)
    in_c.wait()
    gate_out[...] = g_c[...].astype(F32)
    mail.finish()


ANY = pl.BlockSpec(memory_space=pl.ANY)
VMEM = pl.BlockSpec(memory_space=pltpu.VMEM)
SMEM = pl.BlockSpec(memory_space=pltpu.SMEM)


def hand_out(up, dn, gate, total, loss, up_out, dn_out, tanh_out, sigmoid_out, score_out, loss_out):
    up_out[...] = up[...]
    dn_out[...] = dn[...]
    tanh_out[...] = gate[0]
    sigmoid_out[...] = gate[1]
    score_out[pl.ds(0, 128)] = total[0]
    score_out[pl.ds(128, 128)] = total[1]
    loss_out[0] = loss[2, 0]


def per_device(
    patch_class_features, live_tiles, tile_patient, ln_gain, up_weight, down_weight, tanh_weight,
    sigmoid_weight, score_weight, queue_keys, queue_labels, patient_labels, loss_scale,
):
    out = lambda *dims: jax.ShapeDtypeStruct(dims, F32)
    vm = lambda *dims: pltpu.VMEM(dims, BF16)
    vf = lambda *dims: pltpu.VMEM(dims, F32)
    up_grad, down_grad, gate_grad, total = pl.pallas_call(
        kernel,
        name="step",
        out_shape=(out(96, HID), out(96, HID), out(2, 96, GATE), out(8, 128)),
        in_specs=[VMEM, SMEM, VMEM, VMEM, ANY, ANY, VMEM, VMEM, VMEM, ANY, VMEM, SMEM, SMEM],
        out_specs=(VMEM,) * 4,
        scratch_shapes=[
            vm(TOK, D),
            vm(D, TOK),
            vm(D, ROWS),
            vm(2, D, HID),
            vm(2, HID, D),
            vm(D, 2 * HID),
            vm(2, 4, NZ, 2, 48, 128),
            vm(D, 640),
            vm(2 * HID, 2 * GATE),
            vm(2 * GATE, 2 * HID),
            vm(TOK, 2 * HID),
            vm(2 * HID, TOK),
            vm(TOK, 2 * HID),
            vm(TOK, 2 * GATE),
            vm(TOK, 2 * GATE),
            vm(1024, D),
            vm(D, 1024),
            vm(TOK, 2 * HID),
            vm(TOK, 2 * GATE),
            vm(2 * HID, 2 * GATE),
            vm(640, 2 * HID),
            vf(256, HID),
            vm(4, 3, ROWS // 2, 2 * GATE),
            vm(4, 4, ROWS // 2, 2 * GATE),
            vf(NZ, 8, 128),
            vf(3, NZ, 8, 896),
            vf(3, 2, 8, 896),
            vf(NZ, 8, 128),
            vf(NZ, 128),
            vf(NZ, 128),
            vm(TOK, 2 * HID),
            vm(D, 2 * GATE),
            vm(8, 96, 2 * HID),
            vm(8, 96, 2 * HID),
            vm(D, GATE),
            vm(2, 4, 96, 2 * HID),
            vm(2, 4, 96, 2 * HID),
            vm(D, GATE),
            vm(2, 96, 2 * HID),
            vm(2, 2, 96, 2 * HID),
            vm(2, 48, HID),
            vm(2, 96, HID),
            vm(2, 2, 96, HID),
            vm(2, 4, 96, HID),
            vm(2, 48, HID),
            vm(2, 96, HID),
            vm(4, 3, 96, GATE),
            vm(4, 4, 96, GATE),
            vm(4, 192, GATE),
            vm(8, 96, GATE),
            vm(2, 96, GATE),
            vf(NZ, 8, 128),
            vf(4, 8, 128),
            vf(4, 8, 128),
            vf(2, 8, 128),
            pltpu.SemaphoreType.DMA((192,)),
            pltpu.SemaphoreType.DMA((192,)),
            pltpu.SemaphoreType.DMA((4,)),
        ],
        compiler_params=pltpu.CompilerParams(collective_id=1, has_side_effects=True, vmem_limit_bytes=VMEM_LIMIT),
    )(
        patch_class_features, live_tiles, tile_patient[None, :], ln_gain, up_weight, down_weight,
        tanh_weight, sigmoid_weight, score_weight[None, :], queue_keys, queue_labels[None, :], patient_labels,
        loss_scale.reshape(1),
    )
    outputs = pl.pallas_call(
        hand_out,
        name="hand_out",
        out_shape=(out(96, HID), out(96, HID), out(96, GATE), out(96, GATE), out(GATE), out(1)),
        in_specs=[VMEM] * 4 + [SMEM],
        out_specs=(VMEM,) * 5 + (SMEM,),
    )(up_grad, down_grad, gate_grad, total, total)
    return (outputs[0], outputs[1].T, *outputs[2:5], outputs[5].reshape(()))


def solution(mesh):
    placed = (
        P(("pat", "tile"), None),
        P(("pat", "tile")),
        P(("pat", "tile")),
        P(),
        P(None, "tile"),
        P("tile", None),
        P("tile", None),
        P("tile", None),
        P(),
        P("tile", None),
        P("tile"),
        P("pat"),
        P(),
    )
    return jax.shard_map(
        per_device,
        mesh=mesh,
        in_specs=placed,
        out_specs=(P("pat", "tile"), P("tile", "pat"), P("tile", None), P("tile", None), P(), P()),
        check_vma=False,
    )
```

```python
import jax
import jax.numpy as jnp
from jax import lax
from jax.experimental import pallas as pl
from jax.experimental.pallas import tpu as pltpu
from jax.sharding import PartitionSpec as P

MESH = pl.DeviceIdType.MESH
F32 = jnp.float32
BF16 = jnp.bfloat16
HIGH = lax.Precision.HIGHEST
INV_TEMP = 1.0 / 0.07
NZ = 8
NY = 4
NX = 4
ROWS = 128
TOK = NZ * ROWS
D = 1536
HID = 384
GATE = 256
VMEM_LIMIT = 63 << 20


class Place:
    def __init__(self):
        self.pat = lax.axis_index("pat")
        self.tile = lax.axis_index("tile")
        self.z = lax.div(self.tile, 2)
        self.q = lax.rem(self.tile, 2)
        self.xl = lax.div(self.pat, 8)
        self.y = lax.rem(lax.div(self.pat, 2), 4)
        self.c = lax.rem(self.pat, 2)
        self.x = self.q * 2 + self.xl

    def at(self, z=None, y=None, x=None, c=None):
        z = self.z if z is None else z
        y = self.y if y is None else y
        c = self.c if c is None else c
        if x is None:
            xl, q = self.xl, self.q
        else:
            xl, q = lax.rem(x, 2), lax.div(x, 2)
        return (xl * 8 + y * 2 + c, z * 2 + q)

    def dz(self, d):
        return lax.rem(self.z + (d + NZ), NZ)

    def dy(self, d):
        return lax.rem(self.y + (d + NY), NY)

    def dx(self, d):
        return lax.rem(self.x + (d + NX), NX)


def dot(a, b, dims=((1,), (0,))):
    return lax.dot_general(a, b, (dims, ((), ())), preferred_element_type=F32)


class Mail:
    def __init__(self, send_sem, recv_sem):
        self.send_sem, self.recv_sem = send_sem, recv_sem
        self.next = 0
        self.sent = []

    def slots(self, n):
        first = self.next
        self.next += n
        return first

    def send(self, k, src, dst, device):
        copy = pltpu.make_async_remote_copy(
            src_ref=src, dst_ref=dst, send_sem=self.send_sem.at[k], recv_sem=self.recv_sem.at[k],
            device_id=device, device_id_type=MESH,
        )
        copy.start()
        self.sent.append(copy)

    def arrive(self, k, dst, device):
        pltpu.make_async_remote_copy(
            src_ref=dst, dst_ref=dst, send_sem=self.send_sem.at[k], recv_sem=self.recv_sem.at[k],
            device_id=device, device_id_type=MESH,
        ).wait_recv()

    def finish(self):
        for copy in self.sent:
            copy.wait_send()


def rows_at(index, size, offset=0, count=None):
    count = size if count is None else count
    return pl.ds(pl.multiple_of(index * size + offset, 16), count)


def lanes_at(index, size):
    return pl.ds(pl.multiple_of(index * size, 128), size)


class ZGather:
    def __init__(self, mail, place, ref, size):
        self.mail, self.place, self.ref, self.size = mail, place, ref, size
        self.half = size // 2
        self.key = mail.slots(16)
        self.chains = ((1, 0, 4), (-1, 0, 3), (1, 1, 3), (-1, 1, 4))

    def piece(self, owner, half):
        return self.ref.at[rows_at(owner, self.size, half * self.half, self.half)]

    def step(self, s, which=(0, 1, 2, 3)):
        p = self.place
        for i in which:
            way, half, steps = self.chains[i]
            block = self.piece(p.dz(-way * s), half)
            if 0 < s <= steps:
                self.mail.arrive(self.key + i * 4 + s - 1, block, p.at(z=p.dz(-way)))
            if s < steps:
                self.mail.send(self.key + i * 4 + s, block, block, p.at(z=p.dz(way)))


class ZReduce:
    def __init__(self, mail, place, ref, size, stage, recv):
        self.mail, self.place, self.ref, self.size = mail, place, ref, size
        self.stage, self.recv = stage, recv
        self.half = size // 2
        self.key = mail.slots(16)
        self.chains = ((1, 0, 4), (-1, 1, 4), (1, 1, 3), (-1, 0, 3))

    def piece(self, owner, half):
        return rows_at(owner, self.size, half * self.half, self.half)

    def step(self, s, which=(0, 1, 2, 3)):
        p = self.place
        for i in which:
            way, half, steps = self.chains[i]
            if s < steps:
                dest = self.piece(p.dz(way * (steps - s)), half)
                if s == 0:
                    src = self.ref.at[dest]
                else:
                    self.mail.arrive(self.key + i * 4 + s - 1, self.recv.at[i, s - 1], p.at(z=p.dz(-way)))
                    src = self.stage.at[i, s - 1]
                    src[...] = (self.ref[dest].astype(F32) + self.recv[i, s - 1].astype(F32)).astype(BF16)
                self.mail.send(self.key + i * 4 + s, src, self.recv.at[i, s], p.at(z=p.dz(way)))

    def total(self):
        p = self.place
        for i, (way, half, steps) in enumerate(self.chains):
            self.mail.arrive(self.key + i * 4 + steps - 1, self.recv.at[i, steps - 1], p.at(z=p.dz(-way)))
        first = self.ref[self.piece(p.z, 0)].astype(F32) + self.recv[0, 3].astype(F32) + self.recv[3, 2].astype(F32)
        second = self.ref[self.piece(p.z, 1)].astype(F32) + self.recv[1, 3].astype(F32) + self.recv[2, 2].astype(F32)
        return jnp.concatenate([first, second], axis=0)


class Swap:
    def __init__(self, mail, ref, me, n, device_of):
        self.mail, self.ref, self.me, self.n, self.device_of = mail, ref, me, n, device_of
        self.key = mail.slots(n - 1)

    def other(self, d):
        return lax.rem(self.me + d, self.n)

    def start(self):
        for d in range(1, self.n):
            mine = self.ref.at[self.me]
            self.mail.send(self.key + d - 1, mine, mine, self.device_of(self.other(d)))

    def wait(self):
        for d in range(1, self.n):
            source = self.other(self.n - d)
            self.mail.arrive(self.key + d - 1, self.ref.at[source], self.device_of(source))

    def total(self):
        self.wait()
        value = self.ref[0].astype(F32)
        for j in range(1, self.n):
            value = value + self.ref[j].astype(F32)
        return value


def two_part(a):
    top = a.astype(BF16).astype(F32)
    return jnp.concatenate([top, a - top], axis=0).astype(BF16)


def dot_two(a, b, transposed=False):
    dims = (((1,), (1,)), ((), ())) if transposed else (((1,), (0,)), ((), ()))
    both = lax.dot_general(two_part(a), b, dims, preferred_element_type=F32)
    half = a.shape[0]
    return both[:half] + both[half:]


def add_into(acc, others):
    value = acc[...].astype(F32)
    for other in others:
        value = value + other[...].astype(F32)
    acc[...] = value.astype(BF16)


def ring_sum(mail, key, pos, nxt, prv, get, half, hbuf, fbuf):
    at = lambda d: lax.rem(pos + d, 4)
    mail.send(key, half(get(at(2)), 0), hbuf.at[0], nxt)
    mail.send(key + 1, half(get(at(2)), 1), hbuf.at[1], prv)
    yield
    mail.arrive(key, hbuf.at[0], prv)
    add_into(half(get(at(1)), 0), [hbuf.at[0]])
    mail.send(key + 2, get(at(1)), fbuf.at[0], nxt)
    mail.arrive(key + 1, hbuf.at[1], nxt)
    add_into(half(get(at(3)), 1), [hbuf.at[1]])
    mail.send(key + 3, get(at(3)), fbuf.at[1], prv)
    yield
    mail.arrive(key + 2, fbuf.at[0], prv)
    mail.arrive(key + 3, fbuf.at[1], nxt)


K_GELU = 0.7071067811865476
K_SLOPE = 0.3989422804014327
BLOCK16 = 16


def gelu_rows(pre_t, h_s, slope_s, t, row, lanes):
    v = pre_t[pl.ds(t, BLOCK16)]
    half = 0.5 * (1.0 + lax.erf(v * K_GELU))
    h_s[pl.ds(row, BLOCK16), lanes] = (v * half).astype(BF16)
    slope_s[pl.ds(row, BLOCK16), lanes] = (half + v * jnp.exp(-0.5 * v * v) * K_SLOPE).astype(BF16)


def kernel(
    x_ref, live, tile_patient, gain, up_hbm, dn_hbm, wt, ws, sw_ref, keys_hbm, qlab, plab, scale,
    up_out, dn_out, gate_out, misc_out,
    n_all, n_t, x_t, x_mate, up_b, dn_b, dn_t, wq, w_x, w_c, thru, thru_t, h_s, h_t, slope_s, part, uv_all, keys, keys_t,
    pg_s, pre_s, held_t, held_o, held_sum, held, pre2, gx, pre_t,
    stage, recv, pbuf, zbuf, xbuf, sbuf, score_all, alpha_all, pull_s,
    up0, up_acc, dn_acc, g_acc, u_yh, u_yf, u_xh, u_xf, d_xh, d_xf, d_yh, d_yf,
    g_stage, g_recv, g_t, g_y, g_x, g_c, m_z, m_y, m_x, m_c,
    send_sem, recv_sem, local_sem,
):
    p = Place()
    mail = Mail(send_sem, recv_sem)
    mate, beside = p.at(c=1 - p.c), p.at(x=3 - p.x)
    above, below = p.at(y=p.dy(1)), p.at(y=p.dy(-1))
    z_dev = lambda z: p.at(z=z)
    y_dev = lambda y: p.at(y=y)
    x_dev = lambda x: p.at(x=x)
    c_dev = lambda c: p.at(c=c)
    q_dev = lambda q: (p.pat, p.z * 2 + q)
    partners = (
        [z_dev(p.dz(d)) for d in range(1, NZ)]
        + [y_dev(p.dy(d)) for d in (1, 2, 3)]
        + [x_dev(p.dx(d)) for d in (1, 2, 3)]
        + [mate]
    )
    barrier = pltpu.get_barrier_semaphore()
    for device in partners:
        pl.semaphore_signal(barrier, inc=1, device_id=device, device_id_type=MESH)

    fetch_up = pltpu.make_async_copy(up_hbm, up_b.at[p.q], local_sem.at[0])
    fetch_dn = pltpu.make_async_copy(dn_hbm, dn_b.at[p.q], local_sem.at[1])
    fetch_keys = pltpu.make_async_copy(keys_hbm, keys, local_sem.at[2])
    fetch_up.start()
    fetch_dn.start()
    fetch_keys.start()

    def norm_rows(half):
        v = x_ref[pl.ds(half * 64, 64)].astype(F32)
        center = v - jnp.mean(v, axis=1, keepdims=True)
        spread = jnp.mean(center * center, axis=1, keepdims=True)
        n_all[rows_at(p.z, ROWS, half * 64, 64)] = (center * lax.rsqrt(spread + 1e-06) * gain[...][None, :]).astype(BF16)

    g_rows = pl.ds(pl.multiple_of(p.c * 48, 16), 48)
    g_lanes = lanes_at(lax.rem(p.y, 2), 128)
    wq[p.c, p.y, p.q, p.z] = jnp.where(p.y < 2, wt[g_rows, g_lanes], ws[g_rows, g_lanes])

    norm_rows(0)
    pl.semaphore_wait(barrier, len(partners))

    tokens = ZGather(mail, p, n_all, ROWS)
    k_wz, k_w = mail.slots(7), mail.slots(1)
    w_z = lambda z: wq.at[p.c, p.y, p.q, z]
    for d in range(1, NZ):
        mail.send(k_wz + d - 1, w_z(p.z), w_z(p.z), z_dev(p.dz(d)))
    tokens.step(0, (0, 1))
    norm_rows(1)
    k_x0 = mail.slots(1)
    mail.send(k_x0, x_ref, x_mate, mate)

    up_piece = lambda q, y, c: up_b.at[q, rows_at(y * 2 + c, 192)]
    dn_piece = lambda q, y, c: dn_b.at[q, rows_at(y * 2 + c, 48)]
    theirs, other = 1 - p.q, 1 - p.c
    k_px, k_py, k_pm = mail.slots(2), mail.slots(6), mail.slots(8)
    fetch_up.wait()
    mail.send(k_px, up_piece(p.q, p.y, p.c), up_piece(p.q, p.y, p.c), beside)
    fetch_dn.wait()
    mail.send(k_px + 1, dn_piece(p.q, p.y, p.c), dn_piece(p.q, p.y, p.c), beside)

    def to_mate(d, piece, which):
        mail.send(k_pm + which * 4 + d, piece(theirs, p.dy(d), p.c), piece(theirs, p.dy(d), p.c), mate)

    def pieces_x():
        for which, piece in enumerate((up_piece, dn_piece)):
            block = piece(theirs, p.y, p.c)
            mail.arrive(k_px + which, block, beside)
            mail.send(k_py + which * 2, block, block, above)
            mail.send(k_py + which * 2 + 1, block, block, below)
            to_mate(0, piece, which)

    def pieces_y():
        for which, piece in enumerate((up_piece, dn_piece)):
            under, over = piece(theirs, p.dy(-1), p.c), piece(theirs, p.dy(1), p.c)
            mail.arrive(k_py + which * 2, under, below)
            if which == 0:
                mail.send(k_py + 4, under, under, above)
            to_mate(3, piece, which)
            mail.arrive(k_py + which * 2 + 1, over, above)
            if which == 1:
                mail.send(k_py + 5, over, over, below)
            to_mate(1, piece, which)

    def pieces_far():
        mail.arrive(k_py + 4, up_piece(theirs, p.dy(2), p.c), below)
        to_mate(2, up_piece, 0)
        mail.arrive(k_py + 5, dn_piece(theirs, p.dy(2), p.c), above)
        to_mate(2, dn_piece, 1)

    def pieces_mate(which):
        piece = (up_piece, dn_piece)[which]
        for d in range(4):
            mail.arrive(k_pm + which * 4 + d, piece(theirs, p.dy(d), other), mate)

    def hidden(owners, q):
        lhs = jnp.concatenate([n_all[rows_at(o, ROWS)] for o in owners], axis=0)
        count = len(owners) * ROWS
        pre_t[pl.ds(0, count)] = dot(lhs, up_b[q])
        lanes = lanes_at(q, HID)
        for j, o in enumerate(owners):
            def body(i, carry, j=j, o=o):
                t = pl.multiple_of(j * ROWS + i * BLOCK16, BLOCK16)
                row = pl.multiple_of(o * ROWS + i * BLOCK16, BLOCK16)
                gelu_rows(pre_t, h_s, slope_s, t, row, lanes)
                return carry

            lax.fori_loop(0, ROWS // BLOCK16, body, 0)

    def turn(owners):
        for o in owners:
            n_t[:, lanes_at(o, ROWS)] = n_all[rows_at(o, ROWS)].T

    def key_rows(i):
        at = pl.ds(i * 256, 256)
        v = keys[at].astype(F32)
        keys[at] = (v * lax.rsqrt(jnp.sum(v * v, axis=1, keepdims=True) + 1e-06)).astype(BF16)

    k_wy, k_wm = mail.slots(4), mail.slots(1)
    w_y = lambda y: wq.at[p.c, y]
    w_yh = lambda y, half: wq.at[p.c, y, half]
    near = [p.dz(1), p.dz(-1)]
    mid = [p.dz(2), p.dz(-2)]
    far = [p.dz(3), p.dz(-3)]

    hidden([p.z], p.q)
    turn([p.z])
    x_t[:, pl.ds(0, ROWS)] = x_ref[...].T
    for d in range(1, NZ):
        mail.arrive(k_wz + d - 1, w_z(p.dz(-d)), z_dev(p.dz(-d)))
    mail.send(k_w, wq.at[p.c, p.y, p.q], wq.at[p.c, p.y, p.q], beside)
    tokens.step(0, (2, 3))
    fetch_keys.wait()
    key_rows(0)
    pieces_x()
    mail.arrive(k_w, wq.at[p.c, p.y, theirs], beside)
    mail.send(k_wy, w_y(p.y), w_y(p.y), above)
    mail.send(k_wy + 1, w_y(p.y), w_y(p.y), below)
    tokens.step(1, (0, 1))
    key_rows(1)
    tokens.step(1, (2, 3))
    hidden(near, p.q)
    turn(near)
    key_rows(2)
    pieces_y()
    tokens.step(2, (0, 1))
    key_rows(3)
    mail.arrive(k_wy, w_y(p.dy(-1)), below)
    mail.send(k_wy + 2, w_yh(p.dy(-1), 0), w_yh(p.dy(-1), 0), above)
    mail.arrive(k_wy + 1, w_y(p.dy(1)), above)
    mail.send(k_wy + 3, w_yh(p.dy(1), 1), w_yh(p.dy(1), 1), below)
    pieces_far()
    tokens.step(2, (2, 3))
    hidden(mid, p.q)
    turn(mid)
    mail.arrive(k_wy + 2, w_yh(p.dy(2), 0), below)
    mail.arrive(k_wy + 3, w_yh(p.dy(2), 1), above)
    mail.send(k_wm, wq.at[p.c], wq.at[p.c], mate)
    pieces_mate(0)
    hidden([p.z], theirs)
    hidden(near, theirs)
    tokens.step(3, (0, 1))
    hidden(mid, theirs)
    for j in range(2):
        keys_t[:, pl.ds(j * 512, 512)] = keys[pl.ds(j * 512, 512)].T
    tokens.step(3, (2, 3))
    hidden(far, p.q)
    hidden(far, theirs)
    turn(far)
    mail.arrive(k_wm, wq.at[other], mate)

    def place_w(t, carry):
        for y in range(4):
            for c in range(2):
                row = pl.multiple_of(t * 96 + c * 48, 16)
                w_x[pl.ds(row, 48), pl.ds(y * 128, 128)] = wq[c, y, lax.rem(t, 2), lax.div(t, 2)]
        return carry

    lax.fori_loop(0, 16, place_w, 0)
    w_full = lambda: w_x[:, pl.ds(0, 2 * GATE)]
    pieces_mate(1)
    for q in range(2):
        thru[pl.ds(q * HID, HID)] = dot(dn_b[q], w_full()).astype(BF16)

    def gate_part(o, carry):
        at = rows_at(o, ROWS)
        part[at] = dot(h_s[at], thru[...]).astype(BF16)
        return carry

    lax.fori_loop(0, NZ - 1, lambda d, carry: gate_part(lax.rem(p.z + 5 + d, NZ), carry), 0)
    tokens.step(4)
    last = p.dz(4)
    hidden([last], 0)
    hidden([last], 1)
    gate_part(last, 0)

    reduce = ZReduce(mail, p, part, ROWS, stage, recv)
    gather_uv = ZGather(mail, p, uv_all, ROWS)
    swap_p = Swap(mail, pbuf, p.z, NZ, z_dev)
    swap_z = [Swap(mail, zbuf.at[i], p.z, NZ, z_dev) for i in range(3)]
    swap_x = [Swap(mail, xbuf.at[i], p.q, 2, q_dev) for i in range(3)]
    swap_s = Swap(mail, sbuf, p.z, NZ, z_dev)

    row8 = lax.broadcasted_iota(jnp.int32, (8, 128), 0)
    first4 = row8 < 4
    row_patient = lax.rem(row8, 4)
    first4_wide = lax.broadcasted_iota(jnp.int32, (8, 768), 0) < 4
    lane = lax.broadcasted_iota(jnp.int32, (8, 128), 1)

    def pack(v):
        return jnp.where(first4_wide, v[:, :768], v[:, 768:])

    def unpack(v):
        rolled = pltpu.roll(v, 4, 0)
        return jnp.concatenate([jnp.where(first4_wide, v, rolled), jnp.where(first4_wide, rolled, v)], axis=1)

    reduce.step(0, (0, 1))
    turn([last])
    dn_t[:, pl.ds(0, HID)] = dn_b[0].T
    reduce.step(0, (2, 3))
    dn_t[:, pl.ds(HID, HID)] = dn_b[1].T
    gate_x = dot(x_ref[...], w_full())
    reduce.step(1, (0, 1))
    same = jnp.zeros((8, 1024), jnp.int32)
    row_wide = lax.rem(lax.broadcasted_iota(jnp.int32, (8, 1024), 0), 4)
    labels = jnp.broadcast_to(qlab[...], (8, 1024))
    for k in range(4):
        same = jnp.where((row_wide == k) & (labels == plab[k]), 1, same)
    same = same.astype(F32)
    label_sums = dot(same.astype(BF16), keys[...])
    positives = jnp.sum(same, axis=1, keepdims=True)
    reduce.step(1, (2, 3))
    for z in range(NZ):
        h_t[:, pl.ds(z * ROWS, ROWS)] = h_s[pl.ds(z * ROWS, ROWS)].T
    reduce.step(2, (0, 1))
    for i in range(8):
        w_c[pl.ds(i * 96, 96), pl.ds(0, 512)] = w_x[pl.ds(pl.multiple_of((i * 2 + p.c) * 96, 96), 96), pl.ds(0, 512)]
    reduce.step(2, (2, 3))
    mail.arrive(k_x0, x_mate, mate)
    x_t[:, pl.ds(ROWS, ROWS)] = x_mate[...].T
    reduce.step(3, (0, 1))
    gates = reduce.total() + gate_x
    tanh_val = jnp.tanh(gates[:, :GATE])
    sigmoid_val = jax.nn.sigmoid(gates[:, GATE:])
    product = tanh_val * sigmoid_val
    sw = sw_ref[...]
    score = lax.dot_general(
        jnp.broadcast_to(sw, (8, GATE)), product, (((1,), (1,)), ((), ())), precision=HIGH, preferred_element_type=F32
    )
    in_tile = lax.broadcasted_iota(jnp.int32, (8, 128), 1) < live[0]
    onehot = (jnp.broadcast_to(tile_patient[...], (8, 128)) == row_patient) & in_tile
    mass = jnp.where(onehot, jnp.exp(score), 0.0)
    pbuf[p.z] = mass
    swap_p.start()
    common = sw * sigmoid_val
    own_rows = rows_at(p.z, ROWS)
    uv_all[own_rows, pl.ds(0, GATE)] = (common * (1.0 - tanh_val * tanh_val)).astype(BF16)
    uv_all[own_rows, pl.ds(GATE, GATE)] = (common * tanh_val * (1.0 - sigmoid_val)).astype(BF16)
    gather_uv.step(0)

    def post(i, packed, small):
        zbuf[i, p.z, :, pl.ds(0, 768)] = packed
        zbuf[i, p.z, :, pl.ds(768, 128)] = small
        swap_z[i].start()

    def collect_z(i):
        xbuf[i, p.q] = swap_z[i].total()
        swap_x[i].start()

    post(1, pack(label_sums), jnp.broadcast_to(positives, (8, 128)))
    vec_x = dot_two(mass, x_ref[...])
    swap_p.wait()

    total = jnp.zeros((8, 1), F32)
    for z in range(NZ):
        total += jnp.sum(pbuf[z], axis=1, keepdims=True)
    mass_all = jnp.concatenate([pbuf[z] for z in range(NZ)], axis=1)
    mass_h = dot_two(mass_all, h_s[...])
    vec = dot_two(mass_h[:, :HID], dn_b[0]) + dot_two(mass_h[:, HID:], dn_b[1]) + vec_x

    post(0, pack(vec), jnp.broadcast_to(total, (8, 128)))
    collect_z(0)
    gather_uv.step(1)
    collect_z(1)
    thru_t[...] = thru[...].T
    summed = swap_x[0].total()
    total_mass = summed[:, 768:769]
    pooled = unpack(summed[:, :768]) / total_mass
    length = jnp.sqrt(jnp.sum(pooled * pooled, axis=1, keepdims=True) + 1e-06)
    unit = pooled / length

    logits = dot(unit.astype(BF16), keys_t[...]) / 0.07
    exps = jnp.exp(logits)
    exp_part = jnp.sum(exps, axis=1, keepdims=True)
    pos_part = jnp.sum(same * logits, axis=1, keepdims=True)
    post(2, pack(dot_two(exps, keys[...])), jnp.where(lane == 0, exp_part, pos_part))
    collect_z(2)
    gather_uv.step(2)
    labels_total = swap_x[1].total()
    pos_count = labels_total[:, 768:769]
    queue_total = swap_x[2].total()
    exp_total = queue_total[:, 768:769]
    pos_logits = queue_total[:, 769:770]
    unit_grad = (scale[0] * INV_TEMP) * (
        unpack(queue_total[:, :768]) / exp_total - unpack(labels_total[:, :768]) / pos_count
    )
    pooled_grad = (unit_grad - unit * jnp.sum(unit * unit_grad, axis=1, keepdims=True)) / length

    grad_h = dot_two(pooled_grad, dn_t[...])
    own_dots = dot_two(pooled_grad, x_t[:, pl.ds(0, ROWS)])
    dots = dot_two(grad_h, h_t[...])
    for z in range(NZ):
        block = dots[:, z * ROWS : (z + 1) * ROWS] + jnp.where(p.z == z, own_dots, 0.0)
        picked = jnp.where((pbuf[z] > 0.0) & first4, block, 0.0)
        sbuf[p.z, pl.ds(z, 1)] = jnp.sum(picked, axis=0, keepdims=True)
    swap_s.start()
    center = jnp.sum(pooled * pooled_grad, axis=1, keepdims=True)
    log_part = jnp.log(exp_total) - pos_logits / pos_count
    loss = jnp.sum(jnp.where(first4, jnp.broadcast_to(log_part, (8, 128)), 0.0), axis=0, keepdims=True)
    for z in range(NZ):
        block = jnp.where(first4, pbuf[z], 0.0)
        alpha_all[pl.ds(z, 1)] = jnp.sum(block / total_mass, axis=0, keepdims=True)
        score_all[pl.ds(z, 1)] = jnp.sum(jnp.where(block > 0.0, center, 0.0), axis=0, keepdims=True)
    gather_uv.step(3)
    pad = jnp.zeros((120, 768), F32)
    grad_h_pad = jnp.concatenate([jnp.where(first4_wide, grad_h, 0.0), pad], axis=0).astype(BF16)
    rest = jnp.zeros((120, 128), F32)

    def pulled(b, carry):
        mass_b = jnp.where(first4, pbuf[b], 0.0)
        weight = jnp.where(mass_b > 0.0, jnp.broadcast_to(alpha_all[pl.ds(b, 1)], (8, 128)), 0.0)
        at = rows_at(b, ROWS)
        turned = jnp.concatenate([weight, rest], axis=0).T.astype(BF16)
        pull_s[at] = (dot(turned, grad_h_pad) * slope_s[at].astype(F32)).astype(BF16)
        return carry + dot_two(weight, h_s[at])

    held4 = lax.fori_loop(0, NZ, pulled, jnp.zeros((8, 768), F32))
    k_g = mail.slots(1)
    gx[0, :, pl.ds(0, D)] = pooled_grad
    gx[0, :, pl.ds(D, 768)] = jnp.where(first4_wide, held4, 0.0)
    mail.send(k_g, gx.at[0], gx.at[1], mate)
    gather_uv.step(4)

    def scaled(b, carry):
        at = pl.ds(pl.multiple_of(b * 256, 256), 256)
        pg_s[at] = (dot(uv_all[at], thru_t[...]) * slope_s[at].astype(F32)).astype(BF16)
        return carry

    lax.fori_loop(0, 4, scaled, 0)
    mail.arrive(k_g, gx.at[1], mate)
    grad_pad = jnp.concatenate([gx[0, :, pl.ds(0, D)], gx[1, :, pl.ds(0, D)], jnp.zeros((112, D), F32)], axis=0)
    for j in range(D // 128):
        w_x[pl.ds(j * 128, 128), pl.ds(512, 128)] = grad_pad[:, j * 128 : (j + 1) * 128].T.astype(BF16)
    for i in range(8):
        w_c[pl.ds(i * 96, 96), pl.ds(512, 128)] = w_x[pl.ds(pl.multiple_of((i * 2 + p.c) * 96, 96), 96), pl.ds(512, 128)]
    held[pl.ds(512, 128)] = jnp.concatenate(
        [gx[0, :, pl.ds(D, 768)], gx[1, :, pl.ds(D, 768)], jnp.zeros((112, 768), F32)], axis=0
    ).astype(BF16)
    score_all[...] = alpha_all[...] * (swap_s.total() - score_all[...])

    def apply_scores(b, carry):
        at = rows_at(b, ROWS)
        grad = jnp.broadcast_to(score_all[pl.ds(b, 1)], (ROWS, ROWS)).T[:, 0:1]
        pre_s[at] = (grad * uv_all[at].astype(F32)).astype(BF16)
        pg_s[at] = (grad * pg_s[at].astype(F32) + pull_s[at].astype(F32)).astype(BF16)
        return carry

    lax.fori_loop(0, NZ, apply_scores, 0)
    score_part = lax.dot_general(
        jnp.broadcast_to(score_all[pl.ds(p.z, 1)], (8, ROWS)), product, (((1,), (0,)), ((), ())),
        precision=HIGH, preferred_element_type=F32,
    )
    misc = jnp.where(
        row8 == 0, score_part[:, :128], jnp.where(row8 == 1, score_part[:, 128:], jnp.where(row8 == 2, loss / 16.0, 0.0))
    )

    def misc_chain(value):
        stages = [
            (Swap(mail, m_z, p.z, NZ, z_dev), m_z, p.z),
            (Swap(mail, m_y, p.y, 4, y_dev), m_y, p.y),
            (Swap(mail, m_x, p.x, 4, x_dev), m_x, p.x),
            (Swap(mail, m_c, p.c, 2, c_dev), m_c, p.c),
        ]
        for swap, buf, me in stages:
            buf[me] = value
            swap.start()
            yield
            value = swap.total()
        misc_out[...] = value
        yield

    misc_steps = misc_chain(misc)
    next(misc_steps)

    k_h, k_p = mail.slots(1), mail.slots(1)
    for j in range(3):
        held_t[pl.ds(j * 256, 256)] = dot(h_t[pl.ds(j * 256, 256)], pre_s[...]).astype(BF16)
    mail.send(k_h, held_t, held_o, mate)
    theirs_pre = pre_s.at[own_rows, lanes_at(other, GATE)]
    mail.send(k_p, theirs_pre, pre2.at[pl.ds(ROWS, ROWS)], mate)
    pre2[pl.ds(0, ROWS)] = pre_s[own_rows, lanes_at(p.c, GATE)]

    def sum_held():
        mail.arrive(k_h, held_o, mate)
        total_held = (held_t[...].astype(F32) + held_o[...].astype(F32)).astype(BF16)
        held_sum[...] = total_held
        held[pl.ds(0, 512)] = total_held.T

    def gate_grads():
        mail.arrive(k_p, pre2.at[pl.ds(ROWS, ROWS)], mate)

        def gate_rows(i, carry):
            at = pl.ds(pl.multiple_of(i * 512, 512), 512)
            g_acc[at] = (dot(dn_t[at], held_sum[:, lanes_at(p.c, GATE)]) + dot(x_t[at], pre2[...])).astype(BF16)
            return carry

        lax.fori_loop(0, 3, gate_rows, 0)

    def dn_rows(xl):
        value = dot(w_c[rows_at(xl, 384)], held[...]).astype(BF16)
        for y in range(4):
            dn_acc[xl, y] = value[y * 96 : (y + 1) * 96]

    up_p = lambda i, c: keys_t.at[pl.ds(pl.multiple_of((i * 2 + c) * 96, 96), 96), pl.ds(0, 768)]
    k_up0 = mail.slots(8)

    def compute(block, lhs, rhs, index, k, buf):
        def body(j, carry):
            i = index(j)
            value = dot(lhs[pl.ds(pl.multiple_of(i * 192, 192), 192)], rhs[...]).astype(BF16)
            block(i, 0)[...] = value[:96]
            block(i, 1)[...] = value[96:]
            return carry

        lax.fori_loop(0, 2, body, 0)
        for j in range(2):
            mail.send(k + j, block(index(j), other), buf.at[index(j)], mate)

    def collect(block, index, k, buf, acc):
        for j in range(2):
            mail.arrive(k + j, buf.at[index(j)], mate)

        def body(j, carry):
            i = index(j)
            acc[lax.div(i, 4), lax.rem(i, 4)] = (block(i, p.c)[...].astype(F32) + buf[i].astype(F32)).astype(BF16)
            return carry

        lax.fori_loop(0, 2, body, 0)

    up_index = [lambda j, d=d: j * 4 + p.dy(d) for d in (2, 1, -1, 0)]
    up_go = lambda g: compute(up_p, n_t, pg_s, up_index[g], k_up0 + 2 * g, up0)
    up_take = lambda g: collect(up_p, up_index[g], k_up0 + 2 * g, up0, up_acc)
    rows_half = lambda ref, i: ref.at[pl.ds(i * 48, 48)]
    k_up, k_dn = mail.slots(8), mail.slots(8)
    up_chunk = lambda d: up_acc.at[lax.rem(d, 2), p.y, :, lanes_at(lax.div(d, 2), HID)]
    dn_chunk_x = lambda d: dn_acc.at[lax.rem(d, 2), :, :, lanes_at(lax.div(d, 2), HID)]
    dn_chunk = lambda d: dn_acc.at[p.xl, d, :, lanes_at(p.q, HID)]
    up_y = ring_sum(
        mail, k_up, p.y, above, below, lambda d: up_acc.at[:, d], lambda ref, i: ref.at[i], u_yh, u_yf
    )
    up_x = ring_sum(mail, k_up + 4, p.x, x_dev(p.dx(1)), x_dev(p.dx(-1)), up_chunk, rows_half, u_xh, u_xf)
    dn_x = ring_sum(
        mail, k_dn, p.x, x_dev(p.dx(1)), x_dev(p.dx(-1)), dn_chunk_x, lambda ref, i: ref.at[pl.ds(i * 2, 2)], d_xh, d_xf
    )
    dn_y = ring_sum(mail, k_dn + 4, p.y, above, below, dn_chunk, rows_half, d_yh, d_yf)
    step = lambda chain: next(chain, None)
    zred = ZReduce(mail, p, g_acc, 192, g_stage, g_recv)
    in_y = Swap(mail, g_y, p.y, 4, y_dev)
    k_x = mail.slots(3)
    in_c = Swap(mail, g_c, p.c, 2, c_dev)

    up_go(0)
    sum_held()
    gate_grads()
    zred.step(0, (0, 1))
    up_go(1)
    zred.step(0, (2, 3))
    dn_rows(p.xl)
    dn_rows(1 - p.xl)
    step(dn_x)
    up_take(0)
    step(up_y)
    zred.step(1, (0, 1))
    up_go(2)
    zred.step(1, (2, 3))
    up_go(3)
    step(misc_steps)
    zred.step(2, (0, 1))
    up_take(1)
    up_take(2)
    zred.step(2, (2, 3))
    step(up_y)
    step(dn_x)
    zred.step(3)
    up_take(3)
    step(misc_steps)
    sums = zred.total().astype(BF16)
    g_t[0] = sums[:96]
    g_t[1] = sums[96:]
    for d in (1, 2, 3):
        there = p.dx(d)
        mail.send(k_x + d - 1, g_t.at[lax.div(there, 2)], g_x.at[d], x_dev(there))
    step(up_y)
    add_into(up_acc.at[:, p.y], [u_yf.at[0], u_yf.at[1]])
    step(up_x)
    for d in (1, 2, 3):
        mail.arrive(k_x + d - 1, g_x.at[d], x_dev(p.dx(-d)))
    value = g_t[p.q].astype(F32)
    for d in (1, 2, 3):
        value = value + g_x[d].astype(F32)
    g_y[p.y] = value.astype(BF16)
    in_y.start()
    step(dn_x)
    add_into(dn_chunk_x(p.x), [d_xf.at[0], d_xf.at[1]])
    step(dn_y)
    step(misc_steps)
    g_c[p.c] = in_y.total().astype(BF16)
    in_c.start()
    step(up_x)
    step(dn_y)
    step(misc_steps)
    step(up_x)
    up_out[...] = up_chunk(p.x)[...].astype(F32) + u_xf[0].astype(F32) + u_xf[1].astype(F32)
    in_c.wait()
    gate_out[...] = g_c[...].astype(F32)
    step(dn_y)
    dn_out[...] = dn_chunk(p.y)[...].astype(F32) + d_yf[0].astype(F32) + d_yf[1].astype(F32)
    mail.finish()


ANY = pl.BlockSpec(memory_space=pl.ANY)
VMEM = pl.BlockSpec(memory_space=pltpu.VMEM)
SMEM = pl.BlockSpec(memory_space=pltpu.SMEM)


def hand_out(up, dn, gate, total, loss, up_out, dn_out, tanh_out, sigmoid_out, score_out, loss_out):
    up_out[...] = up[...]
    dn_out[...] = dn[...]
    tanh_out[...] = gate[0]
    sigmoid_out[...] = gate[1]
    score_out[pl.ds(0, 128)] = total[0]
    score_out[pl.ds(128, 128)] = total[1]
    loss_out[0] = loss[2, 0]


def per_device(
    patch_class_features, live_tiles, tile_patient, ln_gain, up_weight, down_weight, tanh_weight,
    sigmoid_weight, score_weight, queue_keys, queue_labels, patient_labels, loss_scale,
):
    out = lambda *dims: jax.ShapeDtypeStruct(dims, F32)
    vm = lambda *dims: pltpu.VMEM(dims, BF16)
    vf = lambda *dims: pltpu.VMEM(dims, F32)
    up_grad, down_grad, gate_grad, total = pl.pallas_call(
        kernel,
        name="step",
        out_shape=(out(96, HID), out(96, HID), out(2, 96, GATE), out(8, 128)),
        in_specs=[VMEM, SMEM, VMEM, VMEM, ANY, ANY, VMEM, VMEM, VMEM, ANY, VMEM, SMEM, SMEM],
        out_specs=(VMEM,) * 4,
        scratch_shapes=[
            vm(TOK, D),
            vm(D, TOK),
            vm(D, 2 * ROWS),
            vm(ROWS, D),
            vm(2, D, HID),
            vm(2, HID, D),
            vm(D, 2 * HID),
            vm(2, 4, 2, NZ, 48, 128),
            vm(D, 640),
            vm(768, 640),
            vm(2 * HID, 2 * GATE),
            vm(2 * GATE, 2 * HID),
            vm(TOK, 2 * HID),
            vm(2 * HID, TOK),
            vm(TOK, 2 * HID),
            vm(TOK, 2 * GATE),
            vm(TOK, 2 * GATE),
            vm(1024, D),
            vm(D, 1024),
            vm(TOK, 2 * HID),
            vm(TOK, 2 * GATE),
            vm(2 * HID, 2 * GATE),
            vm(2 * HID, 2 * GATE),
            vm(2 * HID, 2 * GATE),
            vm(640, 2 * HID),
            vm(2 * ROWS, GATE),
            vf(2, 8, D + 768),
            vf(256, HID),
            vm(4, 3, ROWS // 2, 2 * GATE),
            vm(4, 4, ROWS // 2, 2 * GATE),
            vf(NZ, 8, 128),
            vf(3, NZ, 8, 896),
            vf(3, 2, 8, 896),
            vf(NZ, 8, 128),
            vf(NZ, 128),
            vf(NZ, 128),
            vm(TOK, 2 * HID),
            vm(8, 96, 2 * HID),
            vm(2, 4, 96, 2 * HID),
            vm(2, 4, 96, 2 * HID),
            vm(D, GATE),
            vm(2, 96, 2 * HID),
            vm(2, 2, 96, 2 * HID),
            vm(2, 48, HID),
            vm(2, 96, HID),
            vm(2, 2, 96, HID),
            vm(2, 4, 96, HID),
            vm(2, 48, HID),
            vm(2, 96, HID),
            vm(4, 3, 96, GATE),
            vm(4, 4, 96, GATE),
            vm(2, 96, GATE),
            vm(4, 96, GATE),
            vm(4, 96, GATE),
            vm(2, 96, GATE),
            vf(NZ, 8, 128),
            vf(4, 8, 128),
            vf(4, 8, 128),
            vf(2, 8, 128),
            pltpu.SemaphoreType.DMA((192,)),
            pltpu.SemaphoreType.DMA((192,)),
            pltpu.SemaphoreType.DMA((4,)),
        ],
        compiler_params=pltpu.CompilerParams(collective_id=1, has_side_effects=True, vmem_limit_bytes=VMEM_LIMIT),
    )(
        patch_class_features, live_tiles, tile_patient[None, :], ln_gain, up_weight, down_weight,
        tanh_weight, sigmoid_weight, score_weight[None, :], queue_keys, queue_labels[None, :], patient_labels,
        loss_scale.reshape(1),
    )
    outputs = pl.pallas_call(
        hand_out,
        name="hand_out",
        out_shape=(out(96, HID), out(96, HID), out(96, GATE), out(96, GATE), out(GATE), out(1)),
        in_specs=[VMEM] * 4 + [SMEM],
        out_specs=(VMEM,) * 5 + (SMEM,),
    )(up_grad, down_grad, gate_grad, total, total)
    return (outputs[0], outputs[1].T, *outputs[2:5], outputs[5].reshape(()))


def solution(mesh):
    placed = (
        P(("pat", "tile"), None),
        P(("pat", "tile")),
        P(("pat", "tile")),
        P(),
        P(None, "tile"),
        P("tile", None),
        P("tile", None),
        P("tile", None),
        P(),
        P("tile", None),
        P("tile"),
        P("pat"),
        P(),
    )
    return jax.shard_map(
        per_device,
        mesh=mesh,
        in_specs=placed,
        out_specs=(P("pat", "tile"), P("tile", "pat"), P("tile", None), P("tile", None), P(), P()),
        check_vma=False,
    )
```

```python
import jax
import jax.numpy as jnp
from jax import lax
from jax.experimental import pallas as pl
from jax.experimental.pallas import tpu as pltpu
from jax.sharding import PartitionSpec as P

MESH = pl.DeviceIdType.MESH
F32 = jnp.float32
BF16 = jnp.bfloat16
HIGH = lax.Precision.HIGHEST
INV_TEMP = 1.0 / 0.07
NZ = 8
NY = 4
NX = 4
ROWS = 128
TOK = NZ * ROWS
D = 1536
HID = 384
GATE = 256
VMEM_LIMIT = 63 << 20


class Place:
    def __init__(self):
        self.pat = lax.axis_index("pat")
        self.tile = lax.axis_index("tile")
        self.z = lax.div(self.tile, 2)
        self.q = lax.rem(self.tile, 2)
        self.xl = lax.div(self.pat, 8)
        self.y = lax.rem(lax.div(self.pat, 2), 4)
        self.c = lax.rem(self.pat, 2)
        self.x = self.q * 2 + self.xl

    def at(self, z=None, y=None, x=None, c=None):
        z = self.z if z is None else z
        y = self.y if y is None else y
        c = self.c if c is None else c
        if x is None:
            xl, q = self.xl, self.q
        else:
            xl, q = lax.rem(x, 2), lax.div(x, 2)
        return (xl * 8 + y * 2 + c, z * 2 + q)

    def dz(self, d):
        return lax.rem(self.z + (d + NZ), NZ)

    def dy(self, d):
        return lax.rem(self.y + (d + NY), NY)

    def dx(self, d):
        return lax.rem(self.x + (d + NX), NX)


def dot(a, b, dims=((1,), (0,))):
    return lax.dot_general(a, b, (dims, ((), ())), preferred_element_type=F32)


class Mail:
    def __init__(self, send_sem, recv_sem):
        self.send_sem, self.recv_sem = send_sem, recv_sem
        self.next = 0
        self.sent = []

    def slots(self, n):
        first = self.next
        self.next += n
        return first

    def send(self, k, src, dst, device):
        copy = pltpu.make_async_remote_copy(
            src_ref=src, dst_ref=dst, send_sem=self.send_sem.at[k], recv_sem=self.recv_sem.at[k],
            device_id=device, device_id_type=MESH,
        )
        copy.start()
        self.sent.append(copy)

    def arrive(self, k, dst, device):
        pltpu.make_async_remote_copy(
            src_ref=dst, dst_ref=dst, send_sem=self.send_sem.at[k], recv_sem=self.recv_sem.at[k],
            device_id=device, device_id_type=MESH,
        ).wait_recv()

    def finish(self):
        for copy in self.sent:
            copy.wait_send()


def rows_at(index, size, offset=0, count=None):
    count = size if count is None else count
    return pl.ds(pl.multiple_of(index * size + offset, 16), count)


def lanes_at(index, size):
    return pl.ds(pl.multiple_of(index * size, 128), size)


class ZGather:
    def __init__(self, mail, place, ref, size):
        self.mail, self.place, self.ref, self.size = mail, place, ref, size
        self.half = size // 2
        self.key = mail.slots(16)
        self.chains = ((1, 0, 4), (-1, 0, 3), (1, 1, 3), (-1, 1, 4))

    def piece(self, owner, half):
        return self.ref.at[rows_at(owner, self.size, half * self.half, self.half)]

    def step(self, s, which=(0, 1, 2, 3)):
        p = self.place
        for i in which:
            way, half, steps = self.chains[i]
            block = self.piece(p.dz(-way * s), half)
            if 0 < s <= steps:
                self.mail.arrive(self.key + i * 4 + s - 1, block, p.at(z=p.dz(-way)))
            if s < steps:
                self.mail.send(self.key + i * 4 + s, block, block, p.at(z=p.dz(way)))


class ZReduce:
    def __init__(self, mail, place, ref, size, stage, recv):
        self.mail, self.place, self.ref, self.size = mail, place, ref, size
        self.stage, self.recv = stage, recv
        self.half = size // 2
        self.key = mail.slots(16)
        self.chains = ((1, 0, 4), (-1, 1, 4), (1, 1, 3), (-1, 0, 3))

    def piece(self, owner, half):
        return rows_at(owner, self.size, half * self.half, self.half)

    def step(self, s, which=(0, 1, 2, 3)):
        p = self.place
        for i in which:
            way, half, steps = self.chains[i]
            if s < steps:
                dest = self.piece(p.dz(way * (steps - s)), half)
                if s == 0:
                    src = self.ref.at[dest]
                else:
                    self.mail.arrive(self.key + i * 4 + s - 1, self.recv.at[i, s - 1], p.at(z=p.dz(-way)))
                    src = self.stage.at[i, s - 1]
                    src[...] = (self.ref[dest].astype(F32) + self.recv[i, s - 1].astype(F32)).astype(BF16)
                self.mail.send(self.key + i * 4 + s, src, self.recv.at[i, s], p.at(z=p.dz(way)))

    def total(self):
        p = self.place
        for i, (way, half, steps) in enumerate(self.chains):
            self.mail.arrive(self.key + i * 4 + steps - 1, self.recv.at[i, steps - 1], p.at(z=p.dz(-way)))
        first = self.ref[self.piece(p.z, 0)].astype(F32) + self.recv[0, 3].astype(F32) + self.recv[3, 2].astype(F32)
        second = self.ref[self.piece(p.z, 1)].astype(F32) + self.recv[1, 3].astype(F32) + self.recv[2, 2].astype(F32)
        return jnp.concatenate([first, second], axis=0)


class Swap:
    def __init__(self, mail, ref, me, n, device_of):
        self.mail, self.ref, self.me, self.n, self.device_of = mail, ref, me, n, device_of
        self.key = mail.slots(n - 1)

    def other(self, d):
        return lax.rem(self.me + d, self.n)

    def start(self):
        for d in range(1, self.n):
            mine = self.ref.at[self.me]
            self.mail.send(self.key + d - 1, mine, mine, self.device_of(self.other(d)))

    def wait(self):
        for d in range(1, self.n):
            source = self.other(self.n - d)
            self.mail.arrive(self.key + d - 1, self.ref.at[source], self.device_of(source))

    def total(self):
        self.wait()
        value = self.ref[0].astype(F32)
        for j in range(1, self.n):
            value = value + self.ref[j].astype(F32)
        return value


def two_part(a):
    top = a.astype(BF16).astype(F32)
    return jnp.concatenate([top, a - top], axis=0).astype(BF16)


def dot_two(a, b, transposed=False):
    dims = (((1,), (1,)), ((), ())) if transposed else (((1,), (0,)), ((), ()))
    both = lax.dot_general(two_part(a), b, dims, preferred_element_type=F32)
    half = a.shape[0]
    return both[:half] + both[half:]


def add_into(acc, others):
    value = acc[...].astype(F32)
    for other in others:
        value = value + other[...].astype(F32)
    acc[...] = value.astype(BF16)


def ring_sum(mail, key, pos, nxt, prv, get, half, hbuf, fbuf):
    at = lambda d: lax.rem(pos + d, 4)
    mail.send(key, half(get(at(2)), 0), hbuf.at[0], nxt)
    mail.send(key + 1, half(get(at(2)), 1), hbuf.at[1], prv)
    yield
    mail.arrive(key, hbuf.at[0], prv)
    add_into(half(get(at(1)), 0), [hbuf.at[0]])
    mail.send(key + 2, get(at(1)), fbuf.at[0], nxt)
    mail.arrive(key + 1, hbuf.at[1], nxt)
    add_into(half(get(at(3)), 1), [hbuf.at[1]])
    mail.send(key + 3, get(at(3)), fbuf.at[1], prv)
    yield
    mail.arrive(key + 2, fbuf.at[0], prv)
    mail.arrive(key + 3, fbuf.at[1], nxt)


K_GELU = 0.7071067811865476
K_SLOPE = 0.3989422804014327
BLOCK16 = 16


def gelu_rows(pre_t, h_s, slope_s, t, row, lanes):
    v = pre_t[pl.ds(t, BLOCK16)]
    half = 0.5 * (1.0 + lax.erf(v * K_GELU))
    h_s[pl.ds(row, BLOCK16), lanes] = (v * half).astype(BF16)
    slope_s[pl.ds(row, BLOCK16), lanes] = (half + v * jnp.exp(-0.5 * v * v) * K_SLOPE).astype(BF16)


def kernel(
    x_ref, live, tile_patient, gain, up_hbm, dn_hbm, wt, ws, sw_ref, keys_hbm, qlab, plab, scale,
    up_out, dn_out, gate_out, misc_out,
    n_all, n_t, x_t, x_mate, up_b, dn_b, dn_t, wq, w_x, w_c, thru, thru_t, h_s, h_t, slope_s, part, uv_all, keys, keys_t,
    pg_s, pre_s, held_t, held_o, held_sum, held, pre2, gx, pre_t,
    stage, recv, pbuf, zbuf, xbuf, sbuf, score_all, alpha_all, pull_s,
    up0, up_acc, dn_acc, g_acc, u_yh, u_yf, u_xh, u_xf, d_xh, d_xf, d_yh, d_yf,
    g_stage, g_recv, g_t, g_y, g_x, g_c, m_z, m_y, m_x, m_c,
    send_sem, recv_sem, local_sem,
):
    p = Place()
    mail = Mail(send_sem, recv_sem)
    mate, beside = p.at(c=1 - p.c), p.at(x=3 - p.x)
    above, below = p.at(y=p.dy(1)), p.at(y=p.dy(-1))
    z_dev = lambda z: p.at(z=z)
    y_dev = lambda y: p.at(y=y)
    x_dev = lambda x: p.at(x=x)
    c_dev = lambda c: p.at(c=c)
    q_dev = lambda q: (p.pat, p.z * 2 + q)
    partners = (
        [z_dev(p.dz(d)) for d in range(1, NZ)]
        + [y_dev(p.dy(d)) for d in (1, 2, 3)]
        + [x_dev(p.dx(d)) for d in (1, 2, 3)]
        + [mate]
    )
    barrier = pltpu.get_barrier_semaphore()
    for device in partners:
        pl.semaphore_signal(barrier, inc=1, device_id=device, device_id_type=MESH)

    fetch_up = pltpu.make_async_copy(up_hbm, up_b.at[p.q], local_sem.at[0])
    fetch_dn = pltpu.make_async_copy(dn_hbm, dn_b.at[p.q], local_sem.at[1])
    fetch_keys = pltpu.make_async_copy(keys_hbm, keys, local_sem.at[2])
    fetch_up.start()
    fetch_dn.start()
    fetch_keys.start()

    def norm_rows(half):
        v = x_ref[pl.ds(half * 64, 64)].astype(F32)
        center = v - jnp.mean(v, axis=1, keepdims=True)
        spread = jnp.mean(center * center, axis=1, keepdims=True)
        n_all[rows_at(p.z, ROWS, half * 64, 64)] = (center * lax.rsqrt(spread + 1e-06) * gain[...][None, :]).astype(BF16)

    g_rows = pl.ds(pl.multiple_of(p.c * 48, 16), 48)
    g_lanes = lanes_at(lax.rem(p.y, 2), 128)
    wq[p.c, p.y, p.q, p.z] = jnp.where(p.y < 2, wt[g_rows, g_lanes], ws[g_rows, g_lanes])

    norm_rows(0)
    pl.semaphore_wait(barrier, len(partners))

    tokens = ZGather(mail, p, n_all, ROWS)
    k_wz, k_w = mail.slots(7), mail.slots(1)
    w_z = lambda z: wq.at[p.c, p.y, p.q, z]
    for d in range(1, NZ):
        mail.send(k_wz + d - 1, w_z(p.z), w_z(p.z), z_dev(p.dz(d)))
    tokens.step(0, (0, 1))
    norm_rows(1)
    k_x0 = mail.slots(1)
    mail.send(k_x0, x_ref, x_mate, mate)

    up_piece = lambda q, y, c: up_b.at[q, rows_at(y * 2 + c, 192)]
    dn_piece = lambda q, y, c: dn_b.at[q, rows_at(y * 2 + c, 48)]
    theirs, other = 1 - p.q, 1 - p.c
    k_px, k_py, k_pm = mail.slots(2), mail.slots(6), mail.slots(8)
    fetch_up.wait()
    mail.send(k_px, up_piece(p.q, p.y, p.c), up_piece(p.q, p.y, p.c), beside)
    fetch_dn.wait()
    mail.send(k_px + 1, dn_piece(p.q, p.y, p.c), dn_piece(p.q, p.y, p.c), beside)

    def to_mate(d, piece, which):
        mail.send(k_pm + which * 4 + d, piece(theirs, p.dy(d), p.c), piece(theirs, p.dy(d), p.c), mate)

    def pieces_x():
        for which, piece in enumerate((up_piece, dn_piece)):
            block = piece(theirs, p.y, p.c)
            mail.arrive(k_px + which, block, beside)
            mail.send(k_py + which * 2, block, block, above)
            mail.send(k_py + which * 2 + 1, block, block, below)
            to_mate(0, piece, which)

        for which, piece in enumerate((up_piece, dn_piece)):
            block = piece(p.q, p.dy(2), p.c)
            mail.send(k_py + 4 + which, block, block, beside)

    def pieces_y():
        for which, piece in enumerate((up_piece, dn_piece)):
            mail.arrive(k_py + which * 2, piece(theirs, p.dy(-1), p.c), below)
            to_mate(3, piece, which)
            mail.arrive(k_py + which * 2 + 1, piece(theirs, p.dy(1), p.c), above)
            to_mate(1, piece, which)

    def pieces_far():
        for which, piece in enumerate((up_piece, dn_piece)):
            mail.arrive(k_py + 4 + which, piece(theirs, p.dy(2), p.c), beside)
            to_mate(2, piece, which)

    def pieces_mate(which):
        piece = (up_piece, dn_piece)[which]
        for d in range(4):
            mail.arrive(k_pm + which * 4 + d, piece(theirs, p.dy(d), other), mate)

    def hidden(owners, q):
        lhs = jnp.concatenate([n_all[rows_at(o, ROWS)] for o in owners], axis=0)
        count = len(owners) * ROWS
        pre_t[pl.ds(0, count)] = dot(lhs, up_b[q])
        lanes = lanes_at(q, HID)
        for j, o in enumerate(owners):
            def body(i, carry, j=j, o=o):
                t = pl.multiple_of(j * ROWS + i * BLOCK16, BLOCK16)
                row = pl.multiple_of(o * ROWS + i * BLOCK16, BLOCK16)
                gelu_rows(pre_t, h_s, slope_s, t, row, lanes)
                return carry

            lax.fori_loop(0, ROWS // BLOCK16, body, 0)

    def turn(owners):
        for o in owners:
            n_t[:, lanes_at(o, ROWS)] = n_all[rows_at(o, ROWS)].T

    def key_rows(i):
        at = pl.ds(i * 256, 256)
        v = keys[at].astype(F32)
        keys[at] = (v * lax.rsqrt(jnp.sum(v * v, axis=1, keepdims=True) + 1e-06)).astype(BF16)

    k_wy, k_wm = mail.slots(4), mail.slots(1)
    w_y = lambda y: wq.at[p.c, y]
    w_yh = lambda y, half: wq.at[p.c, y, half]
    near = [p.dz(1), p.dz(-1)]
    mid = [p.dz(2), p.dz(-2)]
    far = [p.dz(3), p.dz(-3)]

    hidden([p.z], p.q)
    turn([p.z])
    x_t[:, pl.ds(0, ROWS)] = x_ref[...].T
    for d in range(1, NZ):
        mail.arrive(k_wz + d - 1, w_z(p.dz(-d)), z_dev(p.dz(-d)))
    mail.send(k_w, wq.at[p.c, p.y, p.q], wq.at[p.c, p.y, p.q], beside)
    tokens.step(0, (2, 3))
    fetch_keys.wait()
    key_rows(0)
    tokens.step(1, (0, 1))
    mail.arrive(k_w, wq.at[p.c, p.y, theirs], beside)
    mail.send(k_wy, w_y(p.y), w_y(p.y), above)
    mail.send(k_wy + 1, w_y(p.y), w_y(p.y), below)
    pieces_x()
    tokens.step(1, (2, 3))
    hidden(near, p.q)
    turn(near)
    key_rows(1)
    tokens.step(2, (0, 1))
    key_rows(2)
    key_rows(3)
    mail.arrive(k_wy, w_y(p.dy(-1)), below)
    mail.send(k_wy + 2, w_yh(p.dy(-1), 0), w_yh(p.dy(-1), 0), above)
    mail.arrive(k_wy + 1, w_y(p.dy(1)), above)
    mail.send(k_wy + 3, w_yh(p.dy(1), 1), w_yh(p.dy(1), 1), below)
    tokens.step(2, (2, 3))
    hidden(mid, p.q)
    turn(mid)
    pieces_y()
    mail.arrive(k_wy + 2, w_yh(p.dy(2), 0), below)
    mail.arrive(k_wy + 3, w_yh(p.dy(2), 1), above)
    mail.send(k_wm, wq.at[p.c], wq.at[p.c], mate)
    pieces_far()
    tokens.step(3, (0, 1))
    pieces_mate(0)
    hidden([p.z], theirs)
    hidden(near, theirs)
    hidden(mid, theirs)
    mail.arrive(k_wm, wq.at[other], mate)

    def place_w(t, carry):
        for y in range(4):
            for c in range(2):
                row = pl.multiple_of(t * 96 + c * 48, 16)
                w_x[pl.ds(row, 48), pl.ds(y * 128, 128)] = wq[c, y, lax.rem(t, 2), lax.div(t, 2)]
        return carry

    lax.fori_loop(0, 16, place_w, 0)
    w_full = lambda: w_x[:, pl.ds(0, 2 * GATE)]
    pieces_mate(1)
    for q in range(2):
        thru[pl.ds(q * HID, HID)] = dot(dn_b[q], w_full()).astype(BF16)

    def gate_part(o, carry):
        at = rows_at(o, ROWS)
        part[at] = dot(h_s[at], thru[...]).astype(BF16)
        return carry

    tokens.step(3, (2, 3))
    for j in range(2):
        keys_t[:, pl.ds(j * 512, 512)] = keys[pl.ds(j * 512, 512)].T
    hidden(far, p.q)
    hidden(far, theirs)
    turn(far)
    lax.fori_loop(0, NZ - 1, lambda d, carry: gate_part(lax.rem(p.z + 5 + d, NZ), carry), 0)
    tokens.step(4)
    last = p.dz(4)
    hidden([last], 0)
    hidden([last], 1)
    gate_part(last, 0)

    reduce = ZReduce(mail, p, part, ROWS, stage, recv)
    gather_uv = ZGather(mail, p, uv_all, ROWS)
    swap_p = Swap(mail, pbuf, p.z, NZ, z_dev)
    swap_z = [Swap(mail, zbuf.at[i], p.z, NZ, z_dev) for i in range(3)]
    swap_x = [Swap(mail, xbuf.at[i], p.q, 2, q_dev) for i in range(3)]
    swap_s = Swap(mail, sbuf, p.z, NZ, z_dev)

    row8 = lax.broadcasted_iota(jnp.int32, (8, 128), 0)
    first4 = row8 < 4
    row_patient = lax.rem(row8, 4)
    first4_wide = lax.broadcasted_iota(jnp.int32, (8, 768), 0) < 4
    lane = lax.broadcasted_iota(jnp.int32, (8, 128), 1)

    def pack(v):
        return jnp.where(first4_wide, v[:, :768], v[:, 768:])

    def unpack(v):
        rolled = pltpu.roll(v, 4, 0)
        return jnp.concatenate([jnp.where(first4_wide, v, rolled), jnp.where(first4_wide, rolled, v)], axis=1)

    reduce.step(0, (0, 1))
    turn([last])
    dn_t[:, pl.ds(0, HID)] = dn_b[0].T
    reduce.step(0, (2, 3))
    dn_t[:, pl.ds(HID, HID)] = dn_b[1].T
    gate_x = dot(x_ref[...], w_full())
    reduce.step(1, (0, 1))
    same = jnp.zeros((8, 1024), jnp.int32)
    row_wide = lax.rem(lax.broadcasted_iota(jnp.int32, (8, 1024), 0), 4)
    labels = jnp.broadcast_to(qlab[...], (8, 1024))
    for k in range(4):
        same = jnp.where((row_wide == k) & (labels == plab[k]), 1, same)
    same = same.astype(F32)
    label_sums = dot(same.astype(BF16), keys[...])
    positives = jnp.sum(same, axis=1, keepdims=True)
    reduce.step(1, (2, 3))
    for z in range(NZ):
        h_t[:, pl.ds(z * ROWS, ROWS)] = h_s[pl.ds(z * ROWS, ROWS)].T
    reduce.step(2, (0, 1))
    for i in range(8):
        w_c[pl.ds(i * 96, 96), pl.ds(0, 512)] = w_x[pl.ds(pl.multiple_of((i * 2 + p.c) * 96, 96), 96), pl.ds(0, 512)]
    reduce.step(2, (2, 3))
    mail.arrive(k_x0, x_mate, mate)
    x_t[:, pl.ds(ROWS, ROWS)] = x_mate[...].T
    reduce.step(3, (0, 1))
    gates = reduce.total() + gate_x
    tanh_val = jnp.tanh(gates[:, :GATE])
    sigmoid_val = jax.nn.sigmoid(gates[:, GATE:])
    product = tanh_val * sigmoid_val
    sw = sw_ref[...]
    score = lax.dot_general(
        jnp.broadcast_to(sw, (8, GATE)), product, (((1,), (1,)), ((), ())), precision=HIGH, preferred_element_type=F32
    )
    in_tile = lax.broadcasted_iota(jnp.int32, (8, 128), 1) < live[0]
    onehot = (jnp.broadcast_to(tile_patient[...], (8, 128)) == row_patient) & in_tile
    mass = jnp.where(onehot, jnp.exp(score), 0.0)
    pbuf[p.z] = mass
    swap_p.start()
    common = sw * sigmoid_val
    own_rows = rows_at(p.z, ROWS)
    uv_all[own_rows, pl.ds(0, GATE)] = (common * (1.0 - tanh_val * tanh_val)).astype(BF16)
    uv_all[own_rows, pl.ds(GATE, GATE)] = (common * tanh_val * (1.0 - sigmoid_val)).astype(BF16)
    gather_uv.step(0)

    def post(i, packed, small):
        zbuf[i, p.z, :, pl.ds(0, 768)] = packed
        zbuf[i, p.z, :, pl.ds(768, 128)] = small
        swap_z[i].start()

    def collect_z(i):
        xbuf[i, p.q] = swap_z[i].total()
        swap_x[i].start()

    post(1, pack(label_sums), jnp.broadcast_to(positives, (8, 128)))
    vec_x = dot_two(mass, x_ref[...])
    swap_p.wait()

    total = jnp.zeros((8, 1), F32)
    for z in range(NZ):
        total += jnp.sum(pbuf[z], axis=1, keepdims=True)
    mass_all = jnp.concatenate([pbuf[z] for z in range(NZ)], axis=1)
    mass_h = dot_two(mass_all, h_s[...])
    vec = dot_two(mass_h[:, :HID], dn_b[0]) + dot_two(mass_h[:, HID:], dn_b[1]) + vec_x

    post(0, pack(vec), jnp.broadcast_to(total, (8, 128)))
    collect_z(0)
    gather_uv.step(1)
    collect_z(1)
    thru_t[...] = thru[...].T
    summed = swap_x[0].total()
    total_mass = summed[:, 768:769]
    pooled = unpack(summed[:, :768]) / total_mass
    length = jnp.sqrt(jnp.sum(pooled * pooled, axis=1, keepdims=True) + 1e-06)
    unit = pooled / length

    logits = dot(unit.astype(BF16), keys_t[...]) / 0.07
    exps = jnp.exp(logits)
    exp_part = jnp.sum(exps, axis=1, keepdims=True)
    pos_part = jnp.sum(same * logits, axis=1, keepdims=True)
    post(2, pack(dot_two(exps, keys[...])), jnp.where(lane == 0, exp_part, pos_part))
    collect_z(2)
    gather_uv.step(2)
    labels_total = swap_x[1].total()
    pos_count = labels_total[:, 768:769]
    queue_total = swap_x[2].total()
    exp_total = queue_total[:, 768:769]
    pos_logits = queue_total[:, 769:770]
    unit_grad = (scale[0] * INV_TEMP) * (
        unpack(queue_total[:, :768]) / exp_total - unpack(labels_total[:, :768]) / pos_count
    )
    pooled_grad = (unit_grad - unit * jnp.sum(unit * unit_grad, axis=1, keepdims=True)) / length

    grad_h = dot_two(pooled_grad, dn_t[...])
    own_dots = dot_two(pooled_grad, x_t[:, pl.ds(0, ROWS)])
    dots = dot_two(grad_h, h_t[...])
    for z in range(NZ):
        block = dots[:, z * ROWS : (z + 1) * ROWS] + jnp.where(p.z == z, own_dots, 0.0)
        picked = jnp.where((pbuf[z] > 0.0) & first4, block, 0.0)
        sbuf[p.z, pl.ds(z, 1)] = jnp.sum(picked, axis=0, keepdims=True)
    swap_s.start()
    center = jnp.sum(pooled * pooled_grad, axis=1, keepdims=True)
    log_part = jnp.log(exp_total) - pos_logits / pos_count
    loss = jnp.sum(jnp.where(first4, jnp.broadcast_to(log_part, (8, 128)), 0.0), axis=0, keepdims=True)
    for z in range(NZ):
        block = jnp.where(first4, pbuf[z], 0.0)
        alpha_all[pl.ds(z, 1)] = jnp.sum(block / total_mass, axis=0, keepdims=True)
        score_all[pl.ds(z, 1)] = jnp.sum(jnp.where(block > 0.0, center, 0.0), axis=0, keepdims=True)
    gather_uv.step(3)
    pad = jnp.zeros((120, 768), F32)
    grad_h_pad = jnp.concatenate([jnp.where(first4_wide, grad_h, 0.0), pad], axis=0).astype(BF16)
    rest = jnp.zeros((120, 128), F32)

    def pulled(b, carry):
        mass_b = jnp.where(first4, pbuf[b], 0.0)
        weight = jnp.where(mass_b > 0.0, jnp.broadcast_to(alpha_all[pl.ds(b, 1)], (8, 128)), 0.0)
        at = rows_at(b, ROWS)
        turned = jnp.concatenate([weight, rest], axis=0).T.astype(BF16)
        pull_s[at] = (dot(turned, grad_h_pad) * slope_s[at].astype(F32)).astype(BF16)
        return carry + dot_two(weight, h_s[at])

    held4 = lax.fori_loop(0, NZ, pulled, jnp.zeros((8, 768), F32))
    k_g = mail.slots(1)
    gx[0, :, pl.ds(0, D)] = pooled_grad
    gx[0, :, pl.ds(D, 768)] = jnp.where(first4_wide, held4, 0.0)
    mail.send(k_g, gx.at[0], gx.at[1], mate)
    gather_uv.step(4)

    def scaled(b, carry):
        at = pl.ds(pl.multiple_of(b * 256, 256), 256)
        pg_s[at] = (dot(uv_all[at], thru_t[...]) * slope_s[at].astype(F32)).astype(BF16)
        return carry

    lax.fori_loop(0, 4, scaled, 0)
    mail.arrive(k_g, gx.at[1], mate)
    grad_pad = jnp.concatenate([gx[0, :, pl.ds(0, D)], gx[1, :, pl.ds(0, D)], jnp.zeros((112, D), F32)], axis=0)
    for j in range(D // 128):
        w_x[pl.ds(j * 128, 128), pl.ds(512, 128)] = grad_pad[:, j * 128 : (j + 1) * 128].T.astype(BF16)
    for i in range(8):
        w_c[pl.ds(i * 96, 96), pl.ds(512, 128)] = w_x[pl.ds(pl.multiple_of((i * 2 + p.c) * 96, 96), 96), pl.ds(512, 128)]
    held[pl.ds(512, 128)] = jnp.concatenate(
        [gx[0, :, pl.ds(D, 768)], gx[1, :, pl.ds(D, 768)], jnp.zeros((112, 768), F32)], axis=0
    ).astype(BF16)
    score_all[...] = alpha_all[...] * (swap_s.total() - score_all[...])

    def apply_scores(b, carry):
        at = rows_at(b, ROWS)
        grad = jnp.broadcast_to(score_all[pl.ds(b, 1)], (ROWS, ROWS)).T[:, 0:1]
        pre_s[at] = (grad * uv_all[at].astype(F32)).astype(BF16)
        pg_s[at] = (grad * pg_s[at].astype(F32) + pull_s[at].astype(F32)).astype(BF16)
        return carry

    lax.fori_loop(0, NZ, apply_scores, 0)
    score_part = lax.dot_general(
        jnp.broadcast_to(score_all[pl.ds(p.z, 1)], (8, ROWS)), product, (((1,), (0,)), ((), ())),
        precision=HIGH, preferred_element_type=F32,
    )
    misc = jnp.where(
        row8 == 0, score_part[:, :128], jnp.where(row8 == 1, score_part[:, 128:], jnp.where(row8 == 2, loss / 16.0, 0.0))
    )

    def misc_chain(value):
        stages = [
            (Swap(mail, m_z, p.z, NZ, z_dev), m_z, p.z),
            (Swap(mail, m_y, p.y, 4, y_dev), m_y, p.y),
            (Swap(mail, m_x, p.x, 4, x_dev), m_x, p.x),
            (Swap(mail, m_c, p.c, 2, c_dev), m_c, p.c),
        ]
        for swap, buf, me in stages:
            buf[me] = value
            swap.start()
            yield
            value = swap.total()
        misc_out[...] = value
        yield

    misc_steps = misc_chain(misc)
    next(misc_steps)

    k_h, k_p = mail.slots(1), mail.slots(1)
    for j in range(3):
        held_t[pl.ds(j * 256, 256)] = dot(h_t[pl.ds(j * 256, 256)], pre_s[...]).astype(BF16)
    mail.send(k_h, held_t, held_o, mate)
    theirs_pre = pre_s.at[own_rows, lanes_at(other, GATE)]
    mail.send(k_p, theirs_pre, pre2.at[pl.ds(ROWS, ROWS)], mate)
    pre2[pl.ds(0, ROWS)] = pre_s[own_rows, lanes_at(p.c, GATE)]

    def sum_held():
        mail.arrive(k_h, held_o, mate)
        total_held = (held_t[...].astype(F32) + held_o[...].astype(F32)).astype(BF16)
        held_sum[...] = total_held
        held[pl.ds(0, 512)] = total_held.T

    def gate_grads():
        mail.arrive(k_p, pre2.at[pl.ds(ROWS, ROWS)], mate)

        def gate_rows(i, carry):
            at = pl.ds(pl.multiple_of(i * 512, 512), 512)
            g_acc[at] = (dot(dn_t[at], held_sum[:, lanes_at(p.c, GATE)]) + dot(x_t[at], pre2[...])).astype(BF16)
            return carry

        lax.fori_loop(0, 3, gate_rows, 0)

    def dn_rows(xl):
        value = dot(w_c[rows_at(xl, 384)], held[...]).astype(BF16)
        for y in range(4):
            dn_acc[xl, y] = value[y * 96 : (y + 1) * 96]

    up_p = lambda i, c: keys_t.at[pl.ds(pl.multiple_of((i * 2 + c) * 96, 96), 96), pl.ds(0, 768)]
    k_up0 = mail.slots(8)

    def compute(block, lhs, rhs, index, k, buf):
        def body(j, carry):
            i = index(j)
            value = dot(lhs[pl.ds(pl.multiple_of(i * 192, 192), 192)], rhs[...]).astype(BF16)
            block(i, 0)[...] = value[:96]
            block(i, 1)[...] = value[96:]
            return carry

        lax.fori_loop(0, 2, body, 0)
        for j in range(2):
            mail.send(k + j, block(index(j), other), buf.at[index(j)], mate)

    def collect(block, index, k, buf, acc):
        for j in range(2):
            mail.arrive(k + j, buf.at[index(j)], mate)

        def body(j, carry):
            i = index(j)
            acc[lax.div(i, 4), lax.rem(i, 4)] = (block(i, p.c)[...].astype(F32) + buf[i].astype(F32)).astype(BF16)
            return carry

        lax.fori_loop(0, 2, body, 0)

    up_index = [lambda j, d=d: j * 4 + p.dy(d) for d in (2, 1, -1, 0)]
    up_go = lambda g: compute(up_p, n_t, pg_s, up_index[g], k_up0 + 2 * g, up0)
    up_take = lambda g: collect(up_p, up_index[g], k_up0 + 2 * g, up0, up_acc)
    rows_half = lambda ref, i: ref.at[pl.ds(i * 48, 48)]
    k_up, k_dn = mail.slots(8), mail.slots(8)
    up_chunk = lambda d: up_acc.at[lax.rem(d, 2), p.y, :, lanes_at(lax.div(d, 2), HID)]
    dn_chunk_x = lambda d: dn_acc.at[lax.rem(d, 2), :, :, lanes_at(lax.div(d, 2), HID)]
    dn_chunk = lambda d: dn_acc.at[p.xl, d, :, lanes_at(p.q, HID)]
    up_y = ring_sum(
        mail, k_up, p.y, above, below, lambda d: up_acc.at[:, d], lambda ref, i: ref.at[i], u_yh, u_yf
    )
    up_x = ring_sum(mail, k_up + 4, p.x, x_dev(p.dx(1)), x_dev(p.dx(-1)), up_chunk, rows_half, u_xh, u_xf)
    dn_x = ring_sum(
        mail, k_dn, p.x, x_dev(p.dx(1)), x_dev(p.dx(-1)), dn_chunk_x, lambda ref, i: ref.at[pl.ds(i * 2, 2)], d_xh, d_xf
    )
    dn_y = ring_sum(mail, k_dn + 4, p.y, above, below, dn_chunk, rows_half, d_yh, d_yf)
    step = lambda chain: next(chain, None)
    zred = ZReduce(mail, p, g_acc, 192, g_stage, g_recv)
    in_y = Swap(mail, g_y, p.y, 4, y_dev)
    k_x = mail.slots(3)
    in_c = Swap(mail, g_c, p.c, 2, c_dev)

    up_go(0)
    sum_held()
    gate_grads()
    zred.step(0, (0, 1))
    up_go(1)
    zred.step(0, (2, 3))
    dn_rows(p.xl)
    dn_rows(1 - p.xl)
    step(dn_x)
    up_take(0)
    step(up_y)
    zred.step(1, (0, 1))
    up_go(2)
    zred.step(1, (2, 3))
    up_go(3)
    step(misc_steps)
    zred.step(2, (0, 1))
    up_take(1)
    up_take(2)
    zred.step(2, (2, 3))
    step(up_y)
    step(dn_x)
    zred.step(3)
    up_take(3)
    step(misc_steps)
    sums = zred.total().astype(BF16)
    g_t[0] = sums[:96]
    g_t[1] = sums[96:]
    for d in (1, 2, 3):
        there = p.dx(d)
        mail.send(k_x + d - 1, g_t.at[lax.div(there, 2)], g_x.at[d], x_dev(there))
    step(up_y)
    add_into(up_acc.at[:, p.y], [u_yf.at[0], u_yf.at[1]])
    step(up_x)
    for d in (1, 2, 3):
        mail.arrive(k_x + d - 1, g_x.at[d], x_dev(p.dx(-d)))
    value = g_t[p.q].astype(F32)
    for d in (1, 2, 3):
        value = value + g_x[d].astype(F32)
    g_y[p.y] = value.astype(BF16)
    in_y.start()
    step(dn_x)
    add_into(dn_chunk_x(p.x), [d_xf.at[0], d_xf.at[1]])
    step(dn_y)
    step(misc_steps)
    g_c[p.c] = in_y.total().astype(BF16)
    in_c.start()
    step(up_x)
    step(dn_y)
    step(misc_steps)
    step(up_x)
    up_out[...] = up_chunk(p.x)[...].astype(F32) + u_xf[0].astype(F32) + u_xf[1].astype(F32)
    in_c.wait()
    gate_out[...] = g_c[...].astype(F32)
    step(dn_y)
    dn_out[...] = dn_chunk(p.y)[...].astype(F32) + d_yf[0].astype(F32) + d_yf[1].astype(F32)
    mail.finish()


ANY = pl.BlockSpec(memory_space=pl.ANY)
VMEM = pl.BlockSpec(memory_space=pltpu.VMEM)
SMEM = pl.BlockSpec(memory_space=pltpu.SMEM)


def hand_out(up, dn, gate, total, loss, up_out, dn_out, tanh_out, sigmoid_out, score_out, loss_out):
    up_out[...] = up[...]
    dn_out[...] = dn[...]
    tanh_out[...] = gate[0]
    sigmoid_out[...] = gate[1]
    score_out[pl.ds(0, 128)] = total[0]
    score_out[pl.ds(128, 128)] = total[1]
    loss_out[0] = loss[2, 0]


def per_device(
    patch_class_features, live_tiles, tile_patient, ln_gain, up_weight, down_weight, tanh_weight,
    sigmoid_weight, score_weight, queue_keys, queue_labels, patient_labels, loss_scale,
):
    out = lambda *dims: jax.ShapeDtypeStruct(dims, F32)
    vm = lambda *dims: pltpu.VMEM(dims, BF16)
    vf = lambda *dims: pltpu.VMEM(dims, F32)
    up_grad, down_grad, gate_grad, total = pl.pallas_call(
        kernel,
        name="step",
        out_shape=(out(96, HID), out(96, HID), out(2, 96, GATE), out(8, 128)),
        in_specs=[VMEM, SMEM, VMEM, VMEM, ANY, ANY, VMEM, VMEM, VMEM, ANY, VMEM, SMEM, SMEM],
        out_specs=(VMEM,) * 4,
        scratch_shapes=[
            vm(TOK, D),
            vm(D, TOK),
            vm(D, 2 * ROWS),
            vm(ROWS, D),
            vm(2, D, HID),
            vm(2, HID, D),
            vm(D, 2 * HID),
            vm(2, 4, 2, NZ, 48, 128),
            vm(D, 640),
            vm(768, 640),
            vm(2 * HID, 2 * GATE),
            vm(2 * GATE, 2 * HID),
            vm(TOK, 2 * HID),
            vm(2 * HID, TOK),
            vm(TOK, 2 * HID),
            vm(TOK, 2 * GATE),
            vm(TOK, 2 * GATE),
            vm(1024, D),
            vm(D, 1024),
            vm(TOK, 2 * HID),
            vm(TOK, 2 * GATE),
            vm(2 * HID, 2 * GATE),
            vm(2 * HID, 2 * GATE),
            vm(2 * HID, 2 * GATE),
            vm(640, 2 * HID),
            vm(2 * ROWS, GATE),
            vf(2, 8, D + 768),
            vf(256, HID),
            vm(4, 3, ROWS // 2, 2 * GATE),
            vm(4, 4, ROWS // 2, 2 * GATE),
            vf(NZ, 8, 128),
            vf(3, NZ, 8, 896),
            vf(3, 2, 8, 896),
            vf(NZ, 8, 128),
            vf(NZ, 128),
            vf(NZ, 128),
            vm(TOK, 2 * HID),
            vm(8, 96, 2 * HID),
            vm(2, 4, 96, 2 * HID),
            vm(2, 4, 96, 2 * HID),
            vm(D, GATE),
            vm(2, 96, 2 * HID),
            vm(2, 2, 96, 2 * HID),
            vm(2, 48, HID),
            vm(2, 96, HID),
            vm(2, 2, 96, HID),
            vm(2, 4, 96, HID),
            vm(2, 48, HID),
            vm(2, 96, HID),
            vm(4, 3, 96, GATE),
            vm(4, 4, 96, GATE),
            vm(2, 96, GATE),
            vm(4, 96, GATE),
            vm(4, 96, GATE),
            vm(2, 96, GATE),
            vf(NZ, 8, 128),
            vf(4, 8, 128),
            vf(4, 8, 128),
            vf(2, 8, 128),
            pltpu.SemaphoreType.DMA((192,)),
            pltpu.SemaphoreType.DMA((192,)),
            pltpu.SemaphoreType.DMA((4,)),
        ],
        compiler_params=pltpu.CompilerParams(collective_id=1, has_side_effects=True, vmem_limit_bytes=VMEM_LIMIT),
    )(
        patch_class_features, live_tiles, tile_patient[None, :], ln_gain, up_weight, down_weight,
        tanh_weight, sigmoid_weight, score_weight[None, :], queue_keys, queue_labels[None, :], patient_labels,
        loss_scale.reshape(1),
    )
    outputs = pl.pallas_call(
        hand_out,
        name="hand_out",
        out_shape=(out(96, HID), out(96, HID), out(96, GATE), out(96, GATE), out(GATE), out(1)),
        in_specs=[VMEM] * 4 + [SMEM],
        out_specs=(VMEM,) * 5 + (SMEM,),
    )(up_grad, down_grad, gate_grad, total, total)
    return (outputs[0], outputs[1].T, *outputs[2:5], outputs[5].reshape(()))


def solution(mesh):
    placed = (
        P(("pat", "tile"), None),
        P(("pat", "tile")),
        P(("pat", "tile")),
        P(),
        P(None, "tile"),
        P("tile", None),
        P("tile", None),
        P("tile", None),
        P(),
        P("tile", None),
        P("tile"),
        P("pat"),
        P(),
    )
    return jax.shard_map(
        per_device,
        mesh=mesh,
        in_specs=placed,
        out_specs=(P("pat", "tile"), P("tile", "pat"), P("tile", None), P("tile", None), P(), P()),
        check_vma=False,
    )
```

```python
import jax
import jax.numpy as jnp
from jax import lax
from jax.experimental import pallas as pl
from jax.experimental.pallas import tpu as pltpu
from jax.sharding import PartitionSpec as P

MESH = pl.DeviceIdType.MESH
F32 = jnp.float32
BF16 = jnp.bfloat16
HIGH = lax.Precision.HIGHEST
INV_TEMP = 1.0 / 0.07
NZ = 8
NY = 4
NX = 4
ROWS = 128
TOK = NZ * ROWS
D = 1536
HID = 384
GATE = 256
VMEM_LIMIT = 63 << 20


class Place:
    def __init__(self):
        self.pat = lax.axis_index("pat")
        self.tile = lax.axis_index("tile")
        self.z = lax.div(self.tile, 2)
        self.q = lax.rem(self.tile, 2)
        self.xl = lax.div(self.pat, 8)
        self.y = lax.rem(lax.div(self.pat, 2), 4)
        self.c = lax.rem(self.pat, 2)
        self.x = self.q * 2 + self.xl

    def at(self, z=None, y=None, x=None, c=None):
        z = self.z if z is None else z
        y = self.y if y is None else y
        c = self.c if c is None else c
        if x is None:
            xl, q = self.xl, self.q
        else:
            xl, q = lax.rem(x, 2), lax.div(x, 2)
        return (xl * 8 + y * 2 + c, z * 2 + q)

    def dz(self, d):
        return lax.rem(self.z + (d + NZ), NZ)

    def dy(self, d):
        return lax.rem(self.y + (d + NY), NY)

    def dx(self, d):
        return lax.rem(self.x + (d + NX), NX)


def dot(a, b, dims=((1,), (0,))):
    return lax.dot_general(a, b, (dims, ((), ())), preferred_element_type=F32)


class Mail:
    def __init__(self, send_sem, recv_sem):
        self.send_sem, self.recv_sem = send_sem, recv_sem
        self.next = 0
        self.sent = []

    def slots(self, n):
        first = self.next
        self.next += n
        return first

    def send(self, k, src, dst, device):
        copy = pltpu.make_async_remote_copy(
            src_ref=src, dst_ref=dst, send_sem=self.send_sem.at[k], recv_sem=self.recv_sem.at[k],
            device_id=device, device_id_type=MESH,
        )
        copy.start()
        self.sent.append(copy)

    def arrive(self, k, dst, device):
        pltpu.make_async_remote_copy(
            src_ref=dst, dst_ref=dst, send_sem=self.send_sem.at[k], recv_sem=self.recv_sem.at[k],
            device_id=device, device_id_type=MESH,
        ).wait_recv()

    def settle(self, keep=0):
        done = len(self.sent) - keep
        for copy in self.sent[:done]:
            copy.wait_send()
        self.sent = self.sent[done:]


def rows_at(index, size, offset=0, count=None):
    count = size if count is None else count
    return pl.ds(pl.multiple_of(index * size + offset, 16), count)


def lanes_at(index, size):
    return pl.ds(pl.multiple_of(index * size, 128), size)


class ZGather:
    def __init__(self, mail, place, ref, size):
        self.mail, self.place, self.ref, self.size = mail, place, ref, size
        self.half = size // 2
        self.key = mail.slots(16)
        self.chains = ((1, 0, 4), (-1, 0, 3), (1, 1, 3), (-1, 1, 4))

    def piece(self, owner, half):
        return self.ref.at[rows_at(owner, self.size, half * self.half, self.half)]

    def step(self, s, which=(0, 1, 2, 3)):
        p = self.place
        for i in which:
            way, half, steps = self.chains[i]
            block = self.piece(p.dz(-way * s), half)
            if 0 < s <= steps:
                self.mail.arrive(self.key + i * 4 + s - 1, block, p.at(z=p.dz(-way)))
            if s < steps:
                self.mail.send(self.key + i * 4 + s, block, block, p.at(z=p.dz(way)))


class ZReduce:
    def __init__(self, mail, place, ref, size, stage, recv):
        self.mail, self.place, self.ref, self.size = mail, place, ref, size
        self.stage, self.recv = stage, recv
        self.half = size // 2
        self.key = mail.slots(16)
        self.chains = ((1, 0, 4), (-1, 1, 4), (1, 1, 3), (-1, 0, 3))

    def piece(self, owner, half):
        return rows_at(owner, self.size, half * self.half, self.half)

    def step(self, s, which=(0, 1, 2, 3)):
        p = self.place
        for i in which:
            way, half, steps = self.chains[i]
            if s < steps:
                dest = self.piece(p.dz(way * (steps - s)), half)
                if s == 0:
                    src = self.ref.at[dest]
                else:
                    self.mail.arrive(self.key + i * 4 + s - 1, self.recv.at[i, s - 1], p.at(z=p.dz(-way)))
                    src = self.stage.at[i, s - 1]
                    src[...] = (self.ref[dest].astype(F32) + self.recv[i, s - 1].astype(F32)).astype(BF16)
                self.mail.send(self.key + i * 4 + s, src, self.recv.at[i, s], p.at(z=p.dz(way)))

    def total(self):
        p = self.place
        for i, (way, half, steps) in enumerate(self.chains):
            self.mail.arrive(self.key + i * 4 + steps - 1, self.recv.at[i, steps - 1], p.at(z=p.dz(-way)))
        first = self.ref[self.piece(p.z, 0)].astype(F32) + self.recv[0, 3].astype(F32) + self.recv[3, 2].astype(F32)
        second = self.ref[self.piece(p.z, 1)].astype(F32) + self.recv[1, 3].astype(F32) + self.recv[2, 2].astype(F32)
        return jnp.concatenate([first, second], axis=0)


class Swap:
    def __init__(self, mail, ref, me, n, device_of):
        self.mail, self.ref, self.me, self.n, self.device_of = mail, ref, me, n, device_of
        self.key = mail.slots(n - 1)

    def other(self, d):
        return lax.rem(self.me + d, self.n)

    def start(self):
        for d in range(1, self.n):
            mine = self.ref.at[self.me]
            self.mail.send(self.key + d - 1, mine, mine, self.device_of(self.other(d)))

    def wait(self):
        for d in range(1, self.n):
            source = self.other(self.n - d)
            self.mail.arrive(self.key + d - 1, self.ref.at[source], self.device_of(source))

    def total(self):
        self.wait()
        value = self.ref[0].astype(F32)
        for j in range(1, self.n):
            value = value + self.ref[j].astype(F32)
        return value


def two_part(a):
    top = a.astype(BF16).astype(F32)
    return jnp.concatenate([top, a - top], axis=0).astype(BF16)


def dot_two(a, b, transposed=False):
    dims = (((1,), (1,)), ((), ())) if transposed else (((1,), (0,)), ((), ()))
    both = lax.dot_general(two_part(a), b, dims, preferred_element_type=F32)
    half = a.shape[0]
    return both[:half] + both[half:]


def add_into(acc, others):
    value = acc[...].astype(F32)
    for other in others:
        value = value + other[...].astype(F32)
    acc[...] = value.astype(BF16)


def ring_sum(mail, key, pos, nxt, prv, get, half, hbuf, fbuf):
    at = lambda d: lax.rem(pos + d, 4)
    mail.send(key, half(get(at(2)), 0), hbuf.at[0], nxt)
    mail.send(key + 1, half(get(at(2)), 1), hbuf.at[1], prv)
    yield
    mail.arrive(key, hbuf.at[0], prv)
    add_into(half(get(at(1)), 0), [hbuf.at[0]])
    mail.send(key + 2, get(at(1)), fbuf.at[0], nxt)
    mail.arrive(key + 1, hbuf.at[1], nxt)
    add_into(half(get(at(3)), 1), [hbuf.at[1]])
    mail.send(key + 3, get(at(3)), fbuf.at[1], prv)
    yield
    mail.arrive(key + 2, fbuf.at[0], prv)
    mail.arrive(key + 3, fbuf.at[1], nxt)


K_GELU = 0.7071067811865476
K_SLOPE = 0.3989422804014327
BLOCK16 = 16


def gelu_rows(pre_t, h_s, slope_s, t, row, lanes):
    v = pre_t[pl.ds(t, BLOCK16)]
    half = 0.5 * (1.0 + lax.erf(v * K_GELU))
    h_s[pl.ds(row, BLOCK16), lanes] = (v * half).astype(BF16)
    slope_s[pl.ds(row, BLOCK16), lanes] = (half + v * jnp.exp(-0.5 * v * v) * K_SLOPE).astype(BF16)


def kernel(
    x_ref, live, tile_patient, gain, up_hbm, dn_hbm, wt, ws, sw_ref, keys_hbm, qlab, plab, scale,
    up_out, dn_out, gate_out, misc_out,
    n_all, n_t, x_t, x_mate, up_b, dn_b, dn_t, wq, w_x, w_c, thru, thru_t, h_s, h_t, slope_s, part, uv_all, keys, keys_t,
    pg_s, pre_s, held_t, held_o, held_sum, held, pre2, gx, pre_t,
    stage, recv, pbuf, vbuf, zbuf, xbuf, sbuf, score_all, alpha_all, pull_s,
    up0, up_acc, dn_acc, g_acc, u_yh, u_yf, u_xh, u_xf, d_xh, d_xf, d_yh, d_yf,
    g_stage, g_recv, g_t, g_y, g_x, g_c, m_z, m_y, m_x, m_c,
    send_sem, recv_sem, local_sem,
):
    p = Place()
    mail = Mail(send_sem, recv_sem)
    mate, beside = p.at(c=1 - p.c), p.at(x=3 - p.x)
    above, below = p.at(y=p.dy(1)), p.at(y=p.dy(-1))
    z_dev = lambda z: p.at(z=z)
    y_dev = lambda y: p.at(y=y)
    x_dev = lambda x: p.at(x=x)
    c_dev = lambda c: p.at(c=c)
    q_dev = lambda q: (p.pat, p.z * 2 + q)
    partners = (
        [z_dev(p.dz(d)) for d in range(1, NZ)]
        + [y_dev(p.dy(d)) for d in (1, 2, 3)]
        + [x_dev(p.dx(d)) for d in (1, 2, 3)]
        + [mate]
    )
    barrier = pltpu.get_barrier_semaphore()
    for device in partners:
        pl.semaphore_signal(barrier, inc=1, device_id=device, device_id_type=MESH)

    fetch_up = pltpu.make_async_copy(up_hbm, up_b.at[p.q], local_sem.at[0])
    fetch_dn = pltpu.make_async_copy(dn_hbm, dn_b.at[p.q], local_sem.at[1])
    fetch_keys = pltpu.make_async_copy(keys_hbm, keys, local_sem.at[2])
    fetch_up.start()
    fetch_dn.start()
    fetch_keys.start()

    def norm_rows(half):
        v = x_ref[pl.ds(half * 64, 64)].astype(F32)
        center = v - jnp.mean(v, axis=1, keepdims=True)
        spread = jnp.mean(center * center, axis=1, keepdims=True)
        n_all[rows_at(p.z, ROWS, half * 64, 64)] = (center * lax.rsqrt(spread + 1e-06) * gain[...][None, :]).astype(BF16)

    g_rows = pl.ds(pl.multiple_of(p.c * 48, 16), 48)
    g_lanes = lanes_at(lax.rem(p.y, 2), 128)
    wq[p.c, p.y, p.q, p.z] = jnp.where(p.y < 2, wt[g_rows, g_lanes], ws[g_rows, g_lanes])

    norm_rows(0)
    pl.semaphore_wait(barrier, len(partners))

    tokens = ZGather(mail, p, n_all, ROWS)
    k_wz, k_w = mail.slots(7), mail.slots(1)
    w_z = lambda z: wq.at[p.c, p.y, p.q, z]
    for d in range(1, NZ):
        mail.send(k_wz + d - 1, w_z(p.z), w_z(p.z), z_dev(p.dz(d)))
    tokens.step(0, (0, 1))
    norm_rows(1)
    k_x0 = mail.slots(1)
    mail.send(k_x0, x_ref, x_mate, mate)

    up_piece = lambda q, y, c: up_b.at[q, rows_at(y * 2 + c, 192)]
    dn_piece = lambda q, y, c: dn_b.at[q, rows_at(y * 2 + c, 48)]
    theirs, other = 1 - p.q, 1 - p.c
    k_px, k_py, k_pm = mail.slots(2), mail.slots(6), mail.slots(8)
    fetch_up.wait()
    mail.send(k_px, up_piece(p.q, p.y, p.c), up_piece(p.q, p.y, p.c), beside)
    fetch_dn.wait()
    mail.send(k_px + 1, dn_piece(p.q, p.y, p.c), dn_piece(p.q, p.y, p.c), beside)

    def to_mate(d, piece, which):
        mail.send(k_pm + which * 4 + d, piece(theirs, p.dy(d), p.c), piece(theirs, p.dy(d), p.c), mate)

    def pieces_x():
        for which, piece in enumerate((up_piece, dn_piece)):
            block = piece(theirs, p.y, p.c)
            mail.arrive(k_px + which, block, beside)
            mail.send(k_py + which * 2, block, block, above)
            mail.send(k_py + which * 2 + 1, block, block, below)
            to_mate(0, piece, which)

        for which, piece in enumerate((up_piece, dn_piece)):
            block = piece(p.q, p.dy(2), p.c)
            mail.send(k_py + 4 + which, block, block, beside)

    def pieces_y():
        for which, piece in enumerate((up_piece, dn_piece)):
            mail.arrive(k_py + which * 2, piece(theirs, p.dy(-1), p.c), below)
            to_mate(3, piece, which)
            mail.arrive(k_py + which * 2 + 1, piece(theirs, p.dy(1), p.c), above)
            to_mate(1, piece, which)

    def pieces_far():
        for which, piece in enumerate((up_piece, dn_piece)):
            mail.arrive(k_py + 4 + which, piece(theirs, p.dy(2), p.c), beside)
            to_mate(2, piece, which)

    def pieces_mate(which):
        piece = (up_piece, dn_piece)[which]
        for d in range(4):
            mail.arrive(k_pm + which * 4 + d, piece(theirs, p.dy(d), other), mate)

    def hidden(owners, q):
        lhs = jnp.concatenate([n_all[rows_at(o, ROWS)] for o in owners], axis=0)
        count = len(owners) * ROWS
        pre_t[pl.ds(0, count)] = dot(lhs, up_b[q])
        lanes = lanes_at(q, HID)
        for j, o in enumerate(owners):
            def body(i, carry, j=j, o=o):
                t = pl.multiple_of(j * ROWS + i * BLOCK16, BLOCK16)
                row = pl.multiple_of(o * ROWS + i * BLOCK16, BLOCK16)
                gelu_rows(pre_t, h_s, slope_s, t, row, lanes)
                return carry

            lax.fori_loop(0, ROWS // BLOCK16, body, 0)

    def turn(owners):
        for o in owners:
            n_t[:, lanes_at(o, ROWS)] = n_all[rows_at(o, ROWS)].T

    def key_rows(i):
        at = pl.ds(i * 256, 256)
        v = keys[at].astype(F32)
        keys[at] = (v * lax.rsqrt(jnp.sum(v * v, axis=1, keepdims=True) + 1e-06)).astype(BF16)

    k_wy, k_wm = mail.slots(4), mail.slots(1)
    w_y = lambda y: wq.at[p.c, y]
    w_yh = lambda y, half: wq.at[p.c, y, half]
    near = [p.dz(1), p.dz(-1)]
    mid = [p.dz(2), p.dz(-2)]
    far = [p.dz(3), p.dz(-3)]

    hidden([p.z], p.q)
    turn([p.z])
    x_t[:, pl.ds(0, ROWS)] = x_ref[...].T
    for d in range(1, NZ):
        mail.arrive(k_wz + d - 1, w_z(p.dz(-d)), z_dev(p.dz(-d)))
    mail.send(k_w, wq.at[p.c, p.y, p.q], wq.at[p.c, p.y, p.q], beside)
    tokens.step(0, (2, 3))
    fetch_keys.wait()
    key_rows(0)
    tokens.step(1, (0, 1))
    mail.arrive(k_w, wq.at[p.c, p.y, theirs], beside)
    mail.send(k_wy, w_y(p.y), w_y(p.y), above)
    mail.send(k_wy + 1, w_y(p.y), w_y(p.y), below)
    pieces_x()
    tokens.step(1, (2, 3))
    hidden(near, p.q)
    turn(near)
    key_rows(1)
    tokens.step(2, (0, 1))
    key_rows(2)
    key_rows(3)
    mail.arrive(k_wy, w_y(p.dy(-1)), below)
    mail.send(k_wy + 2, w_yh(p.dy(-1), 0), w_yh(p.dy(-1), 0), above)
    mail.arrive(k_wy + 1, w_y(p.dy(1)), above)
    mail.send(k_wy + 3, w_yh(p.dy(1), 1), w_yh(p.dy(1), 1), below)
    tokens.step(2, (2, 3))
    hidden(mid, p.q)
    turn(mid)
    pieces_y()
    mail.arrive(k_wy + 2, w_yh(p.dy(2), 0), below)
    mail.arrive(k_wy + 3, w_yh(p.dy(2), 1), above)
    mail.send(k_wm, wq.at[p.c], wq.at[p.c], mate)
    pieces_far()
    tokens.step(3, (0, 1))
    pieces_mate(0)
    hidden([p.z], theirs)
    hidden(near, theirs)
    hidden(mid, theirs)
    mail.arrive(k_wm, wq.at[other], mate)

    def place_w(t, carry):
        for y in range(4):
            for c in range(2):
                row = pl.multiple_of(t * 96 + c * 48, 16)
                w_x[pl.ds(row, 48), pl.ds(y * 128, 128)] = wq[c, y, lax.rem(t, 2), lax.div(t, 2)]
        return carry

    lax.fori_loop(0, 16, place_w, 0)
    w_full = lambda: w_x[:, pl.ds(0, 2 * GATE)]
    pieces_mate(1)
    for q in range(2):
        thru[pl.ds(q * HID, HID)] = dot(dn_b[q], w_full()).astype(BF16)

    def gate_part(o, carry):
        at = rows_at(o, ROWS)
        part[at] = dot(h_s[at], thru[...]).astype(BF16)
        return carry

    tokens.step(3, (2, 3))
    for j in range(2):
        keys_t[:, pl.ds(j * 512, 512)] = keys[pl.ds(j * 512, 512)].T
    hidden(far, p.q)
    hidden(far, theirs)
    turn(far)
    lax.fori_loop(0, NZ - 1, lambda d, carry: gate_part(lax.rem(p.z + 5 + d, NZ), carry), 0)
    tokens.step(4)
    last = p.dz(4)
    hidden([last], 0)
    hidden([last], 1)
    gate_part(last, 0)

    reduce = ZReduce(mail, p, part, ROWS, stage, recv)
    gather_uv = ZGather(mail, p, uv_all, ROWS)
    swap_p = Swap(mail, pbuf, p.z, NZ, z_dev)
    swap_z = [Swap(mail, ref, p.z, NZ, z_dev) for ref in (vbuf, zbuf.at[0], zbuf.at[1])]
    swap_x = [Swap(mail, xbuf.at[i], p.q, 2, q_dev) for i in range(3)]
    swap_s = Swap(mail, sbuf, p.z, NZ, z_dev)

    row8 = lax.broadcasted_iota(jnp.int32, (8, 128), 0)
    first4 = row8 < 4
    row_patient = lax.rem(row8, 4)
    first4_wide = lax.broadcasted_iota(jnp.int32, (8, 768), 0) < 4
    lane = lax.broadcasted_iota(jnp.int32, (8, 128), 1)

    def pack(v):
        return jnp.where(first4_wide, v[:, :768], v[:, 768:])

    def unpack(v):
        rolled = pltpu.roll(v, 4, 0)
        return jnp.concatenate([jnp.where(first4_wide, v, rolled), jnp.where(first4_wide, rolled, v)], axis=1)

    reduce.step(0, (0, 1))
    turn([last])
    dn_t[:, pl.ds(0, HID)] = dn_b[0].T
    reduce.step(0, (2, 3))
    dn_t[:, pl.ds(HID, HID)] = dn_b[1].T
    gate_x = dot(x_ref[...], w_full())
    reduce.step(1, (0, 1))
    same = jnp.zeros((8, 1024), jnp.int32)
    row_wide = lax.rem(lax.broadcasted_iota(jnp.int32, (8, 1024), 0), 4)
    labels = jnp.broadcast_to(qlab[...], (8, 1024))
    for k in range(4):
        same = jnp.where((row_wide == k) & (labels == plab[k]), 1, same)
    same = same.astype(F32)
    label_sums = dot(same.astype(BF16), keys[...])
    positives = jnp.sum(same, axis=1, keepdims=True)
    reduce.step(1, (2, 3))
    for z in range(NZ):
        h_t[:, pl.ds(z * ROWS, ROWS)] = h_s[pl.ds(z * ROWS, ROWS)].T
    reduce.step(2, (0, 1))
    for i in range(8):
        w_c[pl.ds(i * 96, 96), pl.ds(0, 512)] = w_x[pl.ds(pl.multiple_of((i * 2 + p.c) * 96, 96), 96), pl.ds(0, 512)]
    reduce.step(2, (2, 3))
    mail.arrive(k_x0, x_mate, mate)
    x_t[:, pl.ds(ROWS, ROWS)] = x_mate[...].T
    reduce.step(3, (0, 1))
    mail.settle(20)
    gates = reduce.total() + gate_x
    tanh_val = jnp.tanh(gates[:, :GATE])
    sigmoid_val = jax.nn.sigmoid(gates[:, GATE:])
    product = tanh_val * sigmoid_val
    sw = sw_ref[...]
    score = lax.dot_general(
        jnp.broadcast_to(sw, (8, GATE)), product, (((1,), (1,)), ((), ())), precision=HIGH, preferred_element_type=F32
    )
    in_tile = lax.broadcasted_iota(jnp.int32, (8, 128), 1) < live[0]
    onehot = (jnp.broadcast_to(tile_patient[...], (8, 128)) == row_patient) & in_tile
    mass = jnp.where(onehot, jnp.exp(score), 0.0)
    pbuf[p.z] = mass
    swap_p.start()
    common = sw * sigmoid_val
    own_rows = rows_at(p.z, ROWS)
    uv_all[own_rows, pl.ds(0, GATE)] = (common * (1.0 - tanh_val * tanh_val)).astype(BF16)
    uv_all[own_rows, pl.ds(GATE, GATE)] = (common * tanh_val * (1.0 - sigmoid_val)).astype(BF16)
    gather_uv.step(0)

    def post(i, packed, small):
        zbuf[i - 1, p.z, :, pl.ds(0, 768)] = packed
        zbuf[i - 1, p.z, :, pl.ds(768, 128)] = small
        swap_z[i].start()

    def collect_z(i):
        xbuf[i, p.q] = swap_z[i].total()
        swap_x[i].start()

    post(1, pack(label_sums), jnp.broadcast_to(positives, (8, 128)))
    vec_x = dot_two(mass, x_ref[...])
    swap_p.wait()

    total = jnp.zeros((8, 1), F32)
    for z in range(NZ):
        total += jnp.sum(pbuf[z], axis=1, keepdims=True)
    mass_all = jnp.concatenate([pbuf[z] for z in range(NZ)], axis=1)
    mass_h = dot_two(mass_all, h_s[...])
    vec = dot_two(mass_h[:, :HID], dn_b[0]) + dot_two(mass_h[:, HID:], dn_b[1]) + vec_x

    packed = pack(vec)
    top = total.astype(BF16).astype(F32)
    small = jnp.where(lane == 0, top, total - top)
    vbuf[p.z, :, pl.ds(0, 384)] = jnp.concatenate([packed[:, :384], packed[:, 384:]], axis=0).astype(BF16)
    vbuf[p.z, :, pl.ds(384, 128)] = jnp.concatenate([small, small], axis=0).astype(BF16)
    swap_z[0].start()
    both = swap_z[0].total()
    xbuf[0, p.q, :, pl.ds(0, 384)] = both[:8, :384]
    xbuf[0, p.q, :, pl.ds(384, 384)] = both[8:, :384]
    xbuf[0, p.q, :, pl.ds(768, 128)] = jnp.broadcast_to(both[:8, 384:385] + both[:8, 385:386], (8, 128))
    swap_x[0].start()
    gather_uv.step(1)
    collect_z(1)
    thru_t[...] = thru[...].T
    summed = swap_x[0].total()
    total_mass = summed[:, 768:769]
    pooled = unpack(summed[:, :768]) / total_mass
    length = jnp.sqrt(jnp.sum(pooled * pooled, axis=1, keepdims=True) + 1e-06)
    unit = pooled / length

    logits = dot(unit.astype(BF16), keys_t[...]) / 0.07
    exps = jnp.exp(logits)
    exp_part = jnp.sum(exps, axis=1, keepdims=True)
    pos_part = jnp.sum(same * logits, axis=1, keepdims=True)
    post(2, pack(dot_two(exps, keys[...])), jnp.where(lane == 0, exp_part, pos_part))
    collect_z(2)
    gather_uv.step(2)
    labels_total = swap_x[1].total()
    pos_count = labels_total[:, 768:769]
    queue_total = swap_x[2].total()
    exp_total = queue_total[:, 768:769]
    pos_logits = queue_total[:, 769:770]
    unit_grad = (scale[0] * INV_TEMP) * (
        unpack(queue_total[:, :768]) / exp_total - unpack(labels_total[:, :768]) / pos_count
    )
    pooled_grad = (unit_grad - unit * jnp.sum(unit * unit_grad, axis=1, keepdims=True)) / length

    grad_h = dot_two(pooled_grad, dn_t[...])
    own_dots = dot_two(pooled_grad, x_t[:, pl.ds(0, ROWS)])
    dots = dot_two(grad_h, h_t[...])
    for z in range(NZ):
        block = dots[:, z * ROWS : (z + 1) * ROWS] + jnp.where(p.z == z, own_dots, 0.0)
        picked = jnp.where((pbuf[z] > 0.0) & first4, block, 0.0)
        sbuf[p.z, pl.ds(z, 1)] = jnp.sum(picked, axis=0, keepdims=True)
    swap_s.start()
    center = jnp.sum(pooled * pooled_grad, axis=1, keepdims=True)
    log_part = jnp.log(exp_total) - pos_logits / pos_count
    loss = jnp.sum(jnp.where(first4, jnp.broadcast_to(log_part, (8, 128)), 0.0), axis=0, keepdims=True)
    for z in range(NZ):
        block = jnp.where(first4, pbuf[z], 0.0)
        alpha_all[pl.ds(z, 1)] = jnp.sum(block / total_mass, axis=0, keepdims=True)
        score_all[pl.ds(z, 1)] = jnp.sum(jnp.where(block > 0.0, center, 0.0), axis=0, keepdims=True)
    gather_uv.step(3)
    pad = jnp.zeros((120, 768), F32)
    grad_h_pad = jnp.concatenate([jnp.where(first4_wide, grad_h, 0.0), pad], axis=0).astype(BF16)
    rest = jnp.zeros((120, 128), F32)

    def pulled(b, carry):
        mass_b = jnp.where(first4, pbuf[b], 0.0)
        weight = jnp.where(mass_b > 0.0, jnp.broadcast_to(alpha_all[pl.ds(b, 1)], (8, 128)), 0.0)
        at = rows_at(b, ROWS)
        turned = jnp.concatenate([weight, rest], axis=0).T.astype(BF16)
        pull_s[at] = (dot(turned, grad_h_pad) * slope_s[at].astype(F32)).astype(BF16)
        return carry + dot_two(weight, h_s[at])

    held4 = lax.fori_loop(0, NZ, pulled, jnp.zeros((8, 768), F32))
    k_g = mail.slots(1)
    gx[0, :, pl.ds(0, D)] = pooled_grad
    gx[0, :, pl.ds(D, 768)] = jnp.where(first4_wide, held4, 0.0)
    mail.send(k_g, gx.at[0], gx.at[1], mate)
    gather_uv.step(4)

    def scaled(b, carry):
        at = pl.ds(pl.multiple_of(b * 256, 256), 256)
        pg_s[at] = (dot(uv_all[at], thru_t[...]) * slope_s[at].astype(F32)).astype(BF16)
        return carry

    lax.fori_loop(0, 4, scaled, 0)
    mail.arrive(k_g, gx.at[1], mate)
    grad_pad = jnp.concatenate([gx[0, :, pl.ds(0, D)], gx[1, :, pl.ds(0, D)], jnp.zeros((112, D), F32)], axis=0)
    for j in range(D // 128):
        w_x[pl.ds(j * 128, 128), pl.ds(512, 128)] = grad_pad[:, j * 128 : (j + 1) * 128].T.astype(BF16)
    for i in range(8):
        w_c[pl.ds(i * 96, 96), pl.ds(512, 128)] = w_x[pl.ds(pl.multiple_of((i * 2 + p.c) * 96, 96), 96), pl.ds(512, 128)]
    held[pl.ds(512, 128)] = jnp.concatenate(
        [gx[0, :, pl.ds(D, 768)], gx[1, :, pl.ds(D, 768)], jnp.zeros((112, 768), F32)], axis=0
    ).astype(BF16)
    mail.settle(12)
    score_all[...] = alpha_all[...] * (swap_s.total() - score_all[...])

    def apply_scores(b, carry):
        at = rows_at(b, ROWS)
        grad = jnp.broadcast_to(score_all[pl.ds(b, 1)], (ROWS, ROWS)).T[:, 0:1]
        pre_s[at] = (grad * uv_all[at].astype(F32)).astype(BF16)
        pg_s[at] = (grad * pg_s[at].astype(F32) + pull_s[at].astype(F32)).astype(BF16)
        return carry

    lax.fori_loop(0, NZ, apply_scores, 0)
    score_part = lax.dot_general(
        jnp.broadcast_to(score_all[pl.ds(p.z, 1)], (8, ROWS)), product, (((1,), (0,)), ((), ())),
        precision=HIGH, preferred_element_type=F32,
    )
    misc = jnp.where(
        row8 == 0, score_part[:, :128], jnp.where(row8 == 1, score_part[:, 128:], jnp.where(row8 == 2, loss / 16.0, 0.0))
    )

    def misc_chain(value):
        stages = [
            (Swap(mail, m_z, p.z, NZ, z_dev), m_z, p.z),
            (Swap(mail, m_y, p.y, 4, y_dev), m_y, p.y),
            (Swap(mail, m_x, p.x, 4, x_dev), m_x, p.x),
            (Swap(mail, m_c, p.c, 2, c_dev), m_c, p.c),
        ]
        for swap, buf, me in stages:
            buf[me] = value
            swap.start()
            yield
            value = swap.total()
        misc_out[...] = value
        yield

    misc_steps = misc_chain(misc)
    next(misc_steps)

    k_h, k_p = mail.slots(1), mail.slots(1)
    for j in range(3):
        held_t[pl.ds(j * 256, 256)] = dot(h_t[pl.ds(j * 256, 256)], pre_s[...]).astype(BF16)
    mail.send(k_h, held_t, held_o, mate)
    theirs_pre = pre_s.at[own_rows, lanes_at(other, GATE)]
    mail.send(k_p, theirs_pre, pre2.at[pl.ds(ROWS, ROWS)], mate)
    pre2[pl.ds(0, ROWS)] = pre_s[own_rows, lanes_at(p.c, GATE)]

    def sum_held():
        mail.arrive(k_h, held_o, mate)
        total_held = (held_t[...].astype(F32) + held_o[...].astype(F32)).astype(BF16)
        held_sum[...] = total_held
        held[pl.ds(0, 512)] = total_held.T

    def gate_grads():
        mail.arrive(k_p, pre2.at[pl.ds(ROWS, ROWS)], mate)

        def gate_rows(i, carry):
            at = pl.ds(pl.multiple_of(i * 512, 512), 512)
            g_acc[at] = (dot(dn_t[at], held_sum[:, lanes_at(p.c, GATE)]) + dot(x_t[at], pre2[...])).astype(BF16)
            return carry

        lax.fori_loop(0, 3, gate_rows, 0)

    def dn_rows(xl):
        value = dot(w_c[rows_at(xl, 384)], held[...]).astype(BF16)
        for y in range(4):
            dn_acc[xl, y] = value[y * 96 : (y + 1) * 96]

    up_p = lambda i, c: keys_t.at[pl.ds(pl.multiple_of((i * 2 + c) * 96, 96), 96), pl.ds(0, 768)]
    k_up0 = mail.slots(8)

    def compute(block, lhs, rhs, index, k, buf):
        def body(j, carry):
            i = index(j)
            value = dot(lhs[pl.ds(pl.multiple_of(i * 192, 192), 192)], rhs[...]).astype(BF16)
            block(i, 0)[...] = value[:96]
            block(i, 1)[...] = value[96:]
            return carry

        lax.fori_loop(0, 2, body, 0)
        for j in range(2):
            mail.send(k + j, block(index(j), other), buf.at[index(j)], mate)

    def collect(block, index, k, buf, acc):
        for j in range(2):
            mail.arrive(k + j, buf.at[index(j)], mate)

        def body(j, carry):
            i = index(j)
            acc[lax.div(i, 4), lax.rem(i, 4)] = (block(i, p.c)[...].astype(F32) + buf[i].astype(F32)).astype(BF16)
            return carry

        lax.fori_loop(0, 2, body, 0)

    up_index = [lambda j, d=d: j * 4 + p.dy(d) for d in (2, 1, -1, 0)]
    up_go = lambda g: compute(up_p, n_t, pg_s, up_index[g], k_up0 + 2 * g, up0)
    up_take = lambda g: collect(up_p, up_index[g], k_up0 + 2 * g, up0, up_acc)
    rows_half = lambda ref, i: ref.at[pl.ds(i * 48, 48)]
    k_up, k_dn = mail.slots(8), mail.slots(8)
    up_chunk = lambda d: up_acc.at[lax.rem(d, 2), p.y, :, lanes_at(lax.div(d, 2), HID)]
    dn_chunk_x = lambda d: dn_acc.at[lax.rem(d, 2), :, :, lanes_at(lax.div(d, 2), HID)]
    dn_chunk = lambda d: dn_acc.at[p.xl, d, :, lanes_at(p.q, HID)]
    up_y = ring_sum(
        mail, k_up, p.y, above, below, lambda d: up_acc.at[:, d], lambda ref, i: ref.at[i], u_yh, u_yf
    )
    up_x = ring_sum(mail, k_up + 4, p.x, x_dev(p.dx(1)), x_dev(p.dx(-1)), up_chunk, rows_half, u_xh, u_xf)
    dn_x = ring_sum(
        mail, k_dn, p.x, x_dev(p.dx(1)), x_dev(p.dx(-1)), dn_chunk_x, lambda ref, i: ref.at[pl.ds(i * 2, 2)], d_xh, d_xf
    )
    dn_y = ring_sum(mail, k_dn + 4, p.y, above, below, dn_chunk, rows_half, d_yh, d_yf)
    step = lambda chain: next(chain, None)
    zred = ZReduce(mail, p, g_acc, 192, g_stage, g_recv)
    in_y = Swap(mail, g_y, p.y, 4, y_dev)
    k_x = mail.slots(3)
    in_c = Swap(mail, g_c, p.c, 2, c_dev)

    up_go(0)
    sum_held()
    gate_grads()
    zred.step(0, (0, 1))
    up_go(1)
    zred.step(0, (2, 3))
    dn_rows(p.xl)
    dn_rows(1 - p.xl)
    step(dn_x)
    up_take(0)
    step(up_y)
    zred.step(1, (0, 1))
    up_go(2)
    zred.step(1, (2, 3))
    up_go(3)
    step(misc_steps)
    zred.step(2, (0, 1))
    up_take(1)
    up_take(2)
    zred.step(2, (2, 3))
    step(up_y)
    step(dn_x)
    zred.step(3)
    up_take(3)
    step(misc_steps)
    sums = zred.total().astype(BF16)
    g_t[0] = sums[:96]
    g_t[1] = sums[96:]
    for d in (1, 2, 3):
        there = p.dx(d)
        mail.send(k_x + d - 1, g_t.at[lax.div(there, 2)], g_x.at[d], x_dev(there))
    step(up_y)
    add_into(up_acc.at[:, p.y], [u_yf.at[0], u_yf.at[1]])
    step(up_x)
    for d in (1, 2, 3):
        mail.arrive(k_x + d - 1, g_x.at[d], x_dev(p.dx(-d)))
    value = g_t[p.q].astype(F32)
    for d in (1, 2, 3):
        value = value + g_x[d].astype(F32)
    g_y[p.y] = value.astype(BF16)
    in_y.start()
    step(dn_x)
    add_into(dn_chunk_x(p.x), [d_xf.at[0], d_xf.at[1]])
    step(dn_y)
    step(misc_steps)
    g_c[p.c] = in_y.total().astype(BF16)
    in_c.start()
    step(up_x)
    step(dn_y)
    step(misc_steps)
    mail.settle(8)
    step(up_x)
    up_out[...] = up_chunk(p.x)[...].astype(F32) + u_xf[0].astype(F32) + u_xf[1].astype(F32)
    in_c.wait()
    gate_out[...] = g_c[...].astype(F32)
    step(dn_y)
    dn_out[...] = dn_chunk(p.y)[...].astype(F32) + d_yf[0].astype(F32) + d_yf[1].astype(F32)
    mail.settle()


ANY = pl.BlockSpec(memory_space=pl.ANY)
VMEM = pl.BlockSpec(memory_space=pltpu.VMEM)
SMEM = pl.BlockSpec(memory_space=pltpu.SMEM)


def hand_out(up, dn, gate, total, loss, up_out, dn_out, tanh_out, sigmoid_out, score_out, loss_out):
    up_out[...] = up[...]
    dn_out[...] = dn[...]
    tanh_out[...] = gate[0]
    sigmoid_out[...] = gate[1]
    score_out[pl.ds(0, 128)] = total[0]
    score_out[pl.ds(128, 128)] = total[1]
    loss_out[0] = loss[2, 0]


def per_device(
    patch_class_features, live_tiles, tile_patient, ln_gain, up_weight, down_weight, tanh_weight,
    sigmoid_weight, score_weight, queue_keys, queue_labels, patient_labels, loss_scale,
):
    out = lambda *dims: jax.ShapeDtypeStruct(dims, F32)
    vm = lambda *dims: pltpu.VMEM(dims, BF16)
    vf = lambda *dims: pltpu.VMEM(dims, F32)
    up_grad, down_grad, gate_grad, total = pl.pallas_call(
        kernel,
        name="step",
        out_shape=(out(96, HID), out(96, HID), out(2, 96, GATE), out(8, 128)),
        in_specs=[VMEM, SMEM, VMEM, VMEM, ANY, ANY, VMEM, VMEM, VMEM, ANY, VMEM, SMEM, SMEM],
        out_specs=(VMEM,) * 4,
        scratch_shapes=[
            vm(TOK, D),
            vm(D, TOK),
            vm(D, 2 * ROWS),
            vm(ROWS, D),
            vm(2, D, HID),
            vm(2, HID, D),
            vm(D, 2 * HID),
            vm(2, 4, 2, NZ, 48, 128),
            vm(D, 640),
            vm(768, 640),
            vm(2 * HID, 2 * GATE),
            vm(2 * GATE, 2 * HID),
            vm(TOK, 2 * HID),
            vm(2 * HID, TOK),
            vm(TOK, 2 * HID),
            vm(TOK, 2 * GATE),
            vm(TOK, 2 * GATE),
            vm(1024, D),
            vm(D, 1024),
            vm(TOK, 2 * HID),
            vm(TOK, 2 * GATE),
            vm(2 * HID, 2 * GATE),
            vm(2 * HID, 2 * GATE),
            vm(2 * HID, 2 * GATE),
            vm(640, 2 * HID),
            vm(2 * ROWS, GATE),
            vf(2, 8, D + 768),
            vf(256, HID),
            vm(4, 3, ROWS // 2, 2 * GATE),
            vm(4, 4, ROWS // 2, 2 * GATE),
            vf(NZ, 8, 128),
            vm(NZ, 16, 512),
            vf(2, NZ, 8, 896),
            vf(3, 2, 8, 896),
            vf(NZ, 8, 128),
            vf(NZ, 128),
            vf(NZ, 128),
            vm(TOK, 2 * HID),
            vm(8, 96, 2 * HID),
            vm(2, 4, 96, 2 * HID),
            vm(2, 4, 96, 2 * HID),
            vm(D, GATE),
            vm(2, 96, 2 * HID),
            vm(2, 2, 96, 2 * HID),
            vm(2, 48, HID),
            vm(2, 96, HID),
            vm(2, 2, 96, HID),
            vm(2, 4, 96, HID),
            vm(2, 48, HID),
            vm(2, 96, HID),
            vm(4, 3, 96, GATE),
            vm(4, 4, 96, GATE),
            vm(2, 96, GATE),
            vm(4, 96, GATE),
            vm(4, 96, GATE),
            vm(2, 96, GATE),
            vf(NZ, 8, 128),
            vf(4, 8, 128),
            vf(4, 8, 128),
            vf(2, 8, 128),
            pltpu.SemaphoreType.DMA((192,)),
            pltpu.SemaphoreType.DMA((192,)),
            pltpu.SemaphoreType.DMA((4,)),
        ],
        compiler_params=pltpu.CompilerParams(collective_id=1, has_side_effects=True, vmem_limit_bytes=VMEM_LIMIT),
    )(
        patch_class_features, live_tiles, tile_patient[None, :], ln_gain, up_weight, down_weight,
        tanh_weight, sigmoid_weight, score_weight[None, :], queue_keys, queue_labels[None, :], patient_labels,
        loss_scale.reshape(1),
    )
    outputs = pl.pallas_call(
        hand_out,
        name="hand_out",
        out_shape=(out(96, HID), out(96, HID), out(96, GATE), out(96, GATE), out(GATE), out(1)),
        in_specs=[VMEM] * 4 + [SMEM],
        out_specs=(VMEM,) * 5 + (SMEM,),
    )(up_grad, down_grad, gate_grad, total, total)
    return (outputs[0], outputs[1].T, *outputs[2:5], outputs[5].reshape(()))


def solution(mesh):
    placed = (
        P(("pat", "tile"), None),
        P(("pat", "tile")),
        P(("pat", "tile")),
        P(),
        P(None, "tile"),
        P("tile", None),
        P("tile", None),
        P("tile", None),
        P(),
        P("tile", None),
        P("tile"),
        P("pat"),
        P(),
    )
    return jax.shard_map(
        per_device,
        mesh=mesh,
        in_specs=placed,
        out_specs=(P("pat", "tile"), P("tile", "pat"), P("tile", None), P("tile", None), P(), P()),
        check_vma=False,
    )
```

```python
import jax
import jax.numpy as jnp
from jax import lax
from jax.experimental import pallas as pl
from jax.experimental.pallas import tpu as pltpu
from jax.sharding import PartitionSpec as P

MESH = pl.DeviceIdType.MESH
F32 = jnp.float32
BF16 = jnp.bfloat16
HIGH = lax.Precision.HIGHEST
INV_TEMP = 1.0 / 0.07
NZ = 8
NY = 4
NX = 4
ROWS = 128
TOK = NZ * ROWS
D = 1536
HID = 384
GATE = 256
VMEM_LIMIT = 63 << 20


class Place:
    def __init__(self):
        self.pat = lax.axis_index("pat")
        self.tile = lax.axis_index("tile")
        self.z = lax.div(self.tile, 2)
        self.q = lax.rem(self.tile, 2)
        self.xl = lax.div(self.pat, 8)
        self.y = lax.rem(lax.div(self.pat, 2), 4)
        self.c = lax.rem(self.pat, 2)
        self.x = self.q * 2 + self.xl

    def at(self, z=None, y=None, x=None, c=None):
        z = self.z if z is None else z
        y = self.y if y is None else y
        c = self.c if c is None else c
        if x is None:
            xl, q = self.xl, self.q
        else:
            xl, q = lax.rem(x, 2), lax.div(x, 2)
        return (xl * 8 + y * 2 + c, z * 2 + q)

    def dz(self, d):
        return lax.rem(self.z + (d + NZ), NZ)

    def dy(self, d):
        return lax.rem(self.y + (d + NY), NY)

    def dx(self, d):
        return lax.rem(self.x + (d + NX), NX)


def dot(a, b, dims=((1,), (0,))):
    return lax.dot_general(a, b, (dims, ((), ())), preferred_element_type=F32)


class Mail:
    def __init__(self, send_sem, recv_sem):
        self.send_sem, self.recv_sem = send_sem, recv_sem
        self.next = 0
        self.sent = []

    def slots(self, n):
        first = self.next
        self.next += n
        return first

    def send(self, k, src, dst, device):
        copy = pltpu.make_async_remote_copy(
            src_ref=src, dst_ref=dst, send_sem=self.send_sem.at[k], recv_sem=self.recv_sem.at[k],
            device_id=device, device_id_type=MESH,
        )
        copy.start()
        self.sent.append(copy)

    def arrive(self, k, dst, device):
        pltpu.make_async_remote_copy(
            src_ref=dst, dst_ref=dst, send_sem=self.send_sem.at[k], recv_sem=self.recv_sem.at[k],
            device_id=device, device_id_type=MESH,
        ).wait_recv()

    def settle(self, keep=0):
        done = len(self.sent) - keep
        for copy in self.sent[:done]:
            copy.wait_send()
        self.sent = self.sent[done:]


def rows_at(index, size, offset=0, count=None):
    count = size if count is None else count
    return pl.ds(pl.multiple_of(index * size + offset, 16), count)


def lanes_at(index, size):
    return pl.ds(pl.multiple_of(index * size, 128), size)


class ZGather:
    def __init__(self, mail, place, ref, size):
        self.mail, self.place, self.ref, self.size = mail, place, ref, size
        self.half = size // 2
        self.key = mail.slots(16)
        self.chains = ((1, 0, 4), (-1, 0, 3), (1, 1, 3), (-1, 1, 4))

    def piece(self, owner, half):
        return self.ref.at[rows_at(owner, self.size, half * self.half, self.half)]

    def step(self, s, which=(0, 1, 2, 3)):
        p = self.place
        for i in which:
            way, half, steps = self.chains[i]
            block = self.piece(p.dz(-way * s), half)
            if 0 < s <= steps:
                self.mail.arrive(self.key + i * 4 + s - 1, block, p.at(z=p.dz(-way)))
            if s < steps:
                self.mail.send(self.key + i * 4 + s, block, block, p.at(z=p.dz(way)))


class ZReduce:
    def __init__(self, mail, place, ref, size, stage, recv):
        self.mail, self.place, self.ref, self.size = mail, place, ref, size
        self.stage, self.recv = stage, recv
        self.half = size // 2
        self.key = mail.slots(16)
        self.chains = ((1, 0, 4), (-1, 1, 4), (1, 1, 3), (-1, 0, 3))

    def piece(self, owner, half):
        return rows_at(owner, self.size, half * self.half, self.half)

    def step(self, s, which=(0, 1, 2, 3)):
        p = self.place
        for i in which:
            way, half, steps = self.chains[i]
            if s < steps:
                dest = self.piece(p.dz(way * (steps - s)), half)
                if s == 0:
                    src = self.ref.at[dest]
                else:
                    self.mail.arrive(self.key + i * 4 + s - 1, self.recv.at[i, s - 1], p.at(z=p.dz(-way)))
                    src = self.stage.at[i, s - 1]
                    src[...] = (self.ref[dest].astype(F32) + self.recv[i, s - 1].astype(F32)).astype(BF16)
                self.mail.send(self.key + i * 4 + s, src, self.recv.at[i, s], p.at(z=p.dz(way)))

    def total(self):
        p = self.place
        for i, (way, half, steps) in enumerate(self.chains):
            self.mail.arrive(self.key + i * 4 + steps - 1, self.recv.at[i, steps - 1], p.at(z=p.dz(-way)))
        first = self.ref[self.piece(p.z, 0)].astype(F32) + self.recv[0, 3].astype(F32) + self.recv[3, 2].astype(F32)
        second = self.ref[self.piece(p.z, 1)].astype(F32) + self.recv[1, 3].astype(F32) + self.recv[2, 2].astype(F32)
        return jnp.concatenate([first, second], axis=0)


class Swap:
    def __init__(self, mail, ref, me, n, device_of):
        self.mail, self.ref, self.me, self.n, self.device_of = mail, ref, me, n, device_of
        self.key = mail.slots(n - 1)

    def other(self, d):
        return lax.rem(self.me + d, self.n)

    def start(self):
        for d in range(1, self.n):
            mine = self.ref.at[self.me]
            self.mail.send(self.key + d - 1, mine, mine, self.device_of(self.other(d)))

    def wait(self):
        for d in range(1, self.n):
            source = self.other(self.n - d)
            self.mail.arrive(self.key + d - 1, self.ref.at[source], self.device_of(source))

    def total(self):
        self.wait()
        value = self.ref[0].astype(F32)
        for j in range(1, self.n):
            value = value + self.ref[j].astype(F32)
        return value


def two_part(a):
    top = a.astype(BF16).astype(F32)
    return jnp.concatenate([top, a - top], axis=0).astype(BF16)


def dot_two(a, b, transposed=False):
    dims = (((1,), (1,)), ((), ())) if transposed else (((1,), (0,)), ((), ()))
    both = lax.dot_general(two_part(a), b, dims, preferred_element_type=F32)
    half = a.shape[0]
    return both[:half] + both[half:]


def add_into(acc, others):
    value = acc[...].astype(F32)
    for other in others:
        value = value + other[...].astype(F32)
    acc[...] = value.astype(BF16)


def ring_sum(mail, key, pos, nxt, prv, get, half, hbuf, fbuf):
    at = lambda d: lax.rem(pos + d, 4)
    mail.send(key, half(get(at(2)), 0), hbuf.at[0], nxt)
    mail.send(key + 1, half(get(at(2)), 1), hbuf.at[1], prv)
    yield
    mail.arrive(key, hbuf.at[0], prv)
    add_into(half(get(at(1)), 0), [hbuf.at[0]])
    mail.send(key + 2, get(at(1)), fbuf.at[0], nxt)
    mail.arrive(key + 1, hbuf.at[1], nxt)
    add_into(half(get(at(3)), 1), [hbuf.at[1]])
    mail.send(key + 3, get(at(3)), fbuf.at[1], prv)
    yield
    mail.arrive(key + 2, fbuf.at[0], prv)
    mail.arrive(key + 3, fbuf.at[1], nxt)


K_GELU = 0.7071067811865476
K_SLOPE = 0.3989422804014327
BLOCK16 = 16


def gelu_rows(pre_t, h_s, slope_s, t, row, lanes):
    v = pre_t[pl.ds(t, BLOCK16)]
    half = 0.5 * (1.0 + lax.erf(v * K_GELU))
    h_s[pl.ds(row, BLOCK16), lanes] = (v * half).astype(BF16)
    slope_s[pl.ds(row, BLOCK16), lanes] = (half + v * jnp.exp(-0.5 * v * v) * K_SLOPE).astype(BF16)


def kernel(
    x_ref, live, tile_patient, gain, up_hbm, dn_hbm, wt, ws, sw_ref, keys_hbm, qlab, plab, scale,
    up_out, dn_out, gate_out, misc_out,
    n_all, n_t, x_t, x_mate, up_b, dn_b, dn_t, wq, w_x, w_c, thru, thru_t, h_s, h_t, slope_s, part, uv_all, keys, keys_t,
    pg_s, pre_s, held_t, held_o, held_sum, held, pre2, gx, pre_t,
    stage, recv, pbuf, vbuf, zbuf, xbuf, sbuf, score_all, alpha_all, pull_s,
    up0, up_acc, dn_acc, g_acc, u_yh, u_yf, u_xh, u_xf, d_xh, d_xf, d_yh, d_yf,
    g_stage, g_recv, g_t, g_y, g_x, g_c, m_z, m_y, m_x, m_c,
    send_sem, recv_sem, local_sem,
):
    p = Place()
    mail = Mail(send_sem, recv_sem)
    mate, beside = p.at(c=1 - p.c), p.at(x=3 - p.x)
    above, below = p.at(y=p.dy(1)), p.at(y=p.dy(-1))
    z_dev = lambda z: p.at(z=z)
    y_dev = lambda y: p.at(y=y)
    x_dev = lambda x: p.at(x=x)
    c_dev = lambda c: p.at(c=c)
    q_dev = lambda q: (p.pat, p.z * 2 + q)
    partners = (
        [z_dev(p.dz(d)) for d in range(1, NZ)]
        + [y_dev(p.dy(d)) for d in (1, 2, 3)]
        + [x_dev(p.dx(d)) for d in (1, 2, 3)]
        + [mate]
    )
    barrier = pltpu.get_barrier_semaphore()
    for device in partners:
        pl.semaphore_signal(barrier, inc=1, device_id=device, device_id_type=MESH)

    fetch_up = pltpu.make_async_copy(up_hbm, up_b.at[p.q], local_sem.at[0])
    fetch_dn = pltpu.make_async_copy(dn_hbm, dn_b.at[p.q], local_sem.at[1])
    fetch_keys = pltpu.make_async_copy(keys_hbm, keys, local_sem.at[2])
    fetch_up.start()
    fetch_dn.start()
    fetch_keys.start()

    def norm_rows(half):
        v = x_ref[pl.ds(half * 64, 64)].astype(F32)
        center = v - jnp.mean(v, axis=1, keepdims=True)
        spread = jnp.mean(center * center, axis=1, keepdims=True)
        n_all[rows_at(p.z, ROWS, half * 64, 64)] = (center * lax.rsqrt(spread + 1e-06) * gain[...][None, :]).astype(BF16)

    g_rows = pl.ds(pl.multiple_of(p.c * 48, 16), 48)
    g_lanes = lanes_at(lax.rem(p.y, 2), 128)
    wq[p.c, p.y, p.q, p.z] = jnp.where(p.y < 2, wt[g_rows, g_lanes], ws[g_rows, g_lanes])

    norm_rows(0)
    pl.semaphore_wait(barrier, len(partners))

    tokens = ZGather(mail, p, n_all, ROWS)
    k_wz, k_w = mail.slots(7), mail.slots(1)
    w_z = lambda z: wq.at[p.c, p.y, p.q, z]
    for d in range(1, NZ):
        mail.send(k_wz + d - 1, w_z(p.z), w_z(p.z), z_dev(p.dz(d)))
    tokens.step(0, (0, 1))
    norm_rows(1)
    k_x0 = mail.slots(1)
    mail.send(k_x0, x_ref, x_mate, mate)

    up_piece = lambda q, y, c: up_b.at[q, rows_at(y * 2 + c, 192)]
    dn_piece = lambda q, y, c: dn_b.at[q, rows_at(y * 2 + c, 48)]
    theirs, other = 1 - p.q, 1 - p.c
    k_px, k_py, k_pm = mail.slots(2), mail.slots(6), mail.slots(8)
    fetch_up.wait()
    mail.send(k_px, up_piece(p.q, p.y, p.c), up_piece(p.q, p.y, p.c), beside)
    fetch_dn.wait()
    mail.send(k_px + 1, dn_piece(p.q, p.y, p.c), dn_piece(p.q, p.y, p.c), beside)

    def to_mate(d, piece, which):
        mail.send(k_pm + which * 4 + d, piece(theirs, p.dy(d), p.c), piece(theirs, p.dy(d), p.c), mate)

    def pieces_x():
        for which, piece in enumerate((up_piece, dn_piece)):
            block = piece(theirs, p.y, p.c)
            mail.arrive(k_px + which, block, beside)
            mail.send(k_py + which * 2, block, block, above)
            mail.send(k_py + which * 2 + 1, block, block, below)
            to_mate(0, piece, which)

        for which, piece in enumerate((up_piece, dn_piece)):
            block = piece(p.q, p.dy(2), p.c)
            mail.send(k_py + 4 + which, block, block, beside)

    def pieces_y():
        for which, piece in enumerate((up_piece, dn_piece)):
            mail.arrive(k_py + which * 2, piece(theirs, p.dy(-1), p.c), below)
            to_mate(3, piece, which)
            mail.arrive(k_py + which * 2 + 1, piece(theirs, p.dy(1), p.c), above)
            to_mate(1, piece, which)

    def pieces_far():
        for which, piece in enumerate((up_piece, dn_piece)):
            mail.arrive(k_py + 4 + which, piece(theirs, p.dy(2), p.c), beside)
            to_mate(2, piece, which)

    def pieces_mate(which):
        piece = (up_piece, dn_piece)[which]
        for d in range(4):
            mail.arrive(k_pm + which * 4 + d, piece(theirs, p.dy(d), other), mate)

    def hidden(owners, q):
        lhs = jnp.concatenate([n_all[rows_at(o, ROWS)] for o in owners], axis=0)
        count = len(owners) * ROWS
        pre_t[pl.ds(0, count)] = dot(lhs, up_b[q])
        lanes = lanes_at(q, HID)
        for j, o in enumerate(owners):
            def body(i, carry, j=j, o=o):
                t = pl.multiple_of(j * ROWS + i * BLOCK16, BLOCK16)
                row = pl.multiple_of(o * ROWS + i * BLOCK16, BLOCK16)
                gelu_rows(pre_t, h_s, slope_s, t, row, lanes)
                return carry

            lax.fori_loop(0, ROWS // BLOCK16, body, 0)

    def turn(owners):
        for o in owners:
            n_t[:, lanes_at(o, ROWS)] = n_all[rows_at(o, ROWS)].T

    def key_rows(i):
        at = pl.ds(i * 256, 256)
        v = keys[at].astype(F32)
        keys[at] = (v * lax.rsqrt(jnp.sum(v * v, axis=1, keepdims=True) + 1e-06)).astype(BF16)

    k_wy, k_wm = mail.slots(4), mail.slots(1)
    w_y = lambda y: wq.at[p.c, y]
    w_yh = lambda y, half: wq.at[p.c, y, half]
    near = [p.dz(1), p.dz(-1)]
    mid = [p.dz(2), p.dz(-2)]
    far = [p.dz(3), p.dz(-3)]

    hidden([p.z], p.q)
    turn([p.z])
    x_t[:, pl.ds(0, ROWS)] = x_ref[...].T
    for d in range(1, NZ):
        mail.arrive(k_wz + d - 1, w_z(p.dz(-d)), z_dev(p.dz(-d)))
    mail.send(k_w, wq.at[p.c, p.y, p.q], wq.at[p.c, p.y, p.q], beside)
    tokens.step(0, (2, 3))
    fetch_keys.wait()
    key_rows(0)
    tokens.step(1, (0, 1))
    mail.arrive(k_w, wq.at[p.c, p.y, theirs], beside)
    mail.send(k_wy, w_y(p.y), w_y(p.y), above)
    mail.send(k_wy + 1, w_y(p.y), w_y(p.y), below)
    pieces_x()
    tokens.step(1, (2, 3))
    hidden(near, p.q)
    turn(near)
    key_rows(1)
    tokens.step(2, (0, 1))
    key_rows(2)
    key_rows(3)
    mail.arrive(k_wy, w_y(p.dy(-1)), below)
    mail.send(k_wy + 2, w_yh(p.dy(-1), 0), w_yh(p.dy(-1), 0), above)
    mail.arrive(k_wy + 1, w_y(p.dy(1)), above)
    mail.send(k_wy + 3, w_yh(p.dy(1), 1), w_yh(p.dy(1), 1), below)
    tokens.step(2, (2, 3))
    hidden(mid, p.q)
    turn(mid)
    pieces_y()
    mail.arrive(k_wy + 2, w_yh(p.dy(2), 0), below)
    mail.arrive(k_wy + 3, w_yh(p.dy(2), 1), above)
    mail.send(k_wm, wq.at[p.c], wq.at[p.c], mate)
    pieces_far()
    tokens.step(3, (0, 1))
    pieces_mate(0)
    hidden([p.z], theirs)
    hidden(near, theirs)
    hidden(mid, theirs)
    mail.arrive(k_wm, wq.at[other], mate)

    def place_w(t, carry):
        for y in range(4):
            for c in range(2):
                row = pl.multiple_of(t * 96 + c * 48, 16)
                w_x[pl.ds(row, 48), pl.ds(y * 128, 128)] = wq[c, y, lax.rem(t, 2), lax.div(t, 2)]
        return carry

    lax.fori_loop(0, 16, place_w, 0)
    w_full = lambda: w_x[:, pl.ds(0, 2 * GATE)]
    pieces_mate(1)
    for q in range(2):
        thru[pl.ds(q * HID, HID)] = dot(dn_b[q], w_full()).astype(BF16)

    def gate_part(o, carry):
        at = rows_at(o, ROWS)
        part[at] = dot(h_s[at], thru[...]).astype(BF16)
        return carry

    tokens.step(3, (2, 3))
    for j in range(2):
        keys_t[:, pl.ds(j * 512, 512)] = keys[pl.ds(j * 512, 512)].T
    hidden(far, p.q)
    hidden(far, theirs)
    turn(far)
    lax.fori_loop(0, NZ - 1, lambda d, carry: gate_part(lax.rem(p.z + 5 + d, NZ), carry), 0)
    tokens.step(4)
    last = p.dz(4)
    hidden([last], 0)
    hidden([last], 1)
    gate_part(last, 0)

    reduce = ZReduce(mail, p, part, ROWS, stage, recv)
    gather_uv = ZGather(mail, p, uv_all, ROWS)
    swap_p = Swap(mail, pbuf, p.z, NZ, z_dev)
    swap_z = [Swap(mail, ref, p.z, NZ, z_dev) for ref in (vbuf, zbuf.at[0], zbuf.at[1])]
    swap_x = [Swap(mail, xbuf.at[i], p.q, 2, q_dev) for i in range(3)]
    swap_s = Swap(mail, sbuf, p.z, NZ, z_dev)

    row8 = lax.broadcasted_iota(jnp.int32, (8, 128), 0)
    first4 = row8 < 4
    row_patient = lax.rem(row8, 4)
    first4_wide = lax.broadcasted_iota(jnp.int32, (8, 768), 0) < 4
    lane = lax.broadcasted_iota(jnp.int32, (8, 128), 1)

    def pack(v):
        return jnp.where(first4_wide, v[:, :768], v[:, 768:])

    def unpack(v):
        rolled = pltpu.roll(v, 4, 0)
        return jnp.concatenate([jnp.where(first4_wide, v, rolled), jnp.where(first4_wide, rolled, v)], axis=1)

    reduce.step(0, (0, 1))
    turn([last])
    dn_t[:, pl.ds(0, HID)] = dn_b[0].T
    reduce.step(0, (2, 3))
    dn_t[:, pl.ds(HID, HID)] = dn_b[1].T
    gate_x = dot(x_ref[...], w_full())
    reduce.step(1, (0, 1))
    same = jnp.zeros((8, 1024), jnp.int32)
    row_wide = lax.rem(lax.broadcasted_iota(jnp.int32, (8, 1024), 0), 4)
    labels = jnp.broadcast_to(qlab[...], (8, 1024))
    for k in range(4):
        same = jnp.where((row_wide == k) & (labels == plab[k]), 1, same)
    same = same.astype(F32)
    label_sums = dot(same.astype(BF16), keys[...])
    positives = jnp.sum(same, axis=1, keepdims=True)
    reduce.step(1, (2, 3))
    for z in range(NZ):
        h_t[:, pl.ds(z * ROWS, ROWS)] = h_s[pl.ds(z * ROWS, ROWS)].T
    reduce.step(2, (0, 1))
    for i in range(8):
        w_c[pl.ds(i * 96, 96), pl.ds(0, 512)] = w_x[pl.ds(pl.multiple_of((i * 2 + p.c) * 96, 96), 96), pl.ds(0, 512)]
    reduce.step(2, (2, 3))
    mail.arrive(k_x0, x_mate, mate)
    x_t[:, pl.ds(ROWS, ROWS)] = x_mate[...].T
    reduce.step(3, (0, 1))
    mail.settle(20)
    gates = reduce.total() + gate_x
    tanh_val = jnp.tanh(gates[:, :GATE])
    sigmoid_val = jax.nn.sigmoid(gates[:, GATE:])
    product = tanh_val * sigmoid_val
    sw = sw_ref[...]
    score = lax.dot_general(
        jnp.broadcast_to(sw, (8, GATE)), product, (((1,), (1,)), ((), ())), precision=HIGH, preferred_element_type=F32
    )
    in_tile = lax.broadcasted_iota(jnp.int32, (8, 128), 1) < live[0]
    onehot = (jnp.broadcast_to(tile_patient[...], (8, 128)) == row_patient) & in_tile
    mass = jnp.where(onehot, jnp.exp(score), 0.0)
    pbuf[p.z] = mass
    swap_p.start()
    common = sw * sigmoid_val
    own_rows = rows_at(p.z, ROWS)
    uv_all[own_rows, pl.ds(0, GATE)] = (common * (1.0 - tanh_val * tanh_val)).astype(BF16)
    uv_all[own_rows, pl.ds(GATE, GATE)] = (common * tanh_val * (1.0 - sigmoid_val)).astype(BF16)
    gather_uv.step(0)

    def post(i, packed, small):
        zbuf[i - 1, p.z, :, pl.ds(0, 768)] = packed
        zbuf[i - 1, p.z, :, pl.ds(768, 128)] = small
        swap_z[i].start()

    def collect_z(i):
        xbuf[i, p.q] = swap_z[i].total()
        swap_x[i].start()

    post(1, pack(label_sums), jnp.broadcast_to(positives, (8, 128)))
    vec_x = dot_two(mass, x_ref[...])
    swap_p.wait()

    total = jnp.zeros((8, 1), F32)
    for z in range(NZ):
        total += jnp.sum(pbuf[z], axis=1, keepdims=True)
    mass_all = jnp.concatenate([pbuf[z] for z in range(NZ)], axis=1)
    mass_h = dot_two(mass_all, h_s[...])
    vec = dot_two(mass_h[:, :HID], dn_b[0]) + dot_two(mass_h[:, HID:], dn_b[1]) + vec_x

    packed = pack(vec)
    top = total.astype(BF16).astype(F32)
    small = jnp.where(lane == 0, top, total - top)
    vbuf[p.z, :, pl.ds(0, 384)] = jnp.concatenate([packed[:, :384], packed[:, 384:]], axis=0).astype(BF16)
    vbuf[p.z, :, pl.ds(384, 128)] = jnp.concatenate([small, small], axis=0).astype(BF16)
    swap_z[0].start()
    both = swap_z[0].total()
    xbuf[0, p.q, :, pl.ds(0, 384)] = both[:8, :384]
    xbuf[0, p.q, :, pl.ds(384, 384)] = both[8:, :384]
    xbuf[0, p.q, :, pl.ds(768, 128)] = jnp.broadcast_to(both[:8, 384:385] + both[:8, 385:386], (8, 128))
    swap_x[0].start()
    gather_uv.step(1)
    collect_z(1)
    thru_t[...] = thru[...].T
    summed = swap_x[0].total()
    total_mass = summed[:, 768:769]
    pooled = unpack(summed[:, :768]) / total_mass
    length = jnp.sqrt(jnp.sum(pooled * pooled, axis=1, keepdims=True) + 1e-06)
    unit = pooled / length

    logits = dot(unit.astype(BF16), keys_t[...]) / 0.07
    exps = jnp.exp(logits)
    exp_part = jnp.sum(exps, axis=1, keepdims=True)
    pos_part = jnp.sum(same * logits, axis=1, keepdims=True)
    post(2, pack(dot_two(exps, keys[...])), jnp.where(lane == 0, exp_part, pos_part))
    collect_z(2)
    gather_uv.step(2)
    labels_total = swap_x[1].total()
    pos_count = labels_total[:, 768:769]
    queue_total = swap_x[2].total()
    exp_total = queue_total[:, 768:769]
    pos_logits = queue_total[:, 769:770]
    unit_grad = (scale[0] * INV_TEMP) * (
        unpack(queue_total[:, :768]) / exp_total - unpack(labels_total[:, :768]) / pos_count
    )
    pooled_grad = (unit_grad - unit * jnp.sum(unit * unit_grad, axis=1, keepdims=True)) / length

    grad_h = dot_two(pooled_grad, dn_t[...])
    own_dots = dot_two(pooled_grad, x_t[:, pl.ds(0, ROWS)])
    dots = dot_two(grad_h, h_t[...])
    for z in range(NZ):
        block = dots[:, z * ROWS : (z + 1) * ROWS] + jnp.where(p.z == z, own_dots, 0.0)
        picked = jnp.where((pbuf[z] > 0.0) & first4, block, 0.0)
        sbuf[p.z, pl.ds(z, 1)] = jnp.sum(picked, axis=0, keepdims=True)
    swap_s.start()
    center = jnp.sum(pooled * pooled_grad, axis=1, keepdims=True)
    log_part = jnp.log(exp_total) - pos_logits / pos_count
    loss = jnp.sum(jnp.where(first4, jnp.broadcast_to(log_part, (8, 128)), 0.0), axis=0, keepdims=True)
    for z in range(NZ):
        block = jnp.where(first4, pbuf[z], 0.0)
        alpha_all[pl.ds(z, 1)] = jnp.sum(block / total_mass, axis=0, keepdims=True)
        score_all[pl.ds(z, 1)] = jnp.sum(jnp.where(block > 0.0, center, 0.0), axis=0, keepdims=True)
    gather_uv.step(3)
    pad = jnp.zeros((120, 768), F32)
    grad_h_pad = jnp.concatenate([jnp.where(first4_wide, grad_h, 0.0), pad], axis=0).astype(BF16)
    rest = jnp.zeros((120, 128), F32)

    def pulled(b, carry):
        mass_b = jnp.where(first4, pbuf[b], 0.0)
        weight = jnp.where(mass_b > 0.0, jnp.broadcast_to(alpha_all[pl.ds(b, 1)], (8, 128)), 0.0)
        at = rows_at(b, ROWS)
        turned = jnp.concatenate([weight, rest], axis=0).T.astype(BF16)
        pull_s[at] = (dot(turned, grad_h_pad) * slope_s[at].astype(F32)).astype(BF16)
        return carry + dot_two(weight, h_s[at])

    held4 = lax.fori_loop(0, NZ, pulled, jnp.zeros((8, 768), F32))
    k_g = mail.slots(1)
    gx[0, :, pl.ds(0, D)] = pooled_grad
    gx[0, :, pl.ds(D, 768)] = jnp.where(first4_wide, held4, 0.0)
    mail.send(k_g, gx.at[0], gx.at[1], mate)
    gather_uv.step(4)

    def scaled(b, carry):
        at = pl.ds(pl.multiple_of(b * 256, 256), 256)
        pg_s[at] = (dot(uv_all[at], thru_t[...]) * slope_s[at].astype(F32)).astype(BF16)
        return carry

    lax.fori_loop(0, 4, scaled, 0)
    mail.arrive(k_g, gx.at[1], mate)
    grad_pad = jnp.concatenate([gx[0, :, pl.ds(0, D)], gx[1, :, pl.ds(0, D)], jnp.zeros((112, D), F32)], axis=0)
    for j in range(D // 128):
        w_x[pl.ds(j * 128, 128), pl.ds(512, 128)] = grad_pad[:, j * 128 : (j + 1) * 128].T.astype(BF16)
    for i in range(8):
        w_c[pl.ds(i * 96, 96), pl.ds(512, 128)] = w_x[pl.ds(pl.multiple_of((i * 2 + p.c) * 96, 96), 96), pl.ds(512, 128)]
    held[pl.ds(512, 128)] = jnp.concatenate(
        [gx[0, :, pl.ds(D, 768)], gx[1, :, pl.ds(D, 768)], jnp.zeros((112, 768), F32)], axis=0
    ).astype(BF16)
    mail.settle(12)
    score_all[...] = alpha_all[...] * (swap_s.total() - score_all[...])

    def apply_scores(b, carry):
        at = rows_at(b, ROWS)
        grad = jnp.broadcast_to(score_all[pl.ds(b, 1)], (ROWS, ROWS)).T[:, 0:1]
        pre_s[at] = (grad * uv_all[at].astype(F32)).astype(BF16)
        pg_s[at] = (grad * pg_s[at].astype(F32) + pull_s[at].astype(F32)).astype(BF16)
        return carry

    lax.fori_loop(0, NZ, apply_scores, 0)
    score_part = lax.dot_general(
        jnp.broadcast_to(score_all[pl.ds(p.z, 1)], (8, ROWS)), product, (((1,), (0,)), ((), ())),
        precision=HIGH, preferred_element_type=F32,
    )
    misc = jnp.where(
        row8 == 0, score_part[:, :128], jnp.where(row8 == 1, score_part[:, 128:], jnp.where(row8 == 2, loss / 16.0, 0.0))
    )

    def misc_chain(value):
        stages = [
            (Swap(mail, m_z, p.z, NZ, z_dev), m_z, p.z),
            (Swap(mail, m_y, p.y, 4, y_dev), m_y, p.y),
            (Swap(mail, m_x, p.x, 4, x_dev), m_x, p.x),
            (Swap(mail, m_c, p.c, 2, c_dev), m_c, p.c),
        ]
        for swap, buf, me in stages:
            buf[me] = value
            swap.start()
            yield
            value = swap.total()
        misc_out[...] = value
        yield

    misc_steps = misc_chain(misc)
    next(misc_steps)

    k_h, k_p = mail.slots(2), mail.slots(1)
    for j in range(3):
        held_t[pl.ds(j * 256, 256)] = dot(h_t[pl.ds(j * 256, 256)], pre_s[...]).astype(BF16)
    half_of = lambda ref, c: ref.at[:, lanes_at(c, GATE)]
    mail.send(k_h, half_of(held_t, other), half_of(held_o, other), mate)
    theirs_pre = pre_s.at[own_rows, lanes_at(other, GATE)]
    mail.send(k_p, theirs_pre, pre2.at[pl.ds(ROWS, ROWS)], mate)
    pre2[pl.ds(0, ROWS)] = pre_s[own_rows, lanes_at(p.c, GATE)]

    def sum_held(k, c):
        mail.arrive(k, half_of(held_o, c), mate)
        lanes = lanes_at(c, GATE)
        total_held = (held_t[:, lanes].astype(F32) + held_o[:, lanes].astype(F32)).astype(BF16)
        held_sum[:, lanes] = total_held
        held[rows_at(c, GATE)] = total_held.T

    def gate_grads():
        mail.arrive(k_p, pre2.at[pl.ds(ROWS, ROWS)], mate)

        def gate_rows(i, carry):
            at = pl.ds(pl.multiple_of(i * 512, 512), 512)
            g_acc[at] = (dot(dn_t[at], held_sum[:, lanes_at(p.c, GATE)]) + dot(x_t[at], pre2[...])).astype(BF16)
            return carry

        lax.fori_loop(0, 3, gate_rows, 0)

    def dn_rows(xl):
        value = dot(w_c[rows_at(xl, 384)], held[...]).astype(BF16)
        for y in range(4):
            dn_acc[xl, y] = value[y * 96 : (y + 1) * 96]

    up_p = lambda i, c: keys_t.at[pl.ds(pl.multiple_of((i * 2 + c) * 96, 96), 96), pl.ds(0, 768)]
    k_up0 = mail.slots(8)

    def compute(block, lhs, rhs, index, k, buf):
        def body(j, carry):
            i = index(j)
            value = dot(lhs[pl.ds(pl.multiple_of(i * 192, 192), 192)], rhs[...]).astype(BF16)
            block(i, 0)[...] = value[:96]
            block(i, 1)[...] = value[96:]
            return carry

        lax.fori_loop(0, 2, body, 0)
        for j in range(2):
            mail.send(k + j, block(index(j), other), buf.at[index(j)], mate)

    def collect(block, index, k, buf, acc):
        for j in range(2):
            mail.arrive(k + j, buf.at[index(j)], mate)

        def body(j, carry):
            i = index(j)
            acc[lax.div(i, 4), lax.rem(i, 4)] = (block(i, p.c)[...].astype(F32) + buf[i].astype(F32)).astype(BF16)
            return carry

        lax.fori_loop(0, 2, body, 0)

    up_index = [lambda j, d=d: j * 4 + p.dy(d) for d in (2, 1, -1, 0)]
    up_go = lambda g: compute(up_p, n_t, pg_s, up_index[g], k_up0 + 2 * g, up0)
    up_take = lambda g: collect(up_p, up_index[g], k_up0 + 2 * g, up0, up_acc)
    rows_half = lambda ref, i: ref.at[pl.ds(i * 48, 48)]
    k_up, k_dn = mail.slots(8), mail.slots(8)
    up_chunk = lambda d: up_acc.at[lax.rem(d, 2), p.y, :, lanes_at(lax.div(d, 2), HID)]
    dn_chunk_x = lambda d: dn_acc.at[lax.rem(d, 2), :, :, lanes_at(lax.div(d, 2), HID)]
    dn_chunk = lambda d: dn_acc.at[p.xl, d, :, lanes_at(p.q, HID)]
    up_y = ring_sum(
        mail, k_up, p.y, above, below, lambda d: up_acc.at[:, d], lambda ref, i: ref.at[i], u_yh, u_yf
    )
    up_x = ring_sum(mail, k_up + 4, p.x, x_dev(p.dx(1)), x_dev(p.dx(-1)), up_chunk, rows_half, u_xh, u_xf)
    dn_x = ring_sum(
        mail, k_dn, p.x, x_dev(p.dx(1)), x_dev(p.dx(-1)), dn_chunk_x, lambda ref, i: ref.at[pl.ds(i * 2, 2)], d_xh, d_xf
    )
    dn_y = ring_sum(mail, k_dn + 4, p.y, above, below, dn_chunk, rows_half, d_yh, d_yf)
    step = lambda chain: next(chain, None)
    zred = ZReduce(mail, p, g_acc, 192, g_stage, g_recv)
    in_y = Swap(mail, g_y, p.y, 4, y_dev)
    k_x = mail.slots(3)
    in_c = Swap(mail, g_c, p.c, 2, c_dev)

    up_go(0)
    mail.send(k_h + 1, half_of(held_t, p.c), half_of(held_o, p.c), mate)
    sum_held(k_h, p.c)
    gate_grads()
    zred.step(0, (0, 1))
    up_go(1)
    zred.step(0, (2, 3))
    sum_held(k_h + 1, other)
    dn_rows(p.xl)
    dn_rows(1 - p.xl)
    step(dn_x)
    up_take(0)
    step(up_y)
    zred.step(1, (0, 1))
    up_go(2)
    zred.step(1, (2, 3))
    up_go(3)
    step(misc_steps)
    zred.step(2, (0, 1))
    up_take(1)
    up_take(2)
    zred.step(2, (2, 3))
    step(up_y)
    step(dn_x)
    zred.step(3)
    up_take(3)
    step(misc_steps)
    sums = zred.total().astype(BF16)
    g_t[0] = sums[:96]
    g_t[1] = sums[96:]
    for d in (1, 2, 3):
        there = p.dx(d)
        mail.send(k_x + d - 1, g_t.at[lax.div(there, 2)], g_x.at[d], x_dev(there))
    step(up_y)
    add_into(up_acc.at[:, p.y], [u_yf.at[0], u_yf.at[1]])
    step(up_x)
    for d in (1, 2, 3):
        mail.arrive(k_x + d - 1, g_x.at[d], x_dev(p.dx(-d)))
    value = g_t[p.q].astype(F32)
    for d in (1, 2, 3):
        value = value + g_x[d].astype(F32)
    g_y[p.y] = value.astype(BF16)
    in_y.start()
    step(dn_x)
    add_into(dn_chunk_x(p.x), [d_xf.at[0], d_xf.at[1]])
    step(dn_y)
    step(misc_steps)
    g_c[p.c] = in_y.total().astype(BF16)
    in_c.start()
    step(up_x)
    step(dn_y)
    step(misc_steps)
    mail.settle(8)
    step(up_x)
    up_out[...] = up_chunk(p.x)[...].astype(F32) + u_xf[0].astype(F32) + u_xf[1].astype(F32)
    in_c.wait()
    gate_out[...] = g_c[...].astype(F32)
    step(dn_y)
    dn_out[...] = dn_chunk(p.y)[...].astype(F32) + d_yf[0].astype(F32) + d_yf[1].astype(F32)
    mail.settle()


ANY = pl.BlockSpec(memory_space=pl.ANY)
VMEM = pl.BlockSpec(memory_space=pltpu.VMEM)
SMEM = pl.BlockSpec(memory_space=pltpu.SMEM)


def hand_out(up, dn, gate, total, loss, up_out, dn_out, tanh_out, sigmoid_out, score_out, loss_out):
    up_out[...] = up[...]
    dn_out[...] = dn[...]
    tanh_out[...] = gate[0]
    sigmoid_out[...] = gate[1]
    score_out[pl.ds(0, 128)] = total[0]
    score_out[pl.ds(128, 128)] = total[1]
    loss_out[0] = loss[2, 0]


def per_device(
    patch_class_features, live_tiles, tile_patient, ln_gain, up_weight, down_weight, tanh_weight,
    sigmoid_weight, score_weight, queue_keys, queue_labels, patient_labels, loss_scale,
):
    out = lambda *dims: jax.ShapeDtypeStruct(dims, F32)
    vm = lambda *dims: pltpu.VMEM(dims, BF16)
    vf = lambda *dims: pltpu.VMEM(dims, F32)
    up_grad, down_grad, gate_grad, total = pl.pallas_call(
        kernel,
        name="step",
        out_shape=(out(96, HID), out(96, HID), out(2, 96, GATE), out(8, 128)),
        in_specs=[VMEM, SMEM, VMEM, VMEM, ANY, ANY, VMEM, VMEM, VMEM, ANY, VMEM, SMEM, SMEM],
        out_specs=(VMEM,) * 4,
        scratch_shapes=[
            vm(TOK, D),
            vm(D, TOK),
            vm(D, 2 * ROWS),
            vm(ROWS, D),
            vm(2, D, HID),
            vm(2, HID, D),
            vm(D, 2 * HID),
            vm(2, 4, 2, NZ, 48, 128),
            vm(D, 640),
            vm(768, 640),
            vm(2 * HID, 2 * GATE),
            vm(2 * GATE, 2 * HID),
            vm(TOK, 2 * HID),
            vm(2 * HID, TOK),
            vm(TOK, 2 * HID),
            vm(TOK, 2 * GATE),
            vm(TOK, 2 * GATE),
            vm(1024, D),
            vm(D, 1024),
            vm(TOK, 2 * HID),
            vm(TOK, 2 * GATE),
            vm(2 * HID, 2 * GATE),
            vm(2 * HID, 2 * GATE),
            vm(2 * HID, 2 * GATE),
            vm(640, 2 * HID),
            vm(2 * ROWS, GATE),
            vf(2, 8, D + 768),
            vf(256, HID),
            vm(4, 3, ROWS // 2, 2 * GATE),
            vm(4, 4, ROWS // 2, 2 * GATE),
            vf(NZ, 8, 128),
            vm(NZ, 16, 512),
            vf(2, NZ, 8, 896),
            vf(3, 2, 8, 896),
            vf(NZ, 8, 128),
            vf(NZ, 128),
            vf(NZ, 128),
            vm(TOK, 2 * HID),
            vm(8, 96, 2 * HID),
            vm(2, 4, 96, 2 * HID),
            vm(2, 4, 96, 2 * HID),
            vm(D, GATE),
            vm(2, 96, 2 * HID),
            vm(2, 2, 96, 2 * HID),
            vm(2, 48, HID),
            vm(2, 96, HID),
            vm(2, 2, 96, HID),
            vm(2, 4, 96, HID),
            vm(2, 48, HID),
            vm(2, 96, HID),
            vm(4, 3, 96, GATE),
            vm(4, 4, 96, GATE),
            vm(2, 96, GATE),
            vm(4, 96, GATE),
            vm(4, 96, GATE),
            vm(2, 96, GATE),
            vf(NZ, 8, 128),
            vf(4, 8, 128),
            vf(4, 8, 128),
            vf(2, 8, 128),
            pltpu.SemaphoreType.DMA((192,)),
            pltpu.SemaphoreType.DMA((192,)),
            pltpu.SemaphoreType.DMA((4,)),
        ],
        compiler_params=pltpu.CompilerParams(collective_id=1, has_side_effects=True, vmem_limit_bytes=VMEM_LIMIT),
    )(
        patch_class_features, live_tiles, tile_patient[None, :], ln_gain, up_weight, down_weight,
        tanh_weight, sigmoid_weight, score_weight[None, :], queue_keys, queue_labels[None, :], patient_labels,
        loss_scale.reshape(1),
    )
    outputs = pl.pallas_call(
        hand_out,
        name="hand_out",
        out_shape=(out(96, HID), out(96, HID), out(96, GATE), out(96, GATE), out(GATE), out(1)),
        in_specs=[VMEM] * 4 + [SMEM],
        out_specs=(VMEM,) * 5 + (SMEM,),
    )(up_grad, down_grad, gate_grad, total, total)
    return (outputs[0], outputs[1].T, *outputs[2:5], outputs[5].reshape(()))


def solution(mesh):
    placed = (
        P(("pat", "tile"), None),
        P(("pat", "tile")),
        P(("pat", "tile")),
        P(),
        P(None, "tile"),
        P("tile", None),
        P("tile", None),
        P("tile", None),
        P(),
        P("tile", None),
        P("tile"),
        P("pat"),
        P(),
    )
    return jax.shard_map(
        per_device,
        mesh=mesh,
        in_specs=placed,
        out_specs=(P("pat", "tile"), P("tile", "pat"), P("tile", None), P("tile", None), P(), P()),
        check_vma=False,
    )
```
